32 devices in a mesh: sp: 4 (over z), fsdp: 8 (over y, x, core).
Axes of the slice: x: 2, y: 2, z: 4, core: 2. Of those that a mesh axis runs over, the one named last changes fastest.
Arguments:
- tokens: bfloat16 [4, 8, 256, 768], P(None, 'fsdp', 'sp'), may hold values from -6 to 6
- lengths: int32 [4], replicated, may hold values from 512 to 2048, as said below
- cotangent: bfloat16 [4, 8, 256, 768], P(None, 'fsdp', 'sp'), may hold values from -6 to 6
- pre_gain: bfloat16 [768], P('fsdp'), may hold values from 0.5 to 1.5
- query_weight: bfloat16 [768, 768], P('fsdp'), may hold values from -0.21875 to 0.21875
- key_weight: bfloat16 [768, 768], P('fsdp'), may hold values from -0.21875 to 0.21875
- value_weight: bfloat16 [768, 768], P('fsdp'), may hold values from -0.21875 to 0.21875
- gate_weight: bfloat16 [768, 768], P('fsdp'), may hold values from -0.21875 to 0.21875
- rate_weight: bfloat16 [768, 12], P('fsdp'), may hold values from -0.21875 to 0.21875
- out_weight: bfloat16 [768, 768], P('fsdp'), may hold values from -0.21875 to 0.21875
- post_gain: bfloat16 [768], P('fsdp'), may hold values from 0.5 to 1.5
- ffn_gate: bfloat16 [768, 2048], P('fsdp'), may hold values from -0.21875 to 0.21875
- ffn_up: bfloat16 [768, 2048], P('fsdp'), may hold values from -0.21875 to 0.21875
- ffn_down: bfloat16 [2048, 768], P('fsdp'), may hold values from -0.125 to 0.125
- inner_first: float32 [12, 64, 256], P('sp'), may hold values from -0.75 to 0.75
- inner_first_bias: float32 [12, 256], P('sp'), may hold values from -1.75 to 1.75
- inner_second: float32 [12, 256, 64], P('sp'), may hold values from -0.375 to 0.375
- inner_second_bias: float32 [12, 64], P('sp'), may hold values from -1.75 to 1.75
- inner_gain: float32 [12, 64], P('sp'), may hold values from 0.5 to 1.5
- inner_shift: float32 [12, 64], P('sp'), may hold values from -1.75 to 1.75
Outputs:
- output: bfloat16 [4, 8, 256, 768], P(None, 'fsdp', 'sp')
- tokens_grad: bfloat16 [4, 8, 256, 768], P(None, 'fsdp', 'sp')
- pre_gain_grad: float32 [768], P('fsdp')
- query_weight_grad: float32 [768, 768], P('fsdp')
- key_weight_grad: float32 [768, 768], P('fsdp')
- value_weight_grad: float32 [768, 768], P('fsdp')
- gate_weight_grad: float32 [768, 768], P('fsdp')
- rate_weight_grad: float32 [768, 12], P('fsdp')
- out_weight_grad: float32 [768, 768], P('fsdp')
- post_gain_grad: float32 [768], P('fsdp')
- ffn_gate_grad: float32 [768, 2048], P('fsdp')
- ffn_up_grad: float32 [768, 2048], P('fsdp')
- ffn_down_grad: float32 [2048, 768], P('fsdp')
- inner_first_grad: float32 [12, 64, 256], P('sp')
- inner_first_bias_grad: float32 [12, 256], P('sp')
- inner_second_grad: float32 [12, 256, 64], P('sp')
- inner_second_bias_grad: float32 [12, 64], P('sp')
- inner_gain_grad: float32 [12, 64], P('sp')
- inner_shift_grad: float32 [12, 64], P('sp')
The draws below stay inside these ranges and needn't reach their ends.
Inputs may be any that keep to these rules, and one draw needn't show every extreme that they name: `lengths`: every micro-batch holds 512 or more tokens followed by padding; in every draw one micro-batch is full (2048 tokens).
All inputs are finite; a program needn't handle non-finite values.
Results may differ from the reference program's by a relative error of at most 0.019.
Values may be sent and summed in bfloat16 or wider, within the bound.
No kernel may reach another device: no remote copies, remote signals or barrier semaphores. Data moves between devices by JAX's collectives and lax.ppermute only.
A program may use at most 128 MiB of HBM per device.

```python
import jax
import jax.numpy as jnp
from jax import lax

D = 768
HEADS = 12
HEAD = 64
INNER = 256
FF = 2048
MINI = 16
MICRO = 4
PIECE = 256
NPIECE = 8
LENGTH = 2048


def draw_lengths(key, part):
    pick_key, fill_key = jax.random.split(jax.random.fold_in(key, 7))
    drawn_lengths = jax.random.randint(fill_key, (MICRO,), LENGTH // 4, LENGTH + 1)
    full_slot = jax.random.randint(pick_key, (), 0, MICRO)
    slot_ids = jnp.arange(MICRO)
    drawn_lengths = jnp.where(slot_ids == full_slot, LENGTH, drawn_lengths)
    return drawn_lengths.astype(jnp.int32)


def level_of(own_key, extent, cuts, least, largest):
    gain = 1.0
    for dim, blocks in cuts:
        heights = jax.random.uniform(jax.random.fold_in(jax.random.fold_in(own_key, 6), dim), (blocks,), jnp.float32, least / len(cuts), largest / len(cuts))
        gain = gain * jnp.repeat(jnp.exp(heights), extent[dim] // blocks).reshape((-1,) + (1,) * (len(extent) - 1 - dim))
    return gain


def gaussian(key, dims, scale, limit, cuts=(), dtype=jnp.bfloat16):
    entries = jax.random.normal(key, dims, jnp.float32) * scale
    if len(cuts) > 0:
        entries = level_of(key, dims, cuts, -0.22, 0.18) * entries
    return jnp.clip(entries, min=-limit, max=limit).astype(dtype)


def setup_inputs(seed: int = 0) -> dict:
    splits = jax.random.split(jax.random.key(seed), 21)
    return {
        "tokens": gaussian(splits[0], (MICRO, NPIECE, PIECE, D), 1.0, 6.0, ((1, 8), (2, 4))),
        "lengths": draw_lengths(jax.random.fold_in(splits[20], 71), 0),
        "cotangent": gaussian(splits[2], (MICRO, NPIECE, PIECE, D), 1.0, 6.0, ((1, 8), (2, 4))),
        "pre_gain": jnp.clip(1.0 + 0.1 * jax.random.normal(splits[3], (D,), jnp.float32), 0.5, 1.5).astype(jnp.bfloat16),
        "query_weight": gaussian(splits[4], (D, D), D ** -0.5, 0.21875, ((0, 8),)),
        "key_weight": gaussian(splits[5], (D, D), D ** -0.5, 0.21875, ((0, 8),)),
        "value_weight": gaussian(splits[6], (D, D), D ** -0.5, 0.21875, ((0, 8),)),
        "gate_weight": gaussian(splits[7], (D, D), D ** -0.5, 0.21875, ((0, 8),)),
        "rate_weight": gaussian(splits[8], (D, HEADS), D ** -0.5, 0.21875, ((0, 8),)),
        "out_weight": gaussian(splits[9], (D, D), D ** -0.5, 0.21875, ((0, 8),)),
        "post_gain": jnp.clip(1.0 + 0.1 * jax.random.normal(splits[10], (D,), jnp.float32), 0.5, 1.5).astype(jnp.bfloat16),
        "ffn_gate": gaussian(splits[11], (D, FF), D ** -0.5, 0.21875, ((0, 8),)),
        "ffn_up": gaussian(splits[12], (D, FF), D ** -0.5, 0.21875, ((0, 8),)),
        "ffn_down": gaussian(splits[13], (FF, D), FF ** -0.5, 0.125, ((0, 8),)),
        "inner_first": gaussian(splits[14], (HEADS, HEAD, INNER), HEAD ** -0.5, 0.75, ((0, 4),), jnp.float32),
        "inner_first_bias": gaussian(splits[15], (HEADS, INNER), 0.3, 1.75, ((0, 4),), jnp.float32),
        "inner_second": gaussian(splits[16], (HEADS, INNER, HEAD), INNER ** -0.5, 0.375, ((0, 4),), jnp.float32),
        "inner_second_bias": gaussian(splits[17], (HEADS, HEAD), 0.3, 1.75, ((0, 4),), jnp.float32),
        "inner_gain": jnp.clip(1.0 + 0.1 * jax.random.normal(splits[18], (HEADS, HEAD), jnp.float32), 0.5, 1.5),
        "inner_shift": gaussian(splits[19], (HEADS, HEAD), 0.3, 1.75, ((0, 4),), jnp.float32),
    }


EPS = 1e-06
RATE = 1.0 / 1024.0
GELU_C = 0.7978845608028654
GELU_K = 0.044715

@jax.custom_vjp
def low(v):
    return lax.optimization_barrier(v.astype(jnp.bfloat16)).astype(jnp.float32)

@jax.custom_vjp
def low_back(v):
    return v

def low_keep(v):
    return (low(v), None)

def low_pass(kept, grad):
    return (grad,)

def back_keep(v):
    return (v, None)

def back_low(kept, grad):
    return (low(grad),)
low.defvjp(low_keep, low_pass)
low_back.defvjp(back_keep, back_low)

def dot_high(left, right):
    return jnp.dot(left, right, precision=lax.Precision.HIGHEST, preferred_element_type=jnp.float32)

def einsum_high(formula, left, right):
    return jnp.einsum(formula, left, right, precision=lax.Precision.HIGHEST)

def gelu_pair(inputs):
    tangent = jnp.tanh(GELU_C * (inputs + GELU_K * inputs * inputs * inputs))
    values_out = 0.5 * inputs * (1.0 + tangent)
    slope = 0.5 * (1.0 + tangent) + 0.5 * inputs * (1.0 - tangent * tangent) * GELU_C * (1.0 + 3.0 * GELU_K * inputs * inputs)
    return (values_out, slope)

def inner_norm(inputs, inner_gain, inner_shift):
    centred = inputs - lax.optimization_barrier(jnp.mean(inputs, -1, keepdims=True))
    spread = lax.rsqrt(lax.optimization_barrier(jnp.mean(centred * centred, -1, keepdims=True)) + EPS)
    normal = centred * spread
    return (normal * inner_gain[:, None, :] + inner_shift[:, None, :], normal, spread)

def mini_step(inner_state, block_in, inner_gain, inner_shift, causal):
    weight_one, bias_one, weight_two, bias_two = inner_state
    query_block, key_block, value_block, rate_block = block_in
    first_pre = einsum_high('gme,gef->gmf', key_block, weight_one) + bias_one[:, None, :]
    first_act, first_slope = gelu_pair(first_pre)
    second_pre = einsum_high('gmf,gfe->gme', first_act, weight_two) + bias_two[:, None, :]
    fitted, normal, spread = inner_norm(second_pre, inner_gain, inner_shift)
    mismatch = fitted - (value_block - key_block)
    grad_normal = mismatch * inner_gain[:, None, :]
    grad_second = spread * (grad_normal - lax.optimization_barrier(jnp.mean(grad_normal, -1, keepdims=True)) - normal * lax.optimization_barrier(jnp.mean(grad_normal * normal, -1, keepdims=True)))
    grad_first = einsum_high('gme,gfe->gmf', grad_second, weight_two) * first_slope
    scaled_first = rate_block[:, :, None] * grad_first
    scaled_second = rate_block[:, :, None] * grad_second
    mask_one = (einsum_high('gme,gne->gmn', query_block, key_block) + 1.0) * causal
    query_pre = einsum_high('gme,gef->gmf', query_block, weight_one) + bias_one[:, None, :] - einsum_high('gmn,gnf->gmf', mask_one, scaled_first)
    query_act = gelu_pair(query_pre)[0]
    mask_two = (einsum_high('gmf,gnf->gmn', query_act, first_act) + 1.0) * causal
    query_out = einsum_high('gmf,gfe->gme', query_act, weight_two) + bias_two[:, None, :] - einsum_high('gmn,gne->gme', mask_two, scaled_second)
    mixed_block = query_block + inner_norm(query_out, inner_gain, inner_shift)[0]
    next_state = (weight_one - einsum_high('gme,gmf->gef', key_block, scaled_first), bias_one - lax.optimization_barrier(jnp.sum(scaled_first, 1)), weight_two - einsum_high('gmf,gme->gfe', first_act, scaled_second), bias_two - lax.optimization_barrier(jnp.sum(scaled_second, 1)))
    return (next_state, mixed_block)

def sequence_mixer(queries, keys_rows, values_rows, rates, inner_state, inner_gain, inner_shift):
    block_count = LENGTH // MINI

    def arrange(tensor):
        return tensor.reshape(block_count, MINI, HEADS, HEAD).transpose(0, 2, 1, 3).reshape(block_count // 16, 16, HEADS, MINI, HEAD)
    rate_blocks = rates.reshape(block_count, MINI, HEADS).transpose(0, 2, 1).reshape(block_count // 16, 16, HEADS, MINI)
    causal = (lax.broadcasted_iota(jnp.int32, (MINI, MINI), 0) >= lax.broadcasted_iota(jnp.int32, (MINI, MINI), 1)).astype(jnp.float32)

    def advance(carried, block_in):
        return mini_step(carried, block_in, inner_gain, inner_shift, causal)

    def group_scan(carried, group_in):
        return lax.scan(advance, carried, group_in)
    mixed_blocks = lax.scan(jax.checkpoint(group_scan), inner_state, (arrange(queries), arrange(keys_rows), arrange(values_rows), rate_blocks))[1]
    return mixed_blocks.reshape(block_count, HEADS, MINI, HEAD).transpose(0, 2, 1, 3).reshape(LENGTH, HEADS * HEAD)

def sequence_forward(weights, inner, token_rows):
    pre_gain, query_weight, key_weight, value_weight, gate_weight, rate_weight, out_weight, post_gain, ffn_gate, ffn_up, ffn_down = weights
    inner_state = (inner[0], inner[1], inner[2], inner[3])
    scale_one = lax.rsqrt(lax.optimization_barrier(jnp.mean(token_rows * token_rows, -1, keepdims=True)) + EPS)
    normed = low(token_rows * scale_one * pre_gain)
    queries = low_back(low(dot_high(normed, query_weight)))
    keys_rows = low_back(low(dot_high(normed, key_weight)))
    values_rows = low_back(low(dot_high(normed, value_weight)))
    gate_logit = low_back(dot_high(normed, gate_weight))
    rate_logit = low_back(dot_high(normed, rate_weight))
    rates = low_back(low(RATE * jax.nn.sigmoid(rate_logit)))
    mixed = low_back(low(sequence_mixer(queries, keys_rows, values_rows, rates, inner_state, inner[4], inner[5])))
    gated = low(gelu_pair(gate_logit)[0] * mixed)
    middle = token_rows + low_back(dot_high(gated, out_weight))
    scale_two = lax.rsqrt(lax.optimization_barrier(jnp.mean(middle * middle, -1, keepdims=True)) + EPS)
    normed_two = low(middle * scale_two * post_gain)
    gate_pre = low_back(dot_high(normed_two, ffn_gate))
    up_pre = low_back(dot_high(normed_two, ffn_up))
    hidden = low(jax.nn.silu(gate_pre) * up_pre)
    return middle + dot_high(hidden, ffn_down)

def reference(tokens, lengths, cotangent, pre_gain, query_weight, key_weight, value_weight, gate_weight, rate_weight, out_weight, post_gain, ffn_gate, ffn_up, ffn_down, inner_first, inner_first_bias, inner_second, inner_second_bias, inner_gain, inner_shift):
    weights = tuple((member.astype(jnp.float32) for member in (pre_gain, query_weight, key_weight, value_weight, gate_weight, rate_weight, out_weight, post_gain, ffn_gate, ffn_up, ffn_down)))
    inner = (inner_first.astype(jnp.float32), inner_first_bias.astype(jnp.float32), inner_second.astype(jnp.float32), inner_second_bias.astype(jnp.float32), inner_gain.astype(jnp.float32), inner_shift.astype(jnp.float32))
    sequences = tokens.astype(jnp.float32).reshape(MICRO, LENGTH, D)

    def forward(weight_set, inner_set, sequence_set):
        checked = jax.checkpoint(sequence_forward)
        return lax.map(lambda token_rows: checked(weight_set, inner_set, token_rows), sequence_set)
    result, pullback = jax.vjp(forward, weights, inner, sequences)
    position = lax.broadcasted_iota(jnp.int32, (MICRO, LENGTH), 1)
    live = (position < lengths.astype(jnp.int32)[:, None]).astype(jnp.float32)
    live_cotangent = cotangent.astype(jnp.float32).reshape(MICRO, LENGTH, D) * live[:, :, None]
    weight_grads, inner_grads, token_grads = pullback(live_cotangent)
    full_shape = tokens.shape
    return (result.astype(jnp.bfloat16).reshape(full_shape), token_grads.astype(jnp.bfloat16).reshape(full_shape), weight_grads[0], weight_grads[1], weight_grads[2], weight_grads[3], weight_grads[4], weight_grads[5], weight_grads[6], weight_grads[7], weight_grads[8], weight_grads[9], weight_grads[10], inner_grads[0], inner_grads[1], inner_grads[2], inner_grads[3], inner_grads[4], inner_grads[5])
```

```python
import functools

import jax
import jax.numpy as jnp
from jax import lax
from jax.experimental import pallas as pl
from jax.experimental.pallas import tpu as pltpu
from jax.sharding import PartitionSpec as P

MINI = 16
EPS = 1e-06
RATE = 1.0 / 1024.0
GELU_C = 0.7978845608028654
GELU_K = 0.044715
VMEM_BYTES = 56 * 1024 * 1024
f32 = jnp.float32
bf16 = jnp.bfloat16

def nn(x,y): return lax.dot_general(x.astype(bf16),y.astype(bf16),(((1,),(0,)),((),())),preferred_element_type=f32)
def nt(x,y): return lax.dot_general(x.astype(bf16),y.astype(bf16),(((1,),(1,)),((),())),preferred_element_type=f32)
def tn(x,y): return lax.dot_general(x.astype(bf16),y.astype(bf16),(((0,),(0,)),((),())),preferred_element_type=f32)
def gelu1(z):
    t=jnp.tanh(GELU_C*z*(1.0+GELU_K*(z*z)))
    return 0.5*z*(1.0+t)
def gelu2(z):
    z2=z*z
    t=jnp.tanh(z*(GELU_C+(GELU_C*GELU_K)*z2))
    h=0.5+0.5*t
    return z*h, h+0.5*z*(1.0-t*t)*(GELU_C+(3.0*GELU_C*GELU_K)*z2)
def gelu3(z):
    z2=z*z
    t=jnp.tanh(z*(GELU_C+(GELU_C*GELU_K)*z2))
    h=0.5+0.5*t
    u=GELU_C+(3.0*GELU_C*GELU_K)*z2
    c=1.0-t*t
    return z*h, h+0.5*z*c*u, c*(u+z*((3.0*GELU_C*GELU_K)*z-t*u*u))

def cat(*xs): return jnp.concatenate(xs,0)
def rs(x): return jnp.sum(x,-1,keepdims=True)*(1.0/64)

def interleave(gens):
    gens=list(gens)
    while gens:
        alive=[]
        for g in gens:
            try:
                next(g); alive.append(g)
            except StopIteration: pass
        gens=alive

def masks():
    lower=lax.broadcasted_iota(jnp.int32,(MINI,MINI),0)>=lax.broadcasted_iota(jnp.int32,(MINI,MINI),1)
    return lower.astype(f32), jnp.where(lower,0.0,1.0)

def fwd_kernel(slots,count,unroll,q_ref,k_ref,v_ref,e_ref,w1_ref,b1_ref,w2_ref,b2_ref,gain_ref,shift_ref,
    mix_ref,w1s_ref,w2s_ref,z1_ref,h_ref,q1_ref,n_ref,g_ref,nq_ref,s_ref,sq_ref,
    W1,B1,W2,B2,Z,ZQ,AP,EP):
    lower,upper=masks()
    steps=q_ref.shape[1]//MINI
    pid=pl.program_id(0)
    @pl.when(pid==0)
    def _():
        for j in range(slots):
            W1[j]=w1_ref[j]; B1[j]=b1_ref[j]; W2[j]=w2_ref[j]; B2[j]=b2_ref[j]
            Z[j]=nn(k_ref[j,:MINI],w1_ref[j])+b1_ref[j]
            ZQ[j]=jnp.zeros((MINI,256),f32); AP[j]=jnp.zeros((MINI,256),bf16); EP[j]=jnp.zeros((MINI,64),bf16)
    def chain(j,i):
        t=pid*count+i
        rows=pl.ds(pl.multiple_of(t*MINI,MINI),MINI)
        prow=pl.ds(pl.multiple_of(jnp.maximum(t-1,0)*MINI,MINI),MINI)
        nrow=pl.ds(pl.multiple_of(jnp.minimum(t+1,steps-1)*MINI,MINI),MINI)
        brow=pl.ds(pl.multiple_of(i*MINI,MINI),MINI)
        gain=gain_ref[j]; shift=shift_ref[j]; g2=gain*gain; mg=rs(g2)
        z1=Z[j]; q1=ZQ[j]; w2=W2[j]; b2=B2[j]
        w2b=w2.astype(bf16)
        Ap=AP[j]; Ep=EP[j]
        A,Ad=gelu2(z1); AQ=gelu1(q1)
        Ab=A.astype(bf16); AQb=AQ.astype(bf16)
        z1_ref[j,brow]=z1.astype(bf16)
        yield
        zz=nt(cat(Ab,AQb),w2b)
        z=zz[:MINI]+b2; qb=zz[MINI:]+b2
        yield
        P2=upper*(nt(AQb,Ap)+1.0)
        K=k_ref[j,rows]; Q=q_ref[j,rows]; Kn=k_ref[j,nrow]
        w1=W1[j]; w1b=w1.astype(bf16); b1=B1[j]
        w1s_ref[j,i]=w1b; w2s_ref[j,i]=w2b
        KQ=cat(Kn,Q)
        KK=nt(KQ,K)+1.0
        L=cat(KK[:MINI].astype(bf16),(lower*KK[MINI:]).astype(bf16),K.T)
        base=nn(KQ,w1b)+b1
        U=gain*(shift-v_ref[j,rows].astype(f32)+K.astype(f32)); mU=rs(U)
        e=e_ref[j,rows]
        yield
        Q2=qb+nn(P2,Ep)
        yield
        zg=z*g2
        mz=rs(z); p0=rs(z*z); p1=rs(zg); p2=rs(z*zg); p3=rs(z*U)
        s=lax.rsqrt(p0-mz*mz+EPS)
        m1=s*(p1-mz*mg)+mU
        m2=s*(s*(p2-2.0*mz*p1+mz*mz*mg)+(p3-mz*mU))
        N=s*(z-mz)
        G=s*(N*(g2-m2)+(U-m1))
        Gb=G.astype(bf16)
        yield
        H=nn(Gb,w2b)
        E2=e*G; E2b=E2.astype(bf16)
        n_ref[j,rows]=N; g_ref[j,rows]=G; s_ref[j,rows]=s
        EP[j]=E2b; AP[j]=Ab
        yield
        W2[j]=w2-tn(E2b,Ab)
        B2[j]=b2-jnp.sum(E2,0,keepdims=True)
        yield
        E1=(e*Ad)*H; E1b=E1.astype(bf16)
        X=nn(L,E1b)
        Z[j]=base[:MINI]-X[:MINI]
        Q1=base[MINI:]-X[MINI:2*MINI]
        ZQ[j]=Q1
        W1[j]=w1-X[2*MINI:]
        B1[j]=b1-jnp.sum(E1,0,keepdims=True)
        h_ref[j,brow]=H.astype(bf16); q1_ref[j,brow]=Q1.astype(bf16)
        yield
        mq=rs(Q2); vq=rs(Q2*Q2)
        sq=lax.rsqrt(vq-mq*mq+EPS)
        Nq=sq*(Q2-mq)
        Qp=q_ref[j,prow].astype(f32)
        mix_ref[j,prow]=(Qp+Nq*gain+shift).astype(bf16)
        nq_ref[j,prow]=Nq; sq_ref[j,prow]=sq
    @pl.loop(0,count//unroll)
    def _(i):
        for u in range(unroll):
            interleave(chain(j,i*unroll+u) for j in range(slots))
    @pl.when(pid==pl.num_programs(0)-1)
    def _():
        for j in range(slots):
            prow=pl.ds((steps-1)*MINI,MINI)
            AQb=gelu1(ZQ[j]).astype(bf16)
            Q2=nt(AQb,W2[j])+B2[j]+nn(upper*(nt(AQb,AP[j])+1.0),EP[j])
            mq=rs(Q2); vq=rs(Q2*Q2)
            sq=lax.rsqrt(vq-mq*mq+EPS)
            Nq=sq*(Q2-mq)
            mix_ref[j,prow]=(q_ref[j,prow].astype(f32)+Nq*gain_ref[j]+shift_ref[j]).astype(bf16)
            nq_ref[j,prow]=Nq; sq_ref[j,prow]=sq

def fwd_call(q,k,v,e,w1,b1,w2,b2,gain,shift,block=256,unroll=1,**kw):
    slots,length,_=q.shape
    count=block//MINI; nb=length//block; steps=length//MINI
    row=lambda w: pl.BlockSpec((slots,block,w),lambda i:(0,i,0))
    full=lambda s: pl.BlockSpec(s,lambda i:(0,)*len(s),pipeline_mode=pl.Buffered(1))
    r64=full((slots,length,64)); r1=full((slots,length,1))
    st=pl.BlockSpec((slots,count,64,256),lambda i:(0,i,0,0))
    S=jax.ShapeDtypeStruct
    return pl.pallas_call(functools.partial(fwd_kernel,slots,count,unroll),
        grid=(nb,),
        in_specs=[r64]*3+[r1]+[full(a.shape) for a in (w1,b1,w2,b2,gain,shift)],
        out_specs=[r64,st,st,row(256),row(256),row(256),r64,r64,r64,r1,r1],
        out_shape=[S((slots,length,64),bf16),S((slots,steps,64,256),bf16),S((slots,steps,64,256),bf16)]+[S((slots,length,256),bf16)]*3+[S((slots,length,64),f32)]*3+[S((slots,length,1),f32)]*2,
        scratch_shapes=[pltpu.VMEM((slots,64,256),f32),pltpu.VMEM((slots,1,256),f32),pltpu.VMEM((slots,64,256),f32),pltpu.VMEM((slots,1,64),f32),pltpu.VMEM((slots,MINI,256),f32),pltpu.VMEM((slots,MINI,256),f32),pltpu.VMEM((slots,MINI,256),bf16),pltpu.VMEM((slots,MINI,64),bf16)],
        compiler_params=pltpu.CompilerParams(dimension_semantics=("arbitrary",),vmem_limit_bytes=VMEM_BYTES),
        name="inner_forward",**kw)(q,k,v,e,w1,b1,w2,b2,gain,shift)


def bwd_kernel(slots,count,unroll,q_ref,k_ref,v_ref,e_ref,do_ref,n_ref,g_ref,nq_ref,s_ref,sq_ref,w1s_ref,w2s_ref,z1_ref,h_ref,q1_ref,gain_ref,shift_ref,
    dq_ref,dk_ref,dv_ref,de_ref,dw1_ref,db1_ref,dw2_ref,db2_ref,dgn_ref,dsh_ref,
    DW1,DB1,G2,DB2,KD,DGN,DSH,DGQ,DSQ,
    sA,sAd,sHA,sGZ,sE1,sE2,sW1,sW2,sR1,sR2,sDA,sQ1,sQ2,sAQ,sb1,sb2):
    lower,_=masks()
    steps=q_ref.shape[1]//MINI
    pid=pl.program_id(0); nb=pl.num_programs(0)
    @pl.when(pid==0)
    def _():
        for r in (DW1,DB1,G2,DB2,KD,DGN,DSH,DGQ,DSQ):
            r[...]=jnp.zeros(r.shape,r.dtype)
        for r in (sA,sAd,sHA,sGZ,sE1,sE2,sW1,sW2,sR1,sR2,sDA,sQ1,sQ2,sAQ,sb1,sb2):
            r[0]=jnp.zeros(r.shape[1:],r.dtype)
    def crit(j,p,t):
        rows=pl.ds(pl.multiple_of(jnp.minimum(t,steps-1)*MINI,MINI),MINI)
        prow=pl.ds(pl.multiple_of(jnp.maximum(t-1,0)*MINI,MINI),MINI)
        gain=gain_ref[j]; shift=shift_ref[j]; g2=gain*gain; mg=rs(g2)
        e=e_ref[j,rows]
        nE1=sR1[p,j]+KD[j]
        dgZ1=(-e)*nE1
        dH=dgZ1*sAd[p,j]
        dHb=dH.astype(bf16)
        w2b=sW2[p,j]
        G2f=G2[j]; G2b=G2f.astype(bf16)
        Ab=sA[p,j]; E2b=sE2[p,j]
        yield
        a1=nt(Ab,G2b)
        yP=nt(dHb,w2b)
        yield
        N=n_ref[j,rows]; G=g_ref[j,rows]; s=s_ref[j,rows]
        K=k_ref[j,rows]; Q=q_ref[j,rows]; Kp=k_ref[j,prow]
        T=shift-v_ref[j,rows].astype(f32)+K.astype(f32)
        U=gain*T
        gN=N*g2
        c1=rs(gN); c2=rs(gN*N); mU=rs(U); UN=rs(U*N)
        a=gN+U; ma=c1+mU; m2=c2+UN
        a2=nn(E2b,G2b)
        E1b=sE1[p,j]; dQ1b=sQ1[p,j]
        DW=DW1[j]; DWb=DW.astype(bf16)
        KDb=nn(Kp,DWb)+DB1[j]
        yield
        a3=nt(E1b,DWb)
        X1=(lower*nt(dQ1b,E1b)).astype(bf16)
        L2=cat((nt(Kp,cat(Q,K))+1.0).astype(bf16),cat(Q,K).T)
        yield
        nE2=sR2[p,j]+a1+DB2[j]
        y=yP-e*nE2
        yg=y*g2; yn=y*N
        ym=rs(y); yN=rs(yn); yG=rs(y*G); ygm=rs(yg); ygN=rs(yg*N)
        mdy=s*ym; mdyN=s*yN
        da=s*y-mdy-N*mdyN
        sN=s*ygN-mdy*c1-mdyN*c2-2.0*m2*mdyN
        mN=s*ygm-mdy*mg-mdyN*c1-ma*mdyN-m2*mdy
        kap=yG+sN
        dN=da*g2-a*mdyN-(s*m2)*y
        dZc=s*(dN-mN-N*kap)
        dZb=dZc.astype(bf16)
        dT=da*gain
        yield
        dA=nn(dZb,w2b)+sDA[p,j]-a2
        yield
        G2[j]=G2f+tn(cat(sQ2[p,j],G.astype(bf16),dZb),cat(sAQ[p,j],dHb,Ab))
        DB2[j]=DB2[j]+sb2[p,j]+jnp.sum(dZc,0,keepdims=True)
        dQs=nn(X1,K); dKs=tn(X1,Q)
        dv_ref[j,rows]=(-dT).astype(bf16)
        dO=do_ref[j,rows].astype(f32)
        DGN[j]=DGN[j]+da*(2.0*gain*N+T)
        DSH[j]=DSH[j]+dT
        de_ref[j,rows]=-(jnp.sum(nE1*sGZ[p,j],-1,keepdims=True)+jnp.sum(nE2*G,-1,keepdims=True))
        yield
        dZ1=dA*sAd[p,j]+dgZ1*sHA[p,j]
        dZ1b=dZ1.astype(bf16)
        dd=cat(dQ1b,dZ1b)
        X=nn(L2,dd)
        KD[j]=KDb+X[:MINI]
        DW1[j]=DW+X[MINI:]
        DB1[j]=DB1[j]+sb1[p,j]+jnp.sum(dZ1,0,keepdims=True)
        yield
        qk=nt(dd,sW1[p,j])
        dq_ref[j,rows]=(dO+qk[:MINI]-dQs).astype(bf16)
        dk_ref[j,rows]=(qk[MINI:]-dKs-a3+dT).astype(bf16)
    def qside(j,p,t,i):
        rows=pl.ds(pl.multiple_of(t*MINI,MINI),MINI)
        brow=pl.ds(pl.multiple_of(i*MINI,MINI),MINI)
        gain=gain_ref[j]
        dO=do_ref[j,rows].astype(f32); Nq=nq_ref[j,rows]
        dNq=dO*gain
        dQ2=sq_ref[j,rows]*(dNq-rs(dNq)-Nq*rs(dNq*Nq))
        dQ2b=dQ2.astype(bf16)
        A,Ad,Add=gelu3(z1_ref[j,brow].astype(f32))
        AQ,AQd=gelu2(q1_ref[j,brow].astype(f32))
        H=h_ref[j,brow].astype(f32); e=e_ref[j,rows]
        Ab=A.astype(bf16); AQb=AQ.astype(bf16)
        gZ1=H*Ad
        E1b=(e*gZ1).astype(bf16); E2b=(e*g_ref[j,rows]).astype(bf16)
        w1b=w1s_ref[j,i]; w2b=w2s_ref[j,i]
        yield
        sA[p,j]=Ab; sAd[p,j]=Ad; sHA[p,j]=H*Add; sGZ[p,j]=gZ1; sE1[p,j]=E1b; sE2[p,j]=E2b; sW1[p,j]=w1b; sW2[p,j]=w2b; sAQ[p,j]=AQb
        sQ2[p,j]=dQ2b; sb2[p,j]=jnp.sum(dQ2,0,keepdims=True)
        DGQ[j]=DGQ[j]+dO*Nq; DSQ[j]=DSQ[j]+dO
        Q=q_ref[j,rows]; K=k_ref[j,rows]
        P1=(lower*(nt(Q,K)+1.0)).astype(bf16)
        P2=(lower*(nt(AQb,Ab)+1.0)).astype(bf16)
        yield
        X2=(lower*nt(dQ2b,E2b)).astype(bf16)
        yield
        b1=nn(dQ2b,w2b)
        yield
        sR2[p,j]=tn(P2,dQ2b)
        yield
        dAQ=b1-nn(X2,Ab)
        sDA[p,j]=-tn(X2,AQb)
        yield
        yield
        dQ1=dAQ*AQd
        dQ1b=dQ1.astype(bf16)
        sQ1[p,j]=dQ1b; sb1[p,j]=jnp.sum(dQ1,0,keepdims=True)
        sR1[p,j]=tn(P1,dQ1b)
    @pl.loop(0,count//unroll)
    def _(i):
        for u in range(unroll):
            ii=count-1-(i*unroll+u)
            t=(nb-1-pid)*count+ii
            interleave([crit(j,u%2,t+1) for j in range(slots)]+[qside(j,(u+1)%2,t,ii) for j in range(slots)])
    @pl.when(pid==nb-1)
    def _():
        interleave([crit(j,0,jnp.int32(0)) for j in range(slots)])
        for j in range(slots):
            dw1_ref[j]=DW1[j]; db1_ref[j]=DB1[j]; dw2_ref[j]=G2[j]; db2_ref[j]=DB2[j]
            dgn_ref[j]=jnp.sum(DGN[j]+DGQ[j],0,keepdims=True); dsh_ref[j]=jnp.sum(DSH[j]+DSQ[j],0,keepdims=True)

def bwd_call(q,k,v,e,dO,n,g,nq,s,sq,w1s,w2s,z1,h,q1,gain,shift,block=256,unroll=2,**kw):
    slots,length,_=q.shape
    count=block//MINI; nb=length//block; steps=length//MINI
    row=lambda w: pl.BlockSpec((slots,block,w),lambda i:(0,nb-1-i,0))
    full=lambda s: pl.BlockSpec(s,lambda i:(0,)*len(s),pipeline_mode=pl.Buffered(1))
    r64=full((slots,length,64)); r1=full((slots,length,1))
    st=pl.BlockSpec((slots,count,64,256),lambda i:(0,nb-1-i,0,0))
    S=jax.ShapeDtypeStruct
    outs=[((slots,64,256),f32),((slots,1,256),f32),((slots,64,256),f32),((slots,1,64),f32),((slots,1,64),f32),((slots,1,64),f32)]
    V=lambda *s,d=f32: pltpu.VMEM(s,d)
    return pl.pallas_call(functools.partial(bwd_kernel,slots,count,unroll),
        grid=(nb,),
        in_specs=[r64]*3+[r1]+[r64]*4+[r1]*2+[st,st]+[row(256)]*3+[full(gain.shape)]*2,
        out_specs=[r64]*3+[r1]+[full(o[0]) for o in outs],
        out_shape=[S((slots,length,64),bf16)]*3+[S((slots,length,1),f32)]+[S(*o) for o in outs],
        scratch_shapes=[V(slots,64,256),V(slots,1,256),V(slots,64,256),V(slots,1,64),V(slots,MINI,256),V(slots,MINI,64),V(slots,MINI,64),V(slots,MINI,64),V(slots,MINI,64),
          V(2,slots,MINI,256,d=bf16),V(2,slots,MINI,256),V(2,slots,MINI,256),V(2,slots,MINI,256),V(2,slots,MINI,256,d=bf16),V(2,slots,MINI,64,d=bf16),
          V(2,slots,64,256,d=bf16),V(2,slots,64,256,d=bf16),V(2,slots,MINI,256),V(2,slots,MINI,64),V(2,slots,MINI,256),V(2,slots,MINI,256,d=bf16),V(2,slots,MINI,64,d=bf16),V(2,slots,MINI,256,d=bf16),V(2,slots,1,256),V(2,slots,1,64)],
        compiler_params=pltpu.CompilerParams(dimension_semantics=("arbitrary",),vmem_limit_bytes=VMEM_BYTES),
        name="inner_backward",**kw)(q,k,v,e,dO,n,g,nq,s,sq,w1s,w2s,z1,h,q1,gain,shift)


def rms_back(grad_scaled, inputs, scale):
    return scale * (
        grad_scaled - inputs * scale * scale * jnp.mean(grad_scaled * inputs, -1, keepdims=True)
    )


def gather(block):
    return lax.all_gather(block, "fsdp", axis=0, tiled=True)


def scatter_sum(block, axis):
    return lax.psum_scatter(block.astype(bf16), axis, scatter_dimension=0, tiled=True).astype(f32)


def swap(block, axes):
    return lax.all_to_all(block, axes, split_axis=0, concat_axis=0, tiled=True)


def pad_to(array_in, size, dim):
    widths = [(0, 0)] * array_in.ndim
    widths[dim] = (0, size - array_in.shape[dim])
    return jnp.pad(array_in, widths)


def shards(
    tokens,
    lengths,
    cotangent,
    pre_gain,
    query_weight,
    key_weight,
    value_weight,
    gate_weight,
    rate_weight,
    out_weight,
    post_gain,
    ffn_gate,
    ffn_up,
    ffn_down,
    inner_first,
    inner_first_bias,
    inner_second,
    inner_second_bias,
    inner_gain,
    inner_shift,
):
    micro, _, rows, width = tokens.shape
    local, head, inner = inner_first.shape
    ff = ffn_gate.shape[1]
    Z = lax.axis_size("sp")
    S = lax.axis_size("fsdp")
    z = lax.axis_index("sp")
    d = lax.axis_index("fsdp")
    groups = S // micro
    slots = -(-local // groups)
    order = [[g for g in range(h, local, groups)] for h in range(groups)]
    flat = [g for part in order for g in part]
    span = 3 * head
    tiles = -(-slots * span // 128)
    piece = Z * rows
    length = S * piece
    total = micro * rows
    own = query_weight.shape[0]
    extra = local * span
    packed_width = -(-(extra + local + 2) // 128) * 128

    def columns(weight, count):
        return lax.dynamic_slice_in_dim(weight, z * count, count, 1)

    q_w, k_w, v_w = (
        columns(w, local * head).reshape(own, local, head)
        for w in (query_weight, key_weight, value_weight)
    )
    r_w = columns(rate_weight, local)
    parts = []
    for g in flat:
        parts += [q_w[:, g], k_w[:, g], v_w[:, g]]
    parts += [r_w, pre_gain[:, None], post_gain[:, None]]
    packed = pad_to(jnp.concatenate(parts, 1), packed_width, 1)
    front = gather(packed)
    all_tokens = lax.all_gather(tokens[:, 0], "sp", axis=0)
    rear_in = (out_weight, gate_weight, ffn_gate, ffn_up, ffn_down)
    rear_in, front, all_tokens = lax.optimization_barrier((rear_in, front, all_tokens))
    pre_full = front[:, extra + local].astype(f32)[None]
    post_full = front[:, extra + local + 1].astype(f32)[None]
    token_rows = all_tokens.reshape(Z * total, width).astype(f32)
    scale_one = lax.rsqrt(jnp.mean(token_rows * token_rows, -1, keepdims=True) + EPS)
    normed = (token_rows * scale_one * pre_full).astype(bf16)
    projected = nn(normed, front)
    rate_sig = jax.nn.sigmoid(projected[:, extra : extra + local])
    rate_rows = (RATE * rate_sig).astype(bf16).reshape(Z, micro, rows, local)
    low = projected.astype(bf16).reshape(Z, micro, rows, packed_width)
    rate_tiles = slots * piece // 128

    def pack_tiles(pieces, rates):
        body = pieces.reshape(S, piece, tiles, 128).transpose(0, 2, 1, 3)
        tail = pad_to(rates.reshape(S, rate_tiles, 128), 16 * (-(-rate_tiles // 16)), 1)
        return jnp.concatenate([body.reshape(S, tiles * piece, 128), tail], 1)

    low_parts = []
    rate_parts = []
    start = 0
    for part in order:
        stop = min(start + tiles * 128, packed_width)
        low_parts.append(pad_to(low[..., start:stop], tiles * 128, 3))
        start += len(part) * span
        here = [rate_rows[..., g : g + 1] for g in part] + [jnp.zeros_like(rate_rows[..., :1])] * (slots - len(part))
        rate_parts.append(jnp.concatenate(here, 3))
    send_low = jnp.stack(low_parts).transpose(0, 2, 1, 3, 4).reshape(S, piece, tiles * 128)
    send_rate = jnp.stack(rate_parts).transpose(0, 2, 4, 1, 3).reshape(S, slots, piece)
    arrived = swap(pack_tiles(send_low, send_rate), "fsdp")
    body = arrived[:, : tiles * piece].reshape(S, tiles, piece, 128)

    def chain_rows(index):
        out = []
        for j in range(slots):
            lane = j * span + index * head
            out.append(body[:, lane // 128, :, lane % 128 : lane % 128 + head].reshape(length, head))
        return jnp.stack(out)

    q, k, v = chain_rows(0), chain_rows(1), chain_rows(2)
    e = arrived[:, tiles * piece : tiles * piece + rate_tiles].reshape(S, slots, piece)
    e = e.transpose(1, 0, 2).reshape(slots, length, 1).astype(f32)

    half = d // micro
    heads_here = [jnp.minimum(half + j * groups, local - 1) for j in range(slots)]

    def of_slots(array_in):
        return jnp.stack([lax.dynamic_index_in_dim(array_in, g, 0, keepdims=False) for g in heads_here])

    w1 = of_slots(inner_first)
    b1 = of_slots(inner_first_bias)[:, None]
    w2 = of_slots(inner_second)
    w2 = (w2 - jnp.mean(w2, -1, keepdims=True)).transpose(0, 2, 1)
    b2 = of_slots(inner_second_bias)[:, None]
    b2 = b2 - jnp.mean(b2, -1, keepdims=True)
    gain = of_slots(inner_gain)[:, None]
    shift = of_slots(inner_shift)[:, None]
    mix, w1s, w2s, z1, h, q1, n, g_, nq, s, sq = fwd_call(q, k, v, e, w1, b1, w2, b2, gain, shift, unroll=2)

    out_in, gate_in, fgate_in, fup_in, down_in = rear_in
    rear = gather(jnp.concatenate([out_in, gate_in, fgate_in, fup_in], 1))
    out_full = rear[:, :width]
    gate_full = rear[:, width : 2 * width]
    fgate_full = rear[:, 2 * width : 2 * width + ff]
    fup_full = rear[:, 2 * width + ff :]
    down_full = gather(down_in)

    def to_tokens(chains):
        send = chains.reshape(slots, S, Z, rows, head).transpose(1, 2, 3, 0, 4)
        got = swap(send.reshape(S * Z, rows, slots * head), ("fsdp", "sp"))
        got = got.reshape(groups, micro, Z, rows, slots, head).transpose(1, 3, 2, 4, 0, 5)
        return got.reshape(total, Z, slots * groups, head)[:, :, :local].reshape(total, width)

    def to_chains(block):
        send = pad_to(block.reshape(micro, rows, Z, local, head), slots * groups, 3)
        send = send.reshape(micro, rows, Z, slots, groups, head).transpose(4, 0, 2, 1, 3, 5)
        got = swap(send.reshape(S * Z, rows, slots * head), ("fsdp", "sp"))
        return got.reshape(length, slots, head).transpose(1, 0, 2)

    mixed_rows = to_tokens(mix).astype(f32)
    own_tokens = tokens.reshape(total, width).astype(f32)
    own_normed = lax.dynamic_slice_in_dim(normed, z * total, total, 0)
    gate_logit = nn(own_normed, gate_full)
    gate_act, gate_slope = gelu2(gate_logit)
    gated = (gate_act * mixed_rows).astype(bf16)
    middle = own_tokens + nn(gated, out_full)
    scale_two = lax.rsqrt(jnp.mean(middle * middle, -1, keepdims=True) + EPS)
    normed_two = (middle * scale_two * post_full).astype(bf16)
    gate_pre = nn(normed_two, fgate_full)
    up_pre = nn(normed_two, fup_full)
    gate_sig = jax.nn.sigmoid(gate_pre)
    silu_act = gate_pre * gate_sig
    hidden = (silu_act * up_pre).astype(bf16)
    output = (middle + nn(hidden, down_full)).astype(bf16)

    position = d * piece + z * rows + lax.broadcasted_iota(jnp.int32, (micro, rows), 1)
    live = (position < lengths[:, None]).astype(f32).reshape(total, 1)
    grad_out = cotangent.reshape(total, width).astype(f32) * live
    grad_low = grad_out.astype(bf16)
    grad_hidden = nt(grad_low, down_full)
    grad_gate_pre = (grad_hidden * up_pre * gate_sig * (1.0 + gate_pre * (1.0 - gate_sig))).astype(bf16)
    grad_up_pre = (grad_hidden * silu_act).astype(bf16)
    grad_normed_two = nt(grad_gate_pre, fgate_full) + nt(grad_up_pre, fup_full)
    grad_middle = grad_out + rms_back(grad_normed_two * post_full, middle, scale_two)
    grad_branch = grad_middle.astype(bf16)
    grad_gated = nt(grad_branch, out_full)
    grad_mixed = (grad_gated * gate_act).astype(bf16)
    grad_gate_logit = (grad_gated * mixed_rows * gate_slope).astype(bf16)
    d_mix = to_chains(grad_mixed)
    rear_grad = jnp.concatenate(
        [
            tn(gated, grad_branch).astype(bf16),
            tn(own_normed, grad_gate_logit).astype(bf16),
            tn(normed_two, grad_gate_pre).astype(bf16),
            tn(normed_two, grad_up_pre).astype(bf16),
        ],
        1,
    )
    down_grad = tn(hidden, grad_low)
    rear_sum = scatter_sum(rear_grad, "fsdp")
    down_sum = scatter_sum(down_grad, "fsdp")
    rear_sum = lax.psum(rear_sum.astype(bf16), "sp").astype(f32)
    down_sum = lax.psum(down_sum.astype(bf16), "sp").astype(f32)
    grad_normed_gate = nt(grad_gate_logit, gate_full)

    dq, dk, dv, de, dw1, db1, dw2, db2, dgn, dsh = bwd_call(
        q, k, v, e, d_mix, n, g_, nq, s, sq, w1s, w2s, z1, h, q1, gain, shift
    )
    dw2 = dw2 - jnp.mean(dw2, 1, keepdims=True)
    db2 = db2 - jnp.mean(db2, -1, keepdims=True)
    small = jnp.concatenate([db1[:, 0], db2[:, 0], dgn[:, 0], dsh[:, 0], jnp.zeros((slots, head), f32)], 1)
    inner_rows = jnp.concatenate([dw1, dw2, pad_to(small.reshape(slots, 2, inner), 8, 1)], 1)
    spread = jnp.zeros((local,) + inner_rows.shape[1:], f32)
    for j in range(slots):
        here = jnp.arange(local)[:, None, None] == half + j * groups
        spread = spread + jnp.where(here, inner_rows[j][None], 0.0)
    inner_sum = lax.psum(spread.astype(bf16), "fsdp").astype(f32)

    grads = jnp.stack([dq, dk, dv], 2).transpose(1, 0, 2, 3).reshape(S, piece, slots * span)
    rates_back = de[..., 0].astype(bf16).reshape(slots, S, piece).transpose(1, 0, 2)
    arrived = swap(pack_tiles(pad_to(grads, tiles * 128, 2), rates_back), "fsdp")
    body = arrived[:, : tiles * piece].reshape(groups, micro, tiles, Z, rows, 128)
    body = body.transpose(3, 1, 4, 0, 2, 5).reshape(Z * total, groups, tiles * 128)
    back = arrived[:, tiles * piece : tiles * piece + rate_tiles].reshape(groups, micro, slots, Z, rows)
    back = back.transpose(3, 1, 4, 2, 0).reshape(Z * total, slots * groups)[:, :local].astype(f32)
    grad_rate_logit = (back * RATE * rate_sig * (1.0 - rate_sig)).astype(bf16)
    grad_packed = pad_to(
        jnp.concatenate(
            [body[:, i, : len(part) * span] for i, part in enumerate(order) if part] + [grad_rate_logit], 1
        ),
        packed_width,
        1,
    )
    weight_grad = scatter_sum(tn(normed, grad_packed), "fsdp")
    weight_all = lax.all_gather(weight_grad.astype(bf16), "sp", axis=1).astype(f32)
    pieces = weight_all[..., :extra].reshape(own, Z, local, 3, head)
    pieces = jnp.stack([pieces[:, :, flat.index(g)] for g in range(local)], 2)
    query_grad, key_grad, value_grad = (pieces[:, :, :, i].reshape(own, width) for i in range(3))
    rate_grad = weight_all[..., extra : extra + local].reshape(own, Z * local)
    grad_normed = scatter_sum(nt(grad_packed, front), "sp") + grad_normed_gate
    own_scale = lax.dynamic_slice_in_dim(scale_one, z * total, total, 0)
    tokens_grad = (grad_middle + rms_back(grad_normed * pre_full, own_tokens, own_scale)).astype(bf16)

    out_grad = rear_sum[:, :width]
    gate_grad = rear_sum[:, width : 2 * width]
    fgate_grad = rear_sum[:, 2 * width : 2 * width + ff]
    fup_grad = rear_sum[:, 2 * width + ff :]

    def row_dot(grad, weight):
        return jnp.sum(grad * weight.astype(f32), -1)

    pre_grad = (
        row_dot(query_grad, query_weight)
        + row_dot(key_grad, key_weight)
        + row_dot(value_grad, value_weight)
        + row_dot(gate_grad, gate_weight)
        + row_dot(rate_grad, rate_weight)
    ) / pre_gain.astype(f32)
    post_grad = (row_dot(fgate_grad, ffn_gate) + row_dot(fup_grad, ffn_up)) / post_gain.astype(f32)

    tail = inner_sum[:, 2 * head : 2 * head + 2].reshape(local, 2 * inner)
    return (
        output.reshape(tokens.shape),
        tokens_grad.reshape(tokens.shape),
        pre_grad,
        query_grad,
        key_grad,
        value_grad,
        gate_grad,
        rate_grad,
        out_grad,
        post_grad,
        fgate_grad,
        fup_grad,
        down_sum,
        inner_sum[:, :head],
        tail[:, :inner],
        inner_sum[:, head : 2 * head].transpose(0, 2, 1),
        tail[:, inner : inner + head],
        tail[:, inner + head : inner + 2 * head],
        tail[:, inner + 2 * head : inner + 3 * head],
    )


def solution(mesh):
    return jax.shard_map(
        shards,
        mesh=mesh,
        in_specs=(
            P(None, "fsdp", "sp", None),
            P(),
            P(None, "fsdp", "sp", None),
            P("fsdp"),
            P("fsdp", None),
            P("fsdp", None),
            P("fsdp", None),
            P("fsdp", None),
            P("fsdp", None),
            P("fsdp", None),
            P("fsdp"),
            P("fsdp", None),
            P("fsdp", None),
            P("fsdp", None),
            P("sp", None, None),
            P("sp", None),
            P("sp", None, None),
            P("sp", None),
            P("sp", None),
            P("sp", None),
        ),
        out_specs=(
            P(None, "fsdp", "sp", None),
            P(None, "fsdp", "sp", None),
            P("fsdp"),
            P("fsdp", None),
            P("fsdp", None),
            P("fsdp", None),
            P("fsdp", None),
            P("fsdp", None),
            P("fsdp", None),
            P("fsdp"),
            P("fsdp", None),
            P("fsdp", None),
            P("fsdp", None),
            P("sp", None, None),
            P("sp", None),
            P("sp", None, None),
            P("sp", None),
            P("sp", None),
            P("sp", None),
        ),
        check_vma=False,
    )
```

```python
import functools

import jax
import jax.numpy as jnp
from jax import lax
from jax.experimental import pallas as pl
from jax.experimental.pallas import tpu as pltpu
from jax.sharding import PartitionSpec as P

MINI = 16
EPS = 1e-06
RATE = 1.0 / 1024.0
GELU_C = 0.7978845608028654
GELU_K = 0.044715
VMEM_BYTES = 56 * 1024 * 1024
f32 = jnp.float32
bf16 = jnp.bfloat16

def nn(x,y): return lax.dot_general(x.astype(bf16),y.astype(bf16),(((1,),(0,)),((),())),preferred_element_type=f32)
def nt(x,y): return lax.dot_general(x.astype(bf16),y.astype(bf16),(((1,),(1,)),((),())),preferred_element_type=f32)
def tn(x,y): return lax.dot_general(x.astype(bf16),y.astype(bf16),(((0,),(0,)),((),())),preferred_element_type=f32)
def gelu1(z):
    t=jnp.tanh(GELU_C*z*(1.0+GELU_K*(z*z)))
    return 0.5*z*(1.0+t)
def gelu2(z):
    z2=z*z
    t=jnp.tanh(z*(GELU_C+(GELU_C*GELU_K)*z2))
    h=0.5+0.5*t
    return z*h, h+0.5*z*(1.0-t*t)*(GELU_C+(3.0*GELU_C*GELU_K)*z2)
def gelu3(z):
    z2=z*z
    t=jnp.tanh(z*(GELU_C+(GELU_C*GELU_K)*z2))
    h=0.5+0.5*t
    u=GELU_C+(3.0*GELU_C*GELU_K)*z2
    c=1.0-t*t
    return z*h, h+0.5*z*c*u, c*(u+z*((3.0*GELU_C*GELU_K)*z-t*u*u))

def cat(*xs): return jnp.concatenate(xs,0)
def rs(x): return jnp.sum(x,-1,keepdims=True)*(1.0/64)

def interleave(gens):
    gens=list(gens)
    while gens:
        alive=[]
        for g in gens:
            try:
                next(g); alive.append(g)
            except StopIteration: pass
        gens=alive

def masks():
    lower=lax.broadcasted_iota(jnp.int32,(MINI,MINI),0)>=lax.broadcasted_iota(jnp.int32,(MINI,MINI),1)
    return lower.astype(f32), jnp.where(lower,0.0,1.0)

def fwd_kernel(slots,count,unroll,q_ref,k_ref,v_ref,e_ref,w1_ref,b1_ref,w2_ref,b2_ref,gain_ref,shift_ref,
    mix_ref,w1s_ref,w2s_ref,z1_ref,h_ref,q1_ref,n_ref,g_ref,nq_ref,
    W1,B1,W2,B2,Z,ZQ,AP,EP):
    lower,upper=masks()
    steps=q_ref.shape[1]//MINI
    pid=pl.program_id(0)
    @pl.when(pid==0)
    def _():
        for j in range(slots):
            W1[j]=w1_ref[j]; B1[j]=b1_ref[j]; W2[j]=w2_ref[j]; B2[j]=b2_ref[j]
            Z[j]=nn(k_ref[j,:MINI],w1_ref[j])+b1_ref[j]
            ZQ[j]=jnp.zeros((MINI,256),f32); AP[j]=jnp.zeros((MINI,256),bf16); EP[j]=jnp.zeros((MINI,64),bf16)
    def chain(j,i):
        t=pid*count+i
        rows=pl.ds(pl.multiple_of(t*MINI,MINI),MINI)
        prow=pl.ds(pl.multiple_of(jnp.maximum(t-1,0)*MINI,MINI),MINI)
        nrow=pl.ds(pl.multiple_of(jnp.minimum(t+1,steps-1)*MINI,MINI),MINI)
        brow=pl.ds(pl.multiple_of(i*MINI,MINI),MINI)
        gain=gain_ref[j]; shift=shift_ref[j]; g2=gain*gain; mg=rs(g2)
        z1=Z[j]; q1=ZQ[j]; w2=W2[j]; b2=B2[j]
        w2b=w2.astype(bf16)
        Ap=AP[j]; Ep=EP[j]
        A,Ad=gelu2(z1); AQ=gelu1(q1)
        Ab=A.astype(bf16); AQb=AQ.astype(bf16)
        z1_ref[j,brow]=z1.astype(bf16)
        yield
        zz=nt(cat(Ab,AQb),w2b)
        z=zz[:MINI]+b2; qb=zz[MINI:]+b2
        yield
        P2=upper*(nt(AQb,Ap)+1.0)
        K=k_ref[j,rows]; Q=q_ref[j,rows]; Kn=k_ref[j,nrow]
        w1=W1[j]; w1b=w1.astype(bf16); b1=B1[j]
        w1s_ref[j,i]=w1b; w2s_ref[j,i]=w2b
        KQ=cat(Kn,Q)
        KK=nt(KQ,K)+1.0
        L=cat(KK[:MINI].astype(bf16),(lower*KK[MINI:]).astype(bf16),K.T)
        base=nn(KQ,w1b)+b1
        U=gain*(shift-v_ref[j,rows].astype(f32)+K.astype(f32)); mU=rs(U)
        e=e_ref[j,rows]
        yield
        Q2=qb+nn(P2,Ep)
        yield
        zg=z*g2
        mz=rs(z); p0=rs(z*z); p1=rs(zg); p2=rs(z*zg); p3=rs(z*U)
        s=lax.rsqrt(p0-mz*mz+EPS)
        m1=s*(p1-mz*mg)+mU
        m2=s*(s*(p2-2.0*mz*p1+mz*mz*mg)+(p3-mz*mU))
        N=s*(z-mz)
        G=s*(N*(g2-m2)+(U-m1))
        Gb=G.astype(bf16)
        yield
        H=nn(Gb,w2b)
        E2=e*G; E2b=E2.astype(bf16)
        n_ref[j,rows]=(z-mz).astype(bf16); g_ref[j,rows]=Gb
        EP[j]=E2b; AP[j]=Ab
        yield
        W2[j]=w2-tn(E2b,Ab)
        B2[j]=b2-jnp.sum(E2,0,keepdims=True)
        yield
        E1=(e*Ad)*H; E1b=E1.astype(bf16)
        X=nn(L,E1b)
        Z[j]=base[:MINI]-X[:MINI]
        Q1=base[MINI:]-X[MINI:2*MINI]
        ZQ[j]=Q1
        W1[j]=w1-X[2*MINI:]
        B1[j]=b1-jnp.sum(E1,0,keepdims=True)
        h_ref[j,brow]=H.astype(bf16); q1_ref[j,brow]=Q1.astype(bf16)
        yield
        mq=rs(Q2); vq=rs(Q2*Q2)
        sq=lax.rsqrt(vq-mq*mq+EPS)
        Nq=sq*(Q2-mq)
        Qp=q_ref[j,prow].astype(f32)
        mix_ref[j,prow]=(Qp+Nq*gain+shift).astype(bf16)
        nq_ref[j,prow]=(Q2-mq).astype(bf16)
    @pl.loop(0,count//unroll)
    def _(i):
        for u in range(unroll):
            interleave(chain(j,i*unroll+u) for j in range(slots))
    @pl.when(pid==pl.num_programs(0)-1)
    def _():
        for j in range(slots):
            prow=pl.ds((steps-1)*MINI,MINI)
            AQb=gelu1(ZQ[j]).astype(bf16)
            Q2=nt(AQb,W2[j])+B2[j]+nn(upper*(nt(AQb,AP[j])+1.0),EP[j])
            mq=rs(Q2); vq=rs(Q2*Q2)
            sq=lax.rsqrt(vq-mq*mq+EPS)
            Nq=sq*(Q2-mq)
            mix_ref[j,prow]=(q_ref[j,prow].astype(f32)+Nq*gain_ref[j]+shift_ref[j]).astype(bf16)
            nq_ref[j,prow]=(Q2-mq).astype(bf16)

def fwd_call(q,k,v,e,w1,b1,w2,b2,gain,shift,block=256,unroll=1,**kw):
    slots,length,_=q.shape
    count=block//MINI; nb=length//block; steps=length//MINI
    row=lambda w: pl.BlockSpec((slots,block,w),lambda i:(0,i,0))
    full=lambda s: pl.BlockSpec(s,lambda i:(0,)*len(s),pipeline_mode=pl.Buffered(1))
    r64=full((slots,length,64)); r1=full((slots,length,1))
    st=pl.BlockSpec((slots,count,64,256),lambda i:(0,i,0,0))
    S=jax.ShapeDtypeStruct
    return pl.pallas_call(functools.partial(fwd_kernel,slots,count,unroll),
        grid=(nb,),
        in_specs=[r64]*3+[r1]+[full(a.shape) for a in (w1,b1,w2,b2,gain,shift)],
        out_specs=[r64,st,st,row(256),row(256),row(256),r64,r64,r64],
        out_shape=[S((slots,length,64),bf16),S((slots,steps,64,256),bf16),S((slots,steps,64,256),bf16)]+[S((slots,length,256),bf16)]*3+[S((slots,length,64),bf16)]*3,
        scratch_shapes=[pltpu.VMEM((slots,64,256),f32),pltpu.VMEM((slots,1,256),f32),pltpu.VMEM((slots,64,256),f32),pltpu.VMEM((slots,1,64),f32),pltpu.VMEM((slots,MINI,256),f32),pltpu.VMEM((slots,MINI,256),f32),pltpu.VMEM((slots,MINI,256),bf16),pltpu.VMEM((slots,MINI,64),bf16)],
        compiler_params=pltpu.CompilerParams(dimension_semantics=("arbitrary",),vmem_limit_bytes=VMEM_BYTES),
        name="inner_forward",cost_estimate=pl.CostEstimate(flops=90_000_000_000,bytes_accessed=40_000_000,transcendentals=0),**kw)(q,k,v,e,w1,b1,w2,b2,gain,shift)


def bwd_kernel(slots,count,unroll,q_ref,k_ref,v_ref,e_ref,do_ref,n_ref,g_ref,nq_ref,w1s_ref,w2s_ref,z1_ref,h_ref,q1_ref,gain_ref,shift_ref,
    dq_ref,dk_ref,dv_ref,de_ref,dw1_ref,db1_ref,dw2_ref,db2_ref,dgn_ref,dsh_ref,
    DW1,DB1,G2,DB2,KD,DGN,DSH,DGQ,DSQ,
    sA,sAd,sHA,sGZ,sE1,sE2,sW1,sW2,sR1,sR2,sDA,sQ1,sQ2,sAQ,sb1,sb2):
    lower,_=masks()
    steps=q_ref.shape[1]//MINI
    pid=pl.program_id(0); nb=pl.num_programs(0)
    @pl.when(pid==0)
    def _():
        for r in (DW1,DB1,G2,DB2,KD,DGN,DSH,DGQ,DSQ):
            r[...]=jnp.zeros(r.shape,r.dtype)
        for r in (sA,sAd,sHA,sGZ,sE1,sE2,sW1,sW2,sR1,sR2,sDA,sQ1,sQ2,sAQ,sb1,sb2):
            r[0]=jnp.zeros(r.shape[1:],r.dtype)
    def crit(j,p,t):
        rows=pl.ds(pl.multiple_of(jnp.minimum(t,steps-1)*MINI,MINI),MINI)
        prow=pl.ds(pl.multiple_of(jnp.maximum(t-1,0)*MINI,MINI),MINI)
        gain=gain_ref[j]; shift=shift_ref[j]; g2=gain*gain; mg=rs(g2)
        e=e_ref[j,rows]
        nE1=sR1[p,j]+KD[j]
        dgZ1=(-e)*nE1
        dH=dgZ1*sAd[p,j]
        dHb=dH.astype(bf16)
        w2b=sW2[p,j]
        G2f=G2[j]; G2b=G2f.astype(bf16)
        Ab=sA[p,j]; E2b=sE2[p,j]
        yield
        a1=nt(Ab,G2b)
        yP=nt(dHb,w2b)
        yield
        Zc=n_ref[j,rows].astype(f32); G=g_ref[j,rows].astype(f32)
        s=lax.rsqrt(rs(Zc*Zc)+EPS); N=s*Zc
        K=k_ref[j,rows]; Q=q_ref[j,rows]; Kp=k_ref[j,prow]
        T=shift-v_ref[j,rows].astype(f32)+K.astype(f32)
        U=gain*T
        gN=N*g2
        c1=rs(gN); c2=rs(gN*N); mU=rs(U); UN=rs(U*N)
        a=gN+U; ma=c1+mU; m2=c2+UN
        a2=nn(E2b,G2b)
        E1b=sE1[p,j]; dQ1b=sQ1[p,j]
        DW=DW1[j]; DWb=DW.astype(bf16)
        KDb=nn(Kp,DWb)+DB1[j]
        yield
        a3=nt(E1b,DWb)
        X1=(lower*nt(dQ1b,E1b)).astype(bf16)
        L2=cat((nt(Kp,cat(Q,K))+1.0).astype(bf16),cat(Q,K).T)
        yield
        nE2=sR2[p,j]+a1+DB2[j]
        y=yP-e*nE2
        yg=y*g2; yn=y*N
        ym=rs(y); yN=rs(yn); yG=rs(y*G); ygm=rs(yg); ygN=rs(yg*N)
        mdy=s*ym; mdyN=s*yN
        da=s*y-mdy-N*mdyN
        sN=s*ygN-mdy*c1-mdyN*c2-2.0*m2*mdyN
        mN=s*ygm-mdy*mg-mdyN*c1-ma*mdyN-m2*mdy
        kap=yG+sN
        dN=da*g2-a*mdyN-(s*m2)*y
        dZc=s*(dN-mN-N*kap)
        dZb=dZc.astype(bf16)
        dT=da*gain
        yield
        dA=nn(dZb,w2b)+sDA[p,j]-a2
        yield
        G2[j]=G2f+tn(cat(sQ2[p,j],g_ref[j,rows],dZb),cat(sAQ[p,j],dHb,Ab))
        DB2[j]=DB2[j]+sb2[p,j]+jnp.sum(dZc,0,keepdims=True)
        dQs=nn(X1,K); dKs=tn(X1,Q)
        dv_ref[j,rows]=(-dT).astype(bf16)
        dO=do_ref[j,rows].astype(f32)
        DGN[j]=DGN[j]+da*(2.0*gain*N+T)
        DSH[j]=DSH[j]+dT
        de_ref[j,rows]=-(jnp.sum(nE1*sGZ[p,j],-1,keepdims=True)+jnp.sum(nE2*G,-1,keepdims=True))
        yield
        dZ1=dA*sAd[p,j]+dgZ1*sHA[p,j]
        dZ1b=dZ1.astype(bf16)
        dd=cat(dQ1b,dZ1b)
        X=nn(L2,dd)
        KD[j]=KDb+X[:MINI]
        DW1[j]=DW+X[MINI:]
        DB1[j]=DB1[j]+sb1[p,j]+jnp.sum(dZ1,0,keepdims=True)
        yield
        qk=nt(dd,sW1[p,j])
        dq_ref[j,rows]=(dO+qk[:MINI]-dQs).astype(bf16)
        dk_ref[j,rows]=(qk[MINI:]-dKs-a3+dT).astype(bf16)
    def qside(j,p,t,i):
        rows=pl.ds(pl.multiple_of(t*MINI,MINI),MINI)
        brow=pl.ds(pl.multiple_of(i*MINI,MINI),MINI)
        gain=gain_ref[j]
        dO=do_ref[j,rows].astype(f32); Qc=nq_ref[j,rows].astype(f32)
        sq=lax.rsqrt(rs(Qc*Qc)+EPS); Nq=sq*Qc
        dNq=dO*gain
        dQ2=sq*(dNq-rs(dNq)-Nq*rs(dNq*Nq))
        dQ2b=dQ2.astype(bf16)
        A,Ad,Add=gelu3(z1_ref[j,brow].astype(f32))
        AQ,AQd=gelu2(q1_ref[j,brow].astype(f32))
        H=h_ref[j,brow].astype(f32); e=e_ref[j,rows]
        Ab=A.astype(bf16); AQb=AQ.astype(bf16)
        gZ1=H*Ad
        E1b=(e*gZ1).astype(bf16); E2b=(e*g_ref[j,rows].astype(f32)).astype(bf16)
        w1b=w1s_ref[j,i]; w2b=w2s_ref[j,i]
        yield
        sA[p,j]=Ab; sAd[p,j]=Ad; sHA[p,j]=H*Add; sGZ[p,j]=gZ1; sE1[p,j]=E1b; sE2[p,j]=E2b; sW1[p,j]=w1b; sW2[p,j]=w2b; sAQ[p,j]=AQb
        sQ2[p,j]=dQ2b; sb2[p,j]=jnp.sum(dQ2,0,keepdims=True)
        DGQ[j]=DGQ[j]+dO*Nq; DSQ[j]=DSQ[j]+dO
        Q=q_ref[j,rows]; K=k_ref[j,rows]
        P1=(lower*(nt(Q,K)+1.0)).astype(bf16)
        P2=(lower*(nt(AQb,Ab)+1.0)).astype(bf16)
        yield
        X2=(lower*nt(dQ2b,E2b)).astype(bf16)
        yield
        b1=nn(dQ2b,w2b)
        yield
        sR2[p,j]=tn(P2,dQ2b)
        yield
        dAQ=b1-nn(X2,Ab)
        sDA[p,j]=-tn(X2,AQb)
        yield
        yield
        dQ1=dAQ*AQd
        dQ1b=dQ1.astype(bf16)
        sQ1[p,j]=dQ1b; sb1[p,j]=jnp.sum(dQ1,0,keepdims=True)
        sR1[p,j]=tn(P1,dQ1b)
    @pl.loop(0,count//unroll)
    def _(i):
        for u in range(unroll):
            ii=count-1-(i*unroll+u)
            t=(nb-1-pid)*count+ii
            interleave([crit(j,u%2,t+1) for j in range(slots)]+[qside(j,(u+1)%2,t,ii) for j in range(slots)])
    @pl.when(pid==nb-1)
    def _():
        interleave([crit(j,0,jnp.int32(0)) for j in range(slots)])
        for j in range(slots):
            dw1_ref[j]=DW1[j]; db1_ref[j]=DB1[j]; dw2_ref[j]=G2[j]; db2_ref[j]=DB2[j]
            dgn_ref[j]=jnp.sum(DGN[j]+DGQ[j],0,keepdims=True); dsh_ref[j]=jnp.sum(DSH[j]+DSQ[j],0,keepdims=True)

def bwd_call(q,k,v,e,dO,n,g,nq,w1s,w2s,z1,h,q1,gain,shift,block=256,unroll=2,**kw):
    slots,length,_=q.shape
    count=block//MINI; nb=length//block; steps=length//MINI
    row=lambda w: pl.BlockSpec((slots,block,w),lambda i:(0,nb-1-i,0))
    full=lambda s: pl.BlockSpec(s,lambda i:(0,)*len(s),pipeline_mode=pl.Buffered(1))
    r64=full((slots,length,64)); r1=full((slots,length,1))
    st=pl.BlockSpec((slots,count,64,256),lambda i:(0,nb-1-i,0,0))
    S=jax.ShapeDtypeStruct
    outs=[((slots,64,256),f32),((slots,1,256),f32),((slots,64,256),f32),((slots,1,64),f32),((slots,1,64),f32),((slots,1,64),f32)]
    V=lambda *s,d=f32: pltpu.VMEM(s,d)
    return pl.pallas_call(functools.partial(bwd_kernel,slots,count,unroll),
        grid=(nb,),
        in_specs=[r64]*3+[r1]+[r64]*4+[st,st]+[row(256)]*3+[full(gain.shape)]*2,
        out_specs=[r64]*3+[r1]+[full(o[0]) for o in outs],
        out_shape=[S((slots,length,64),bf16)]*3+[S((slots,length,1),f32)]+[S(*o) for o in outs],
        scratch_shapes=[V(slots,64,256),V(slots,1,256),V(slots,64,256),V(slots,1,64),V(slots,MINI,256),V(slots,MINI,64),V(slots,MINI,64),V(slots,MINI,64),V(slots,MINI,64),
          V(2,slots,MINI,256,d=bf16),V(2,slots,MINI,256),V(2,slots,MINI,256),V(2,slots,MINI,256),V(2,slots,MINI,256,d=bf16),V(2,slots,MINI,64,d=bf16),
          V(2,slots,64,256,d=bf16),V(2,slots,64,256,d=bf16),V(2,slots,MINI,256),V(2,slots,MINI,64),V(2,slots,MINI,256),V(2,slots,MINI,256,d=bf16),V(2,slots,MINI,64,d=bf16),V(2,slots,MINI,256,d=bf16),V(2,slots,1,256),V(2,slots,1,64)],
        compiler_params=pltpu.CompilerParams(dimension_semantics=("arbitrary",),vmem_limit_bytes=VMEM_BYTES),
        name="inner_backward",cost_estimate=pl.CostEstimate(flops=110_000_000_000,bytes_accessed=40_000_000,transcendentals=0),**kw)(q,k,v,e,dO,n,g,nq,w1s,w2s,z1,h,q1,gain,shift)


def rms_back(grad_scaled, inputs, scale):
    return scale * (
        grad_scaled - inputs * scale * scale * jnp.mean(grad_scaled * inputs, -1, keepdims=True)
    )


def gather(block):
    return lax.all_gather(block, "fsdp", axis=0, tiled=True)


def swap(block, axes):
    return lax.all_to_all(block, axes, split_axis=0, concat_axis=0, tiled=True)


def pad_to(array_in, size, dim):
    widths = [(0, 0)] * array_in.ndim
    widths[dim] = (0, size - array_in.shape[dim])
    return jnp.pad(array_in, widths)


def shards(
    tokens,
    lengths,
    cotangent,
    pre_gain,
    query_weight,
    key_weight,
    value_weight,
    gate_weight,
    rate_weight,
    out_weight,
    post_gain,
    ffn_gate,
    ffn_up,
    ffn_down,
    inner_first,
    inner_first_bias,
    inner_second,
    inner_second_bias,
    inner_gain,
    inner_shift,
):
    micro, _, rows, width = tokens.shape
    local, head, inner = inner_first.shape
    ff = ffn_gate.shape[1]
    Z = lax.axis_size("sp")
    S = lax.axis_size("fsdp")
    z = lax.axis_index("sp")
    d = lax.axis_index("fsdp")
    groups = S // micro
    slots = -(-local // groups)
    order = [[g for g in range(h, local, groups)] for h in range(groups)]
    flat = [g for part in order for g in part]
    span = 3 * head
    tiles = -(-slots * span // 128)
    piece = Z * rows
    length = S * piece
    total = micro * rows
    own = query_weight.shape[0]
    extra = local * span
    packed_width = -(-(extra + local + 2) // 128) * 128

    def columns(weight, count):
        return lax.dynamic_slice_in_dim(weight, z * count, count, 1)

    q_w, k_w, v_w = (
        columns(w, local * head).reshape(own, local, head)
        for w in (query_weight, key_weight, value_weight)
    )
    r_w = columns(rate_weight, local)
    parts = []
    for g in flat:
        parts += [q_w[:, g], k_w[:, g], v_w[:, g]]
    parts += [r_w, pre_gain[:, None], post_gain[:, None]]
    packed = pad_to(jnp.concatenate(parts, 1), packed_width, 1)
    front = gather(packed)
    all_tokens = lax.all_gather(tokens[:, 0], "sp", axis=0)
    rear_in = (out_weight, gate_weight, ffn_gate, ffn_up, ffn_down)
    rear_in, front, all_tokens = lax.optimization_barrier((rear_in, front, all_tokens))
    pre_full = front[:, extra + local].astype(f32)[None]
    post_full = front[:, extra + local + 1].astype(f32)[None]
    token_rows = all_tokens.reshape(Z * total, width).astype(f32)
    scale_one = lax.rsqrt(jnp.mean(token_rows * token_rows, -1, keepdims=True) + EPS)
    normed = (token_rows * scale_one * pre_full).astype(bf16)
    projected = nn(normed, front)
    rate_sig = jax.nn.sigmoid(projected[:, extra : extra + local])
    rate_rows = (RATE * rate_sig).astype(bf16).reshape(Z, micro, rows, local)
    low = projected.astype(bf16).reshape(Z, micro, rows, packed_width)
    rate_tiles = slots * piece // 128

    def pack_tiles(pieces, rates):
        body = pieces.reshape(S, piece, tiles, 128).transpose(0, 2, 1, 3)
        tail = pad_to(rates.reshape(S, rate_tiles, 128), 16 * (-(-rate_tiles // 16)), 1)
        return jnp.concatenate([body.reshape(S, tiles * piece, 128), tail], 1)

    low_parts = []
    rate_parts = []
    start = 0
    for part in order:
        stop = min(start + tiles * 128, packed_width)
        low_parts.append(pad_to(low[..., start:stop], tiles * 128, 3))
        start += len(part) * span
        here = [rate_rows[..., g : g + 1] for g in part] + [jnp.zeros_like(rate_rows[..., :1])] * (slots - len(part))
        rate_parts.append(jnp.concatenate(here, 3))
    send_low = jnp.stack(low_parts).transpose(0, 2, 1, 3, 4).reshape(S, piece, tiles * 128)
    send_rate = jnp.stack(rate_parts).transpose(0, 2, 4, 1, 3).reshape(S, slots, piece)
    arrived = swap(pack_tiles(send_low, send_rate), "fsdp")
    body = arrived[:, : tiles * piece].reshape(S, tiles, piece, 128)

    def chain_rows(index):
        out = []
        for j in range(slots):
            lane = j * span + index * head
            out.append(body[:, lane // 128, :, lane % 128 : lane % 128 + head].reshape(length, head))
        return jnp.stack(out)

    q, k, v = chain_rows(0), chain_rows(1), chain_rows(2)
    e = arrived[:, tiles * piece : tiles * piece + rate_tiles].reshape(S, slots, piece)
    e = e.transpose(1, 0, 2).reshape(slots, length, 1).astype(f32)

    half = d // micro
    heads_here = [jnp.minimum(half + j * groups, local - 1) for j in range(slots)]

    def of_slots(array_in):
        return jnp.stack([lax.dynamic_index_in_dim(array_in, g, 0, keepdims=False) for g in heads_here])

    w1 = of_slots(inner_first)
    b1 = of_slots(inner_first_bias)[:, None]
    w2 = of_slots(inner_second)
    w2 = (w2 - jnp.mean(w2, -1, keepdims=True)).transpose(0, 2, 1)
    b2 = of_slots(inner_second_bias)[:, None]
    b2 = b2 - jnp.mean(b2, -1, keepdims=True)
    gain = of_slots(inner_gain)[:, None]
    shift = of_slots(inner_shift)[:, None]
    mix, w1s, w2s, z1, h, q1, n, g_, nq = fwd_call(q, k, v, e, w1, b1, w2, b2, gain, shift, unroll=2)

    out_in, gate_in, fgate_in, fup_in, down_in = rear_in
    rear = gather(jnp.concatenate([out_in, gate_in, fgate_in, fup_in], 1))
    out_full = rear[:, :width]
    gate_full = rear[:, width : 2 * width]
    fgate_full = rear[:, 2 * width : 2 * width + ff]
    fup_full = rear[:, 2 * width + ff :]
    down_full = gather(down_in)

    def to_tokens(chains):
        send = chains.reshape(slots, S, Z, rows, head).transpose(1, 2, 3, 0, 4)
        got = swap(send.reshape(S * Z, rows, slots * head), ("fsdp", "sp"))
        got = got.reshape(groups, micro, Z, rows, slots, head).transpose(1, 3, 2, 4, 0, 5)
        return got.reshape(total, Z, slots * groups, head)[:, :, :local].reshape(total, width)

    def to_chains(block):
        send = pad_to(block.reshape(micro, rows, Z, local, head), slots * groups, 3)
        send = send.reshape(micro, rows, Z, slots, groups, head).transpose(4, 0, 2, 1, 3, 5)
        got = swap(send.reshape(S * Z, rows, slots * head), ("fsdp", "sp"))
        return got.reshape(length, slots, head).transpose(1, 0, 2)

    mixed_rows = to_tokens(mix).astype(f32)
    own_tokens = tokens.reshape(total, width).astype(f32)
    own_normed = lax.dynamic_slice_in_dim(normed, z * total, total, 0)
    gate_logit = nn(own_normed, gate_full)
    gate_act, gate_slope = gelu2(gate_logit)
    gated = (gate_act * mixed_rows).astype(bf16)
    middle = own_tokens + nn(gated, out_full)
    scale_two = lax.rsqrt(jnp.mean(middle * middle, -1, keepdims=True) + EPS)
    normed_two = (middle * scale_two * post_full).astype(bf16)
    gate_pre = nn(normed_two, fgate_full)
    up_pre = nn(normed_two, fup_full)
    gate_sig = jax.nn.sigmoid(gate_pre)
    silu_act = gate_pre * gate_sig
    hidden = (silu_act * up_pre).astype(bf16)
    output = (middle + nn(hidden, down_full)).astype(bf16)

    position = d * piece + z * rows + lax.broadcasted_iota(jnp.int32, (micro, rows), 1)
    live = (position < lengths[:, None]).astype(f32).reshape(total, 1)
    grad_out = cotangent.reshape(total, width).astype(f32) * live
    grad_low = grad_out.astype(bf16)
    grad_hidden = nt(grad_low, down_full)
    grad_gate_pre = (grad_hidden * up_pre * gate_sig * (1.0 + gate_pre * (1.0 - gate_sig))).astype(bf16)
    grad_up_pre = (grad_hidden * silu_act).astype(bf16)
    grad_normed_two = nt(grad_gate_pre, fgate_full) + nt(grad_up_pre, fup_full)
    grad_middle = grad_out + rms_back(grad_normed_two * post_full, middle, scale_two)
    grad_branch = grad_middle.astype(bf16)
    grad_gated = nt(grad_branch, out_full)
    grad_mixed = (grad_gated * gate_act).astype(bf16)
    grad_gate_logit = (grad_gated * mixed_rows * gate_slope).astype(bf16)
    d_mix = to_chains(grad_mixed)
    rear_grad = jnp.concatenate(
        [
            tn(gated, grad_branch).astype(bf16),
            tn(own_normed, grad_gate_logit).astype(bf16),
            tn(normed_two, grad_gate_pre).astype(bf16),
            tn(normed_two, grad_up_pre).astype(bf16),
            tn(hidden, grad_low).astype(bf16).reshape(width, ff),
        ],
        1,
    )
    d_mix, rear_grad = lax.optimization_barrier((d_mix, rear_grad))
    rear_part = lax.psum_scatter(rear_grad, "fsdp", scatter_dimension=0, tiled=True)
    grad_normed_gate = nt(grad_gate_logit, gate_full)

    dq, dk, dv, de, dw1, db1, dw2, db2, dgn, dsh = bwd_call(
        q, k, v, e, d_mix, n, g_, nq, w1s, w2s, z1, h, q1, gain, shift
    )
    (dq, dk, dv, de, dw1, db1, dw2, db2), rear_part = lax.optimization_barrier(
        ((dq, dk, dv, de, dw1, db1, dw2, db2), rear_part)
    )
    rear_sum = lax.psum(rear_part, "sp")
    dw2 = dw2 - jnp.mean(dw2, 1, keepdims=True)
    db2 = db2 - jnp.mean(db2, -1, keepdims=True)
    small = jnp.concatenate([db1[:, 0], db2[:, 0], dgn[:, 0], dsh[:, 0], jnp.zeros((slots, head), f32)], 1)
    inner_rows = jnp.concatenate([dw1, dw2, pad_to(small.reshape(slots, 2, inner), -(-(2 * head + 2) // S) * S - 2 * head, 1)], 1)
    share = inner_rows.shape[1] // S
    inner_send = inner_rows.astype(bf16).reshape(slots, S, share, 2, 128).transpose(1, 0, 3, 2, 4)
    inner_send = inner_send.reshape(S, slots * 2 * share, 128)

    grads = jnp.stack([dq, dk, dv], 2).transpose(1, 0, 2, 3).reshape(S, piece, slots * span)
    rates_back = de[..., 0].astype(bf16).reshape(slots, S, piece).transpose(1, 0, 2)
    packed_back = pack_tiles(pad_to(grads, tiles * 128, 2), rates_back)
    used = packed_back.shape[1]
    extent = -(-inner_send.shape[1] // 16) * 16
    arrived = swap(jnp.concatenate([packed_back, pad_to(inner_send, extent, 1)], 1), "fsdp")
    inner_part = arrived[:, used : used + inner_send.shape[1]].astype(f32)
    inner_part = jnp.sum(inner_part.reshape(groups, micro, slots, 2, share, 128), 1)
    inner_part = inner_part.transpose(1, 0, 3, 2, 4).reshape(slots * groups, share, 2 * 128)[:local]
    inner_sum = lax.all_gather(inner_part.astype(bf16), "fsdp", axis=1, tiled=True).astype(f32)
    body = arrived[:, : tiles * piece].reshape(groups, micro, tiles, Z, rows, 128)
    body = body.transpose(3, 1, 4, 0, 2, 5).reshape(Z * total, groups, tiles * 128)
    back = arrived[:, tiles * piece : tiles * piece + rate_tiles].reshape(groups, micro, slots, Z, rows)
    back = back.transpose(3, 1, 4, 2, 0).reshape(Z * total, slots * groups)[:, :local].astype(f32)
    grad_rate_logit = (back * RATE * rate_sig * (1.0 - rate_sig)).astype(bf16)
    grad_packed = pad_to(
        jnp.concatenate(
            [body[:, i, : len(part) * span] for i, part in enumerate(order) if part] + [grad_rate_logit], 1
        ),
        packed_width,
        1,
    )
    weight_parts = tn(normed, grad_packed).astype(bf16).reshape(S, own, packed_width)
    weight_grad = jnp.sum(swap(weight_parts, "fsdp").astype(f32), 0)
    rear_sum, weight_grad = lax.optimization_barrier((rear_sum, weight_grad))
    rear_sum = rear_sum.astype(f32)
    weight_all = lax.all_gather(weight_grad.astype(bf16), "sp", axis=1).astype(f32)
    pieces = weight_all[..., :extra].reshape(own, Z, local, 3, head)
    pieces = jnp.stack([pieces[:, :, flat.index(g)] for g in range(local)], 2)
    query_grad, key_grad, value_grad = (pieces[:, :, :, i].reshape(own, width) for i in range(3))
    rate_grad = weight_all[..., extra : extra + local].reshape(own, Z * local)
    normed_parts = nt(grad_packed, front).astype(bf16).reshape(Z, total, width)
    grad_normed = jnp.sum(swap(normed_parts, "sp").astype(f32), 0) + grad_normed_gate
    own_scale = lax.dynamic_slice_in_dim(scale_one, z * total, total, 0)
    tokens_grad = (grad_middle + rms_back(grad_normed * pre_full, own_tokens, own_scale)).astype(bf16)

    out_grad = rear_sum[:, :width]
    gate_grad = rear_sum[:, width : 2 * width]
    fgate_grad = rear_sum[:, 2 * width : 2 * width + ff]
    fup_grad = rear_sum[:, 2 * width + ff : 2 * width + 2 * ff]
    down_grad = rear_sum[:, 2 * width + 2 * ff :].reshape(-1, width)

    def row_dot(grad, weight):
        return jnp.sum(grad * weight.astype(f32), -1)

    pre_grad = (
        row_dot(query_grad, query_weight)
        + row_dot(key_grad, key_weight)
        + row_dot(value_grad, value_weight)
        + row_dot(gate_grad, gate_weight)
        + row_dot(rate_grad, rate_weight)
    ) / pre_gain.astype(f32)
    post_grad = (row_dot(fgate_grad, ffn_gate) + row_dot(fup_grad, ffn_up)) / post_gain.astype(f32)

    tail = inner_sum[:, 2 * head : 2 * head + 2].reshape(local, 2 * inner)
    return (
        output.reshape(tokens.shape),
        tokens_grad.reshape(tokens.shape),
        pre_grad,
        query_grad,
        key_grad,
        value_grad,
        gate_grad,
        rate_grad,
        out_grad,
        post_grad,
        fgate_grad,
        fup_grad,
        down_grad,
        inner_sum[:, :head],
        tail[:, :inner],
        inner_sum[:, head : 2 * head].transpose(0, 2, 1),
        tail[:, inner : inner + head],
        tail[:, inner + head : inner + 2 * head],
        tail[:, inner + 2 * head : inner + 3 * head],
    )


def solution(mesh):
    return jax.shard_map(
        shards,
        mesh=mesh,
        in_specs=(
            P(None, "fsdp", "sp", None),
            P(),
            P(None, "fsdp", "sp", None),
            P("fsdp"),
            P("fsdp", None),
            P("fsdp", None),
            P("fsdp", None),
            P("fsdp", None),
            P("fsdp", None),
            P("fsdp", None),
            P("fsdp"),
            P("fsdp", None),
            P("fsdp", None),
            P("fsdp", None),
            P("sp", None, None),
            P("sp", None),
            P("sp", None, None),
            P("sp", None),
            P("sp", None),
            P("sp", None),
        ),
        out_specs=(
            P(None, "fsdp", "sp", None),
            P(None, "fsdp", "sp", None),
            P("fsdp"),
            P("fsdp", None),
            P("fsdp", None),
            P("fsdp", None),
            P("fsdp", None),
            P("fsdp", None),
            P("fsdp", None),
            P("fsdp"),
            P("fsdp", None),
            P("fsdp", None),
            P("fsdp", None),
            P("sp", None, None),
            P("sp", None),
            P("sp", None, None),
            P("sp", None),
            P("sp", None),
            P("sp", None),
        ),
        check_vma=False,
    )
```

```python
import functools

import jax
import jax.numpy as jnp
from jax import lax
from jax.experimental import pallas as pl
from jax.experimental.pallas import tpu as pltpu
from jax.sharding import PartitionSpec as P

MINI = 16
EPS = 1e-06
RATE = 1.0 / 1024.0
GELU_C = 0.7978845608028654
GELU_K = 0.044715
VMEM_BYTES = 56 * 1024 * 1024
f32 = jnp.float32
bf16 = jnp.bfloat16

def nn(x,y): return lax.dot_general(x.astype(bf16),y.astype(bf16),(((1,),(0,)),((),())),preferred_element_type=f32)
def nt(x,y): return lax.dot_general(x.astype(bf16),y.astype(bf16),(((1,),(1,)),((),())),preferred_element_type=f32)
def tn(x,y): return lax.dot_general(x.astype(bf16),y.astype(bf16),(((0,),(0,)),((),())),preferred_element_type=f32)
def gelu1(z):
    t=jnp.tanh(GELU_C*z*(1.0+GELU_K*(z*z)))
    return 0.5*z*(1.0+t)
def gelu2(z):
    z2=z*z
    t=jnp.tanh(z*(GELU_C+(GELU_C*GELU_K)*z2))
    h=0.5+0.5*t
    return z*h, h+0.5*z*(1.0-t*t)*(GELU_C+(3.0*GELU_C*GELU_K)*z2)
def gelu3(z):
    z2=z*z
    t=jnp.tanh(z*(GELU_C+(GELU_C*GELU_K)*z2))
    h=0.5+0.5*t
    u=GELU_C+(3.0*GELU_C*GELU_K)*z2
    c=1.0-t*t
    return z*h, h+0.5*z*c*u, c*(u+z*((3.0*GELU_C*GELU_K)*z-t*u*u))

def cat(*xs): return jnp.concatenate(xs,0)
def rs(x): return jnp.sum(x,-1,keepdims=True)*(1.0/64)

def interleave(gens):
    gens=list(gens)
    while gens:
        alive=[]
        for g in gens:
            try:
                next(g); alive.append(g)
            except StopIteration: pass
        gens=alive

def masks():
    lower=lax.broadcasted_iota(jnp.int32,(MINI,MINI),0)>=lax.broadcasted_iota(jnp.int32,(MINI,MINI),1)
    return lower.astype(f32), jnp.where(lower,0.0,1.0)

def fwd_kernel(slots,count,unroll,piece,tiles,x_ref,w1_ref,b1_ref,w2_ref,b2_ref,gain_ref,shift_ref,
    mix_ref,q_ref,k_ref,v_ref,e_ref,w1s_ref,w2s_ref,z1_ref,h_ref,q1_ref,n_ref,g_ref,nq_ref,
    W1,B1,W2,B2,Z,ZQ,AP,EP):
    lower,upper=masks()
    steps=q_ref.shape[1]//MINI
    pid=pl.program_id(0)
    @pl.when(pid==0)
    def _():
        eye=lax.broadcasted_iota(jnp.int32,(128,128),0)==lax.broadcasted_iota(jnp.int32,(128,128),1)
        @pl.loop(0,x_ref.shape[0])
        def _(src):
            base=pl.multiple_of(src*piece,piece)
            for j in range(slots):
                for index,ref in enumerate((q_ref,k_ref,v_ref)):
                    lane=(3*j+index)*64
                    top=lane//128*piece
                    ref[j,pl.ds(base,piece)]=x_ref[src,top:top+piece,lane%128:lane%128+64]
            rates=x_ref[src,tiles*piece:tiles*piece+16].astype(f32)
            for j in range(slots):
                for i in range(piece//128):
                    n=j*(piece//128)+i
                    column=jnp.sum(jnp.where(eye,rates[n:n+1],0.0),1,keepdims=True)
                    e_ref[j,pl.ds(base+i*128,128)]=column
        for j in range(slots):
            W1[j]=w1_ref[j]; B1[j]=b1_ref[j]; W2[j]=w2_ref[j]; B2[j]=b2_ref[j]
            Z[j]=nn(k_ref[j,:MINI],w1_ref[j])+b1_ref[j]
            ZQ[j]=jnp.zeros((MINI,256),f32); AP[j]=jnp.zeros((MINI,256),bf16); EP[j]=jnp.zeros((MINI,64),bf16)
    def chain(j,i):
        t=pid*count+i
        rows=pl.ds(pl.multiple_of(t*MINI,MINI),MINI)
        prow=pl.ds(pl.multiple_of(jnp.maximum(t-1,0)*MINI,MINI),MINI)
        nrow=pl.ds(pl.multiple_of(jnp.minimum(t+1,steps-1)*MINI,MINI),MINI)
        brow=pl.ds(pl.multiple_of(i*MINI,MINI),MINI)
        gain=gain_ref[j]; shift=shift_ref[j]; g2=gain*gain; mg=rs(g2)
        z1=Z[j]; q1=ZQ[j]; w2=W2[j]; b2=B2[j]
        w2b=w2.astype(bf16)
        Ap=AP[j]; Ep=EP[j]
        A,Ad=gelu2(z1); AQ=gelu1(q1)
        Ab=A.astype(bf16); AQb=AQ.astype(bf16)
        z1_ref[j,brow]=z1.astype(bf16)
        yield
        zz=nt(cat(Ab,AQb),w2b)
        z=zz[:MINI]+b2; qb=zz[MINI:]+b2
        yield
        P2=upper*(nt(AQb,Ap)+1.0)
        K=k_ref[j,rows]; Q=q_ref[j,rows]; Kn=k_ref[j,nrow]
        w1=W1[j]; w1b=w1.astype(bf16); b1=B1[j]
        w1s_ref[j,i]=w1b; w2s_ref[j,i]=w2b
        KQ=cat(Kn,Q)
        KK=nt(KQ,K)+1.0
        L=cat(KK[:MINI].astype(bf16),(lower*KK[MINI:]).astype(bf16),K.T)
        base=nn(KQ,w1b)+b1
        U=gain*(shift-v_ref[j,rows].astype(f32)+K.astype(f32)); mU=rs(U)
        e=e_ref[j,rows]
        yield
        Q2=qb+nn(P2,Ep)
        yield
        zg=z*g2
        mz=rs(z); p0=rs(z*z); p1=rs(zg); p2=rs(z*zg); p3=rs(z*U)
        s=lax.rsqrt(p0-mz*mz+EPS)
        m1=s*(p1-mz*mg)+mU
        m2=s*(s*(p2-2.0*mz*p1+mz*mz*mg)+(p3-mz*mU))
        N=s*(z-mz)
        G=s*(N*(g2-m2)+(U-m1))
        Gb=G.astype(bf16)
        yield
        H=nn(Gb,w2b)
        E2=e*G; E2b=E2.astype(bf16)
        n_ref[j,rows]=(z-mz).astype(bf16); g_ref[j,rows]=Gb
        EP[j]=E2b; AP[j]=Ab
        yield
        W2[j]=w2-tn(E2b,Ab)
        B2[j]=b2-jnp.sum(E2,0,keepdims=True)
        yield
        E1=(e*Ad)*H; E1b=E1.astype(bf16)
        X=nn(L,E1b)
        Z[j]=base[:MINI]-X[:MINI]
        Q1=base[MINI:]-X[MINI:2*MINI]
        ZQ[j]=Q1
        W1[j]=w1-X[2*MINI:]
        B1[j]=b1-jnp.sum(E1,0,keepdims=True)
        h_ref[j,brow]=H.astype(bf16); q1_ref[j,brow]=Q1.astype(bf16)
        yield
        mq=rs(Q2); vq=rs(Q2*Q2)
        sq=lax.rsqrt(vq-mq*mq+EPS)
        Nq=sq*(Q2-mq)
        Qp=q_ref[j,prow].astype(f32)
        mix_ref[prow,64*j:64*j+64]=(Qp+Nq*gain+shift).astype(bf16)
        nq_ref[j,prow]=(Q2-mq).astype(bf16)
    @pl.loop(0,count//unroll)
    def _(i):
        for u in range(unroll):
            interleave(chain(j,i*unroll+u) for j in range(slots))
    @pl.when(pid==pl.num_programs(0)-1)
    def _():
        for j in range(slots):
            prow=pl.ds((steps-1)*MINI,MINI)
            AQb=gelu1(ZQ[j]).astype(bf16)
            Q2=nt(AQb,W2[j])+B2[j]+nn(upper*(nt(AQb,AP[j])+1.0),EP[j])
            mq=rs(Q2); vq=rs(Q2*Q2)
            sq=lax.rsqrt(vq-mq*mq+EPS)
            Nq=sq*(Q2-mq)
            mix_ref[prow,64*j:64*j+64]=(q_ref[j,prow].astype(f32)+Nq*gain_ref[j]+shift_ref[j]).astype(bf16)
            nq_ref[j,prow]=(Q2-mq).astype(bf16)

def fwd_call(x,w1,b1,w2,b2,gain,shift,piece,tiles,block=256,unroll=2,**kw):
    slots=w1.shape[0]; length=x.shape[0]*piece
    count=block//MINI; nb=length//block; steps=length//MINI
    row=lambda w: pl.BlockSpec((slots,block,w),lambda i:(0,i,0))
    full=lambda s: pl.BlockSpec(s,lambda i:(0,)*len(s),pipeline_mode=pl.Buffered(1))
    r64=full((slots,length,64)); r1=full((slots,length,1)); rm_=full((length,64*slots))
    st=pl.BlockSpec((slots,count,64,256),lambda i:(0,i,0,0))
    S=jax.ShapeDtypeStruct
    return pl.pallas_call(functools.partial(fwd_kernel,slots,count,unroll,piece,tiles),
        grid=(nb,),
        in_specs=[full(a.shape) for a in (x,w1,b1,w2,b2,gain,shift)],
        out_specs=[rm_,r64,r64,r64,r1,st,st,row(256),row(256),row(256),r64,r64,r64],
        out_shape=[S((length,64*slots),bf16)]+[S((slots,length,64),bf16)]*3+[S((slots,length,1),f32)]+[S((slots,steps,64,256),bf16)]*2+[S((slots,length,256),bf16)]*3+[S((slots,length,64),bf16)]*3,
        scratch_shapes=[pltpu.VMEM((slots,64,256),f32),pltpu.VMEM((slots,1,256),f32),pltpu.VMEM((slots,64,256),f32),pltpu.VMEM((slots,1,64),f32),pltpu.VMEM((slots,MINI,256),f32),pltpu.VMEM((slots,MINI,256),f32),pltpu.VMEM((slots,MINI,256),bf16),pltpu.VMEM((slots,MINI,64),bf16)],
        compiler_params=pltpu.CompilerParams(dimension_semantics=("arbitrary",),vmem_limit_bytes=VMEM_BYTES),
        name="inner_forward",cost_estimate=pl.CostEstimate(flops=90_000_000_000,bytes_accessed=40_000_000,transcendentals=0),**kw)(x,w1,b1,w2,b2,gain,shift)


def bwd_kernel(slots,count,unroll,piece,tiles,q_ref,k_ref,v_ref,e_ref,dx_ref,n_ref,g_ref,nq_ref,w1s_ref,w2s_ref,z1_ref,h_ref,q1_ref,gain_ref,shift_ref,
    out_ref,dw1_ref,db1_ref,dw2_ref,db2_ref,dgn_ref,dsh_ref,
    do_ref,de_ref,    DW1,DB1,G2,DB2,KD,DGN,DSH,DGQ,DSQ,
    sA,sAd,sHA,sGZ,sE1,sE2,sW1,sW2,sR1,sR2,sDA,sQ1,sQ2,sAQ,sb1,sb2):
    lower,_=masks()
    steps=q_ref.shape[1]//MINI
    pid=pl.program_id(0); nb=pl.num_programs(0)
    @pl.when(pid==0)
    def _():
        @pl.loop(0,out_ref.shape[0])
        def _(src):
            rows=pl.ds(pl.multiple_of(src*piece,piece),piece)
            for j in range(slots):
                do_ref[j,rows]=dx_ref[rows,64*j:64*j+64]
        for r in (DW1,DB1,G2,DB2,KD,DGN,DSH,DGQ,DSQ):
            r[...]=jnp.zeros(r.shape,r.dtype)
        for r in (sA,sAd,sHA,sGZ,sE1,sE2,sW1,sW2,sR1,sR2,sDA,sQ1,sQ2,sAQ,sb1,sb2):
            r[0]=jnp.zeros(r.shape[1:],r.dtype)
    def put(j,index,t,value):
        t=jnp.minimum(t,steps-1)
        lane=(3*j+index)*64
        top=lane//128*piece
        part=piece//MINI
        rows=pl.ds(pl.multiple_of(top+lax.rem(t,part)*MINI,MINI),MINI)
        out_ref[lax.div(t,part),rows,lane%128:lane%128+64]=value.astype(bf16)
    def crit(j,p,t):
        rows=pl.ds(pl.multiple_of(jnp.minimum(t,steps-1)*MINI,MINI),MINI)
        prow=pl.ds(pl.multiple_of(jnp.maximum(t-1,0)*MINI,MINI),MINI)
        gain=gain_ref[j]; shift=shift_ref[j]; g2=gain*gain; mg=rs(g2)
        e=e_ref[j,rows]
        nE1=sR1[p,j]+KD[j]
        dgZ1=(-e)*nE1
        dH=dgZ1*sAd[p,j]
        dHb=dH.astype(bf16)
        w2b=sW2[p,j]
        G2f=G2[j]; G2b=G2f.astype(bf16)
        Ab=sA[p,j]; E2b=sE2[p,j]
        yield
        a1=nt(Ab,G2b)
        yP=nt(dHb,w2b)
        yield
        Zc=n_ref[j,rows].astype(f32); G=g_ref[j,rows].astype(f32)
        s=lax.rsqrt(rs(Zc*Zc)+EPS); N=s*Zc
        K=k_ref[j,rows]; Q=q_ref[j,rows]; Kp=k_ref[j,prow]
        T=shift-v_ref[j,rows].astype(f32)+K.astype(f32)
        U=gain*T
        gN=N*g2
        c1=rs(gN); c2=rs(gN*N); mU=rs(U); UN=rs(U*N)
        a=gN+U; ma=c1+mU; m2=c2+UN
        a2=nn(E2b,G2b)
        E1b=sE1[p,j]; dQ1b=sQ1[p,j]
        DW=DW1[j]; DWb=DW.astype(bf16)
        KDb=nn(Kp,DWb)+DB1[j]
        yield
        a3=nt(E1b,DWb)
        X1=(lower*nt(dQ1b,E1b)).astype(bf16)
        L2=cat((nt(Kp,cat(Q,K))+1.0).astype(bf16),cat(Q,K).T)
        yield
        nE2=sR2[p,j]+a1+DB2[j]
        y=yP-e*nE2
        yg=y*g2; yn=y*N
        ym=rs(y); yN=rs(yn); yG=rs(y*G); ygm=rs(yg); ygN=rs(yg*N)
        mdy=s*ym; mdyN=s*yN
        da=s*y-mdy-N*mdyN
        sN=s*ygN-mdy*c1-mdyN*c2-2.0*m2*mdyN
        mN=s*ygm-mdy*mg-mdyN*c1-ma*mdyN-m2*mdy
        kap=yG+sN
        dN=da*g2-a*mdyN-(s*m2)*y
        dZc=s*(dN-mN-N*kap)
        dZb=dZc.astype(bf16)
        dT=da*gain
        yield
        dA=nn(dZb,w2b)+sDA[p,j]-a2
        yield
        G2[j]=G2f+tn(cat(sQ2[p,j],g_ref[j,rows],dZb),cat(sAQ[p,j],dHb,Ab))
        DB2[j]=DB2[j]+sb2[p,j]+jnp.sum(dZc,0,keepdims=True)
        dQs=nn(X1,K); dKs=tn(X1,Q)
        put(j,2,t,-dT)
        dO=do_ref[j,rows].astype(f32)
        DGN[j]=DGN[j]+da*(2.0*gain*N+T)
        DSH[j]=DSH[j]+dT
        de_ref[j,rows]=-(jnp.sum(nE1*sGZ[p,j],-1,keepdims=True)+jnp.sum(nE2*G,-1,keepdims=True))
        yield
        dZ1=dA*sAd[p,j]+dgZ1*sHA[p,j]
        dZ1b=dZ1.astype(bf16)
        dd=cat(dQ1b,dZ1b)
        X=nn(L2,dd)
        KD[j]=KDb+X[:MINI]
        DW1[j]=DW+X[MINI:]
        DB1[j]=DB1[j]+sb1[p,j]+jnp.sum(dZ1,0,keepdims=True)
        yield
        qk=nt(dd,sW1[p,j])
        put(j,0,t,dO+qk[:MINI]-dQs)
        put(j,1,t,qk[MINI:]-dKs-a3+dT)
    def qside(j,p,t,i):
        rows=pl.ds(pl.multiple_of(t*MINI,MINI),MINI)
        brow=pl.ds(pl.multiple_of(i*MINI,MINI),MINI)
        gain=gain_ref[j]
        dO=do_ref[j,rows].astype(f32); Qc=nq_ref[j,rows].astype(f32)
        sq=lax.rsqrt(rs(Qc*Qc)+EPS); Nq=sq*Qc
        dNq=dO*gain
        dQ2=sq*(dNq-rs(dNq)-Nq*rs(dNq*Nq))
        dQ2b=dQ2.astype(bf16)
        A,Ad,Add=gelu3(z1_ref[j,brow].astype(f32))
        AQ,AQd=gelu2(q1_ref[j,brow].astype(f32))
        H=h_ref[j,brow].astype(f32); e=e_ref[j,rows]
        Ab=A.astype(bf16); AQb=AQ.astype(bf16)
        gZ1=H*Ad
        E1b=(e*gZ1).astype(bf16); E2b=(e*g_ref[j,rows].astype(f32)).astype(bf16)
        w1b=w1s_ref[j,i]; w2b=w2s_ref[j,i]
        yield
        sA[p,j]=Ab; sAd[p,j]=Ad; sHA[p,j]=H*Add; sGZ[p,j]=gZ1; sE1[p,j]=E1b; sE2[p,j]=E2b; sW1[p,j]=w1b; sW2[p,j]=w2b; sAQ[p,j]=AQb
        sQ2[p,j]=dQ2b; sb2[p,j]=jnp.sum(dQ2,0,keepdims=True)
        DGQ[j]=DGQ[j]+dO*Nq; DSQ[j]=DSQ[j]+dO
        Q=q_ref[j,rows]; K=k_ref[j,rows]
        P1=(lower*(nt(Q,K)+1.0)).astype(bf16)
        P2=(lower*(nt(AQb,Ab)+1.0)).astype(bf16)
        yield
        X2=(lower*nt(dQ2b,E2b)).astype(bf16)
        yield
        b1=nn(dQ2b,w2b)
        yield
        sR2[p,j]=tn(P2,dQ2b)
        yield
        dAQ=b1-nn(X2,Ab)
        sDA[p,j]=-tn(X2,AQb)
        yield
        yield
        dQ1=dAQ*AQd
        dQ1b=dQ1.astype(bf16)
        sQ1[p,j]=dQ1b; sb1[p,j]=jnp.sum(dQ1,0,keepdims=True)
        sR1[p,j]=tn(P1,dQ1b)
    @pl.loop(0,count//unroll)
    def _(i):
        for u in range(unroll):
            ii=count-1-(i*unroll+u)
            t=(nb-1-pid)*count+ii
            interleave([crit(j,u%2,t+1) for j in range(slots)]+[qside(j,(u+1)%2,t,ii) for j in range(slots)])
    @pl.when(pid==nb-1)
    def _():
        interleave([crit(j,0,jnp.int32(0)) for j in range(slots)])
        eye=lax.broadcasted_iota(jnp.int32,(128,128),0)==lax.broadcasted_iota(jnp.int32,(128,128),1)
        @pl.loop(0,out_ref.shape[0])
        def _(dst):
            base=pl.multiple_of(dst*piece,piece)
            rows=[jnp.sum(jnp.where(eye,de_ref[j,pl.ds(base+i*128,128)],0.0),0,keepdims=True) for j in range(slots) for i in range(piece//128)]
            rows.append(jnp.zeros((16-len(rows),128),f32))
            out_ref[dst,tiles*piece:tiles*piece+16]=cat(*rows).astype(bf16)
            if tiles*128>slots*192:
                out_ref[dst,(tiles-1)*piece:tiles*piece,(slots*192)%128:]=jnp.zeros((piece,128-(slots*192)%128),bf16)
        for j in range(slots):
            dw1_ref[j]=DW1[j]; db1_ref[j]=DB1[j]; dw2_ref[j]=G2[j]; db2_ref[j]=DB2[j]
            dgn_ref[j]=jnp.sum(DGN[j]+DGQ[j],0,keepdims=True); dsh_ref[j]=jnp.sum(DSH[j]+DSQ[j],0,keepdims=True)

def bwd_call(q,k,v,e,dO,n,g,nq,w1s,w2s,z1,h,q1,gain,shift,piece,tiles,block=256,unroll=2,**kw):
    slots,length,_=q.shape
    count=block//MINI; nb=length//block; steps=length//MINI
    row=lambda w: pl.BlockSpec((slots,block,w),lambda i:(0,nb-1-i,0))
    full=lambda s: pl.BlockSpec(s,lambda i:(0,)*len(s),pipeline_mode=pl.Buffered(1))
    r64=full((slots,length,64)); r1=full((slots,length,1))
    st=pl.BlockSpec((slots,count,64,256),lambda i:(0,nb-1-i,0,0))
    S=jax.ShapeDtypeStruct
    outs=[((length//piece,tiles*piece+16,128),bf16),((slots,64,256),f32),((slots,1,256),f32),((slots,64,256),f32),((slots,1,64),f32),((slots,1,64),f32),((slots,1,64),f32)]
    V=lambda *s,d=f32: pltpu.VMEM(s,d)
    return pl.pallas_call(functools.partial(bwd_kernel,slots,count,unroll,piece,tiles),
        grid=(nb,),
        in_specs=[r64]*3+[r1,full(dO.shape)]+[r64]*3+[st,st]+[row(256)]*3+[full(gain.shape)]*2,
        out_specs=[full(o[0]) for o in outs],
        out_shape=[S(*o) for o in outs],
        scratch_shapes=[V(slots,length,64,d=bf16),V(slots,length,1),V(slots,64,256),V(slots,1,256),V(slots,64,256),V(slots,1,64),V(slots,MINI,256),V(slots,MINI,64),V(slots,MINI,64),V(slots,MINI,64),V(slots,MINI,64),
          V(2,slots,MINI,256,d=bf16),V(2,slots,MINI,256),V(2,slots,MINI,256),V(2,slots,MINI,256),V(2,slots,MINI,256,d=bf16),V(2,slots,MINI,64,d=bf16),
          V(2,slots,64,256,d=bf16),V(2,slots,64,256,d=bf16),V(2,slots,MINI,256),V(2,slots,MINI,64),V(2,slots,MINI,256),V(2,slots,MINI,256,d=bf16),V(2,slots,MINI,64,d=bf16),V(2,slots,MINI,256,d=bf16),V(2,slots,1,256),V(2,slots,1,64)],
        compiler_params=pltpu.CompilerParams(dimension_semantics=("arbitrary",),vmem_limit_bytes=VMEM_BYTES),
        name="inner_backward",cost_estimate=pl.CostEstimate(flops=110_000_000_000,bytes_accessed=40_000_000,transcendentals=0),**kw)(q,k,v,e,dO,n,g,nq,w1s,w2s,z1,h,q1,gain,shift)


def rms_back(grad_scaled, inputs, scale):
    return scale * (
        grad_scaled - inputs * scale * scale * jnp.mean(grad_scaled * inputs, -1, keepdims=True)
    )


def gather(block):
    return lax.all_gather(block, "fsdp", axis=0, tiled=True)


def swap(block, axes):
    return lax.all_to_all(block, axes, split_axis=0, concat_axis=0, tiled=True)


def pad_to(array_in, size, dim):
    widths = [(0, 0)] * array_in.ndim
    widths[dim] = (0, size - array_in.shape[dim])
    return jnp.pad(array_in, widths)


def back_kernel(layout, piece, tiles, a_ref, slope_ref, front_ref, grad_ref, parts_ref):
    micro_step = pl.program_id(0)
    groups, slots, local, micro = layout["groups"], layout["slots"], layout["local"], layout["micro"]
    eye = lax.broadcasted_iota(jnp.int32, (128, 128), 0) == lax.broadcasted_iota(jnp.int32, (128, 128), 1)
    lanes = lax.broadcasted_iota(jnp.int32, (piece, 64), 1)
    rates = jnp.zeros((piece, 64), f32)
    for h, part in enumerate(layout["order"]):
        block = a_ref[h * micro + micro_step, tiles * piece : tiles * piece + 16].astype(f32)
        for j, g in enumerate(part):
            column = []
            for i in range(piece // 128):
                n = j * (piece // 128) + i
                column.append(jnp.sum(jnp.where(eye, block[n : n + 1], 0.0), 1, keepdims=True))
            rates = jnp.where(lanes == g, cat(*column), rates)
    slope = slope_ref[:, 0].reshape(piece, slope_ref.shape[-1])
    rates = rates * slope[:, :64]
    halves = []
    for h, part in enumerate(layout["order"]):
        for lane in range(0, len(part) * 192, 64):
            halves.append((h, lane))
    halves.append(None)
    chunks = []
    for n in range(0, len(halves), 2):
        pair = halves[n : n + 2]
        if pair[0] is not None and len(pair) == 2 and pair[1] is not None:
            (h, lane), (h2, lane2) = pair
            if h == h2 and lane % 128 == 0:
                top = lane // 128 * piece
                chunks.append(a_ref[h * micro + micro_step, top : top + piece])
                continue
        values = []
        for half in pair:
            if half is None:
                values.append(rates.astype(bf16))
            else:
                h, lane = half
                top = lane // 128 * piece
                values.append(a_ref[h * micro + micro_step, top : top + piece, lane % 128 : lane % 128 + 64])
        if len(values) == 1:
            values.append(jnp.zeros((piece, 64), bf16))
        chunks.append(jnp.concatenate(values, 1))
    grad = jnp.concatenate(chunks, 1)
    product = nt(grad, front_ref[...]).astype(bf16)
    rows = piece // grad_ref.shape[0]
    grad_ref[:, 0] = grad.reshape(grad_ref.shape[0], rows, grad.shape[1])
    parts_ref[:, 0] = product.reshape(parts_ref.shape[0], rows, product.shape[1])


def back_call(arrived, slope, front, layout, piece, tiles):
    Z, micro, rows, _ = slope.shape
    width = front.shape[0]
    packed = front.shape[1]
    full = lambda s: pl.BlockSpec(s, lambda i: (0,) * len(s), pipeline_mode=pl.Buffered(1))
    step = lambda w: pl.BlockSpec((Z, 1, rows, w), lambda i: (0, i, 0, 0))
    return pl.pallas_call(
        functools.partial(back_kernel, layout, piece, tiles),
        grid=(micro,),
        in_specs=[full(arrived.shape), step(slope.shape[-1]), full(front.shape)],
        out_specs=[step(packed), step(width)],
        out_shape=[
            jax.ShapeDtypeStruct((Z, micro, rows, packed), bf16),
            jax.ShapeDtypeStruct((Z, micro, rows, width), bf16),
        ],
        compiler_params=pltpu.CompilerParams(dimension_semantics=("arbitrary",), vmem_limit_bytes=VMEM_BYTES),
        name="projection_gradients",
        cost_estimate=pl.CostEstimate(flops=1_000_000_000, bytes_accessed=8_000_000, transcendentals=0),
    )(arrived, slope, front)


def finish_kernel(layout, all_ref, q_ref, k_ref, v_ref, dq_ref, dk_ref, dv_ref, dr_ref, dot_ref):
    local = layout["local"]
    flat = layout["flat"]
    Z = all_ref.shape[0]
    own = dq_ref.shape[0]
    dot = jnp.zeros((own, 1), f32)
    rate = jnp.zeros((own, dr_ref.shape[1]), f32)
    lanes = lax.broadcasted_iota(jnp.int32, rate.shape, 1)
    for index, (weight, out) in enumerate(((q_ref, dq_ref), (k_ref, dk_ref), (v_ref, dv_ref))):
        for z in range(Z):
            for g in range(local):
                start = (flat.index(g) * 3 + index) * 64
                value = all_ref[z, :, start : start + 64].astype(f32)
                place = (z * local + g) * 64
                out[:, place : place + 64] = value
        dot = dot + jnp.sum(out[...] * weight[...].astype(f32), 1, keepdims=True)
    for z in range(Z):
        for g in range(local):
            n = local * 192 + g
            rate = jnp.where(lanes == z * local + g, all_ref[z, :, n : n + 1].astype(f32), rate)
    dr_ref[...] = rate
    dot_ref[...] = dot


def finish_call(gathered, q_w, k_w, v_w, layout):
    own, width = q_w.shape
    Z = gathered.shape[0]
    shapes = [(own, width)] * 3 + [(own, Z * layout["local"]), (own, 1)]
    return pl.pallas_call(
        functools.partial(finish_kernel, layout),
        out_shape=[jax.ShapeDtypeStruct(s, f32) for s in shapes],
        compiler_params=pltpu.CompilerParams(vmem_limit_bytes=VMEM_BYTES),
        name="weight_gradients",
        cost_estimate=pl.CostEstimate(flops=10_000_000, bytes_accessed=2_000_000, transcendentals=0),
    )(gathered, q_w, k_w, v_w)


def shards(
    tokens,
    lengths,
    cotangent,
    pre_gain,
    query_weight,
    key_weight,
    value_weight,
    gate_weight,
    rate_weight,
    out_weight,
    post_gain,
    ffn_gate,
    ffn_up,
    ffn_down,
    inner_first,
    inner_first_bias,
    inner_second,
    inner_second_bias,
    inner_gain,
    inner_shift,
):
    micro, _, rows, width = tokens.shape
    local, head, inner = inner_first.shape
    ff = ffn_gate.shape[1]
    Z = lax.axis_size("sp")
    S = lax.axis_size("fsdp")
    z = lax.axis_index("sp")
    d = lax.axis_index("fsdp")
    groups = S // micro
    slots = -(-local // groups)
    order = [[g for g in range(h, local, groups)] for h in range(groups)]
    flat = [g for part in order for g in part]
    span = 3 * head
    tiles = -(-slots * span // 128)
    piece = Z * rows
    length = S * piece
    total = micro * rows
    own = query_weight.shape[0]
    extra = local * span
    packed_width = -(-(extra + local + 2) // 128) * 128

    def columns(weight, count):
        return lax.dynamic_slice_in_dim(weight, z * count, count, 1)

    q_w, k_w, v_w = (
        columns(w, local * head).reshape(own, local, head)
        for w in (query_weight, key_weight, value_weight)
    )
    r_w = columns(rate_weight, local)
    parts = []
    for g in flat:
        parts += [q_w[:, g], k_w[:, g], v_w[:, g]]
    parts += [r_w, pre_gain[:, None], post_gain[:, None]]
    packed = pad_to(jnp.concatenate(parts, 1), packed_width, 1)
    front = gather(packed)
    all_tokens = lax.all_gather(tokens[:, 0], "sp", axis=0)
    rear_in = (out_weight, gate_weight, ffn_gate, ffn_up, ffn_down)
    rear_in, front, all_tokens = lax.optimization_barrier((rear_in, front, all_tokens))
    pre_full = front[:, extra + local].astype(f32)[None]
    post_full = front[:, extra + local + 1].astype(f32)[None]
    token_rows = all_tokens.reshape(Z * total, width).astype(f32)
    scale_one = lax.rsqrt(jnp.mean(token_rows * token_rows, -1, keepdims=True) + EPS)
    normed = (token_rows * scale_one * pre_full).astype(bf16)
    projected = nn(normed, front)
    rate_sig = jax.nn.sigmoid(projected[:, extra : extra + local])
    rate_rows = (RATE * rate_sig).astype(bf16).reshape(Z, micro, rows, local)
    rate_slope = pad_to(RATE * rate_sig * (1.0 - rate_sig), 128, 1).reshape(Z, micro, rows, 128)
    layout = dict(groups=groups, slots=slots, local=local, micro=micro, order=order, flat=flat)
    low = projected.astype(bf16).reshape(Z, micro, rows, packed_width)
    rate_tiles = slots * piece // 128

    def pack_tiles(pieces, rates):
        body = pieces.reshape(S, piece, tiles, 128).transpose(0, 2, 1, 3)
        tail = pad_to(rates.reshape(S, rate_tiles, 128), 16 * (-(-rate_tiles // 16)), 1)
        return jnp.concatenate([body.reshape(S, tiles * piece, 128), tail], 1)

    low_parts = []
    rate_parts = []
    start = 0
    for part in order:
        stop = min(start + tiles * 128, packed_width)
        low_parts.append(pad_to(low[..., start:stop], tiles * 128, 3))
        start += len(part) * span
        here = [rate_rows[..., g : g + 1] for g in part] + [jnp.zeros_like(rate_rows[..., :1])] * (slots - len(part))
        rate_parts.append(jnp.concatenate(here, 3))
    send_low = jnp.stack(low_parts).transpose(0, 2, 1, 3, 4).reshape(S, piece, tiles * 128)
    send_rate = jnp.stack(rate_parts).transpose(0, 2, 4, 1, 3).reshape(S, slots, piece)
    arrived = swap(pack_tiles(send_low, send_rate), "fsdp")

    half = d // micro
    heads_here = [jnp.minimum(half + j * groups, local - 1) for j in range(slots)]

    def of_slots(array_in):
        return jnp.stack([lax.dynamic_index_in_dim(array_in, g, 0, keepdims=False) for g in heads_here])

    w1 = of_slots(inner_first)
    b1 = of_slots(inner_first_bias)[:, None]
    w2 = of_slots(inner_second)
    w2 = (w2 - jnp.mean(w2, -1, keepdims=True)).transpose(0, 2, 1)
    b2 = of_slots(inner_second_bias)[:, None]
    b2 = b2 - jnp.mean(b2, -1, keepdims=True)
    gain = of_slots(inner_gain)[:, None]
    shift = of_slots(inner_shift)[:, None]
    mix, q, k, v, e, *saved = fwd_call(arrived, w1, b1, w2, b2, gain, shift, piece, tiles)
    w1s, w2s, z1, h, q1, n, g_, nq = saved

    out_in, gate_in, fgate_in, fup_in, down_in = rear_in
    rear = gather(jnp.concatenate([out_in, gate_in, fgate_in, fup_in], 1))
    out_full = rear[:, :width]
    gate_full = rear[:, width : 2 * width]
    fgate_full = rear[:, 2 * width : 2 * width + ff]
    fup_full = rear[:, 2 * width + ff :]
    down_full = gather(down_in)

    def to_tokens(chains):
        got = swap(chains.reshape(S * Z, rows, slots * head), ("fsdp", "sp"))
        got = got.reshape(groups, micro, Z, rows, slots, head).transpose(1, 3, 2, 4, 0, 5)
        return got.reshape(total, Z, slots * groups, head)[:, :, :local].reshape(total, width)

    def to_chains(block):
        send = pad_to(block.reshape(micro, rows, Z, local, head), slots * groups, 3)
        send = send.reshape(micro, rows, Z, slots, groups, head).transpose(4, 0, 2, 1, 3, 5)
        got = swap(send.reshape(S * Z, rows, slots * head), ("fsdp", "sp"))
        return got.reshape(length, slots * head)

    mixed_rows = to_tokens(mix).astype(f32)
    own_tokens = tokens.reshape(total, width).astype(f32)
    own_normed = lax.dynamic_slice_in_dim(normed, z * total, total, 0)
    gate_logit = nn(own_normed, gate_full)
    gate_act, gate_slope = gelu2(gate_logit)
    gated = (gate_act * mixed_rows).astype(bf16)
    middle = own_tokens + nn(gated, out_full)
    scale_two = lax.rsqrt(jnp.mean(middle * middle, -1, keepdims=True) + EPS)
    normed_two = (middle * scale_two * post_full).astype(bf16)
    gate_pre = nn(normed_two, fgate_full)
    up_pre = nn(normed_two, fup_full)
    gate_sig = jax.nn.sigmoid(gate_pre)
    silu_act = gate_pre * gate_sig
    hidden = (silu_act * up_pre).astype(bf16)
    output = (middle + nn(hidden, down_full)).astype(bf16)

    position = d * piece + z * rows + lax.broadcasted_iota(jnp.int32, (micro, rows), 1)
    live = (position < lengths[:, None]).astype(f32).reshape(total, 1)
    grad_out = cotangent.reshape(total, width).astype(f32) * live
    grad_low = grad_out.astype(bf16)
    grad_hidden = nt(grad_low, down_full)
    grad_gate_pre = (grad_hidden * up_pre * gate_sig * (1.0 + gate_pre * (1.0 - gate_sig))).astype(bf16)
    grad_up_pre = (grad_hidden * silu_act).astype(bf16)
    grad_normed_two = nt(grad_gate_pre, fgate_full) + nt(grad_up_pre, fup_full)
    grad_middle = grad_out + rms_back(grad_normed_two * post_full, middle, scale_two)
    grad_branch = grad_middle.astype(bf16)
    grad_gated = nt(grad_branch, out_full)
    grad_mixed = (grad_gated * gate_act).astype(bf16)
    grad_gate_logit = (grad_gated * mixed_rows * gate_slope).astype(bf16)
    d_mix = to_chains(grad_mixed)
    rear_grad = jnp.concatenate(
        [
            tn(gated, grad_branch).astype(bf16),
            tn(own_normed, grad_gate_logit).astype(bf16),
            tn(normed_two, grad_gate_pre).astype(bf16),
            tn(normed_two, grad_up_pre).astype(bf16),
            tn(hidden, grad_low).astype(bf16).reshape(width, ff),
        ],
        1,
    )
    d_mix, rear_grad = lax.optimization_barrier((d_mix, rear_grad))
    rear_part = lax.psum_scatter(rear_grad, "fsdp", scatter_dimension=0, tiled=True)
    grad_normed_gate = nt(grad_gate_logit, gate_full)

    packed_back, dw1, db1, dw2, db2, dgn, dsh = bwd_call(
        q, k, v, e, d_mix, n, g_, nq, w1s, w2s, z1, h, q1, gain, shift, piece, tiles
    )
    packed_back, rear_part = lax.optimization_barrier((packed_back, rear_part))
    rear_sum = lax.psum(rear_part, "sp")
    dw2 = dw2 - jnp.mean(dw2, 1, keepdims=True)
    db2 = db2 - jnp.mean(db2, -1, keepdims=True)
    small = jnp.concatenate([db1[:, 0], db2[:, 0], dgn[:, 0], dsh[:, 0], jnp.zeros((slots, head), f32)], 1)
    inner_rows = jnp.concatenate([dw1, dw2, pad_to(small.reshape(slots, 2, inner), -(-(2 * head + 2) // S) * S - 2 * head, 1)], 1)
    share = inner_rows.shape[1] // S
    inner_send = inner_rows.astype(bf16).reshape(slots, S, share, 2, 128).transpose(1, 0, 3, 2, 4)
    inner_send = inner_send.reshape(S, slots * 2 * share, 128)

    arrived = swap(packed_back, "fsdp")
    grad_packed, normed_parts = back_call(arrived, rate_slope, front, layout, piece, tiles)
    weight_parts = tn(normed, grad_packed.reshape(Z * total, packed_width)).astype(bf16)
    weight_parts = weight_parts.reshape(S, own, packed_width)
    extent = -(-inner_send.shape[1] * 128 // packed_width)
    inner_send = pad_to(inner_send.reshape(S, -1), extent * packed_width, 1).reshape(S, extent, packed_width)
    got = swap(jnp.concatenate([weight_parts, inner_send], 1), "fsdp")
    got, normed_parts, rear_sum = lax.optimization_barrier((got, normed_parts, rear_sum))
    normed_parts = swap(normed_parts.reshape(Z, total, width), "sp")
    got_sum = jnp.sum(got[:, :own].astype(f32), 0).astype(bf16)
    rear_sum = rear_sum.astype(f32)
    out_grad = rear_sum[:, :width]
    gate_grad = rear_sum[:, width : 2 * width]
    fgate_grad = rear_sum[:, 2 * width : 2 * width + ff]
    fup_grad = rear_sum[:, 2 * width + ff : 2 * width + 2 * ff]
    down_grad = rear_sum[:, 2 * width + 2 * ff :].reshape(-1, width)

    def row_dot(grad, weight):
        return jnp.sum(grad * weight.astype(f32), -1)

    post_grad = (row_dot(fgate_grad, ffn_gate) + row_dot(fup_grad, ffn_up)) / post_gain.astype(f32)
    gate_dot = row_dot(gate_grad, gate_weight)
    inner_part = got[:, own:].reshape(S, -1)[:, : slots * 2 * share * 128].astype(f32)
    inner_part = jnp.sum(inner_part.reshape(groups, micro, slots, 2, share, 128), 1)
    inner_part = inner_part.transpose(1, 0, 3, 2, 4).reshape(slots * groups, share, 2 * 128)[:local]
    rear_done = (out_grad, gate_grad, fgate_grad, fup_grad, down_grad, post_grad, gate_dot)
    rear_done, got_sum, inner_part = lax.optimization_barrier((rear_done, got_sum, inner_part.astype(bf16)))
    out_grad, gate_grad, fgate_grad, fup_grad, down_grad, post_grad, gate_dot = rear_done
    inner_sum = lax.all_gather(inner_part, "fsdp", axis=1, tiled=True)
    weight_all = lax.all_gather(got_sum, "sp", axis=0)
    inner_sum = inner_sum.astype(f32)
    query_grad, key_grad, value_grad, rate_grad, front_dot = finish_call(
        weight_all, query_weight, key_weight, value_weight, layout
    )
    grad_normed = jnp.sum(normed_parts.astype(f32), 0) + grad_normed_gate
    own_scale = lax.dynamic_slice_in_dim(scale_one, z * total, total, 0)
    tokens_grad = (grad_middle + rms_back(grad_normed * pre_full, own_tokens, own_scale)).astype(bf16)

    pre_grad = (
        front_dot[:, 0]
        + gate_dot
        + row_dot(rate_grad, rate_weight)
    ) / pre_gain.astype(f32)

    tail = inner_sum[:, 2 * head : 2 * head + 2].reshape(local, 2 * inner)
    return (
        output.reshape(tokens.shape),
        tokens_grad.reshape(tokens.shape),
        pre_grad,
        query_grad,
        key_grad,
        value_grad,
        gate_grad,
        rate_grad,
        out_grad,
        post_grad,
        fgate_grad,
        fup_grad,
        down_grad,
        inner_sum[:, :head],
        tail[:, :inner],
        inner_sum[:, head : 2 * head].transpose(0, 2, 1),
        tail[:, inner : inner + head],
        tail[:, inner + head : inner + 2 * head],
        tail[:, inner + 2 * head : inner + 3 * head],
    )


def solution(mesh):
    return jax.shard_map(
        shards,
        mesh=mesh,
        in_specs=(
            P(None, "fsdp", "sp", None),
            P(),
            P(None, "fsdp", "sp", None),
            P("fsdp"),
            P("fsdp", None),
            P("fsdp", None),
            P("fsdp", None),
            P("fsdp", None),
            P("fsdp", None),
            P("fsdp", None),
            P("fsdp"),
            P("fsdp", None),
            P("fsdp", None),
            P("fsdp", None),
            P("sp", None, None),
            P("sp", None),
            P("sp", None, None),
            P("sp", None),
            P("sp", None),
            P("sp", None),
        ),
        out_specs=(
            P(None, "fsdp", "sp", None),
            P(None, "fsdp", "sp", None),
            P("fsdp"),
            P("fsdp", None),
            P("fsdp", None),
            P("fsdp", None),
            P("fsdp", None),
            P("fsdp", None),
            P("fsdp", None),
            P("fsdp"),
            P("fsdp", None),
            P("fsdp", None),
            P("fsdp", None),
            P("sp", None, None),
            P("sp", None),
            P("sp", None, None),
            P("sp", None),
            P("sp", None),
            P("sp", None),
        ),
        check_vma=False,
    )
```

```python
import functools

import jax
import jax.numpy as jnp
from jax import lax
from jax.experimental import pallas as pl
from jax.experimental.pallas import tpu as pltpu
from jax.sharding import PartitionSpec as P

MINI = 16
EPS = 1e-06
RATE = 1.0 / 1024.0
GELU_C = 0.7978845608028654
GELU_K = 0.044715
VMEM_BYTES = 58 * 1024 * 1024
f32 = jnp.float32
bf16 = jnp.bfloat16

def nn(x,y): return lax.dot_general(x.astype(bf16),y.astype(bf16),(((1,),(0,)),((),())),preferred_element_type=f32)
def nt(x,y): return lax.dot_general(x.astype(bf16),y.astype(bf16),(((1,),(1,)),((),())),preferred_element_type=f32)
def tn(x,y): return lax.dot_general(x.astype(bf16),y.astype(bf16),(((0,),(0,)),((),())),preferred_element_type=f32)
def gelu1(z):
    t=jnp.tanh(GELU_C*z*(1.0+GELU_K*(z*z)))
    return 0.5*z*(1.0+t)
def gelu2(z):
    z2=z*z
    t=jnp.tanh(z*(GELU_C+(GELU_C*GELU_K)*z2))
    h=0.5+0.5*t
    return z*h, h+0.5*z*(1.0-t*t)*(GELU_C+(3.0*GELU_C*GELU_K)*z2)
def gelu3(z):
    z2=z*z
    t=jnp.tanh(z*(GELU_C+(GELU_C*GELU_K)*z2))
    h=0.5+0.5*t
    u=GELU_C+(3.0*GELU_C*GELU_K)*z2
    c=1.0-t*t
    return z*h, h+0.5*z*c*u, c*(u+z*((3.0*GELU_C*GELU_K)*z-t*u*u))

def cat(*xs): return jnp.concatenate(xs,0)
def rs(x): return jnp.sum(x,-1,keepdims=True)*(1.0/64)

def interleave(gens):
    gens=list(gens)
    while gens:
        alive=[]
        for g in gens:
            try:
                next(g); alive.append(g)
            except StopIteration: pass
        gens=alive

def masks():
    lower=lax.broadcasted_iota(jnp.int32,(MINI,MINI),0)>=lax.broadcasted_iota(jnp.int32,(MINI,MINI),1)
    return lower.astype(f32), jnp.where(lower,0.0,1.0)

def fwd_kernel(slots,count,unroll,piece,tiles,x_ref,w1_ref,b1_ref,w2_ref,b2_ref,gain_ref,shift_ref,
    mix_ref,q_ref,k_ref,v_ref,e_ref,w1s_ref,w2s_ref,z1_ref,h_ref,q1_ref,n_ref,g_ref,nq_ref,
    W1,B1,W2,B2,Z,ZQ,AP,EP):
    lower,upper=masks()
    steps=q_ref.shape[1]//MINI
    pid=pl.program_id(0)
    @pl.when(pid==0)
    def _():
        eye=lax.broadcasted_iota(jnp.int32,(128,128),0)==lax.broadcasted_iota(jnp.int32,(128,128),1)
        @pl.loop(0,x_ref.shape[0])
        def _(src):
            base=pl.multiple_of(src*piece,piece)
            for j in range(slots):
                for index,ref in enumerate((q_ref,k_ref,v_ref)):
                    lane=(3*j+index)*64
                    top=lane//128*piece
                    ref[j,pl.ds(base,piece)]=x_ref[src,top:top+piece,lane%128:lane%128+64]
            rates=x_ref[src,tiles*piece:tiles*piece+16].astype(f32)
            for j in range(slots):
                for i in range(piece//128):
                    n=j*(piece//128)+i
                    column=jnp.sum(jnp.where(eye,rates[n:n+1],0.0),1,keepdims=True)
                    e_ref[j,pl.ds(base+i*128,128)]=column
        for j in range(slots):
            W1[j]=w1_ref[j]; B1[j]=b1_ref[j]; W2[j]=w2_ref[j]; B2[j]=b2_ref[j]
            Z[j]=nn(k_ref[j,:MINI],w1_ref[j])+b1_ref[j]
            ZQ[j]=jnp.zeros((MINI,256),f32); AP[j]=jnp.zeros((MINI,256),bf16); EP[j]=jnp.zeros((MINI,64),bf16)
    def chain(j,i):
        t=pid*count+i
        rows=pl.ds(pl.multiple_of(t*MINI,MINI),MINI)
        prow=pl.ds(pl.multiple_of(jnp.maximum(t-1,0)*MINI,MINI),MINI)
        nrow=pl.ds(pl.multiple_of(jnp.minimum(t+1,steps-1)*MINI,MINI),MINI)
        brow=pl.ds(pl.multiple_of(i*MINI,MINI),MINI)
        gain=gain_ref[j]; shift=shift_ref[j]; g2=gain*gain; mg=rs(g2)
        z1=Z[j]; q1=ZQ[j]; w2=W2[j]; b2=B2[j]
        w2b=w2.astype(bf16)
        Ap=AP[j]; Ep=EP[j]
        A,Ad=gelu2(z1); AQ=gelu1(q1)
        Ab=A.astype(bf16); AQb=AQ.astype(bf16)
        z1_ref[j,brow]=z1.astype(bf16)
        yield
        zz=nt(cat(Ab,AQb),w2b)
        z=zz[:MINI]+b2; qb=zz[MINI:]+b2
        yield
        P2=upper*(nt(AQb,Ap)+1.0)
        K=k_ref[j,rows]; Q=q_ref[j,rows]; Kn=k_ref[j,nrow]
        w1=W1[j]; w1b=w1.astype(bf16); b1=B1[j]
        w1s_ref[j,i]=w1b; w2s_ref[j,i]=w2b
        KQ=cat(Kn,Q)
        KK=nt(KQ,K)+1.0
        L=cat(KK[:MINI].astype(bf16),(lower*KK[MINI:]).astype(bf16),K.T)
        base=nn(KQ,w1b)+b1
        U=gain*(shift-v_ref[j,rows].astype(f32)+K.astype(f32)); mU=rs(U)
        e=e_ref[j,rows]
        yield
        Q2=qb+nn(P2,Ep)
        yield
        zg=z*g2
        mz=rs(z); p0=rs(z*z); p1=rs(zg); p2=rs(z*zg); p3=rs(z*U)
        s=lax.rsqrt(p0-mz*mz+EPS)
        m1=s*(p1-mz*mg)+mU
        m2=s*(s*(p2-2.0*mz*p1+mz*mz*mg)+(p3-mz*mU))
        N=s*(z-mz)
        G=s*(N*(g2-m2)+(U-m1))
        Gb=G.astype(bf16)
        yield
        H=nn(Gb,w2b)
        E2=e*G; E2b=E2.astype(bf16)
        n_ref[j,rows]=(z-mz).astype(bf16); g_ref[j,rows]=Gb
        EP[j]=E2b; AP[j]=Ab
        yield
        W2[j]=w2-tn(E2b,Ab)
        B2[j]=b2-jnp.sum(E2,0,keepdims=True)
        yield
        E1=(e*Ad)*H; E1b=E1.astype(bf16)
        X=nn(L,E1b)
        Z[j]=base[:MINI]-X[:MINI]
        Q1=base[MINI:]-X[MINI:2*MINI]
        ZQ[j]=Q1
        W1[j]=w1-X[2*MINI:]
        B1[j]=b1-jnp.sum(E1,0,keepdims=True)
        h_ref[j,brow]=H.astype(bf16); q1_ref[j,brow]=Q1.astype(bf16)
        yield
        mq=rs(Q2); vq=rs(Q2*Q2)
        sq=lax.rsqrt(vq-mq*mq+EPS)
        Nq=sq*(Q2-mq)
        Qp=q_ref[j,prow].astype(f32)
        mix_ref[prow,64*j:64*j+64]=(Qp+Nq*gain+shift).astype(bf16)
        nq_ref[j,prow]=(Q2-mq).astype(bf16)
    @pl.loop(0,count//unroll)
    def _(i):
        for u in range(unroll):
            interleave(chain(j,i*unroll+u) for j in range(slots))
    @pl.when(pid==pl.num_programs(0)-1)
    def _():
        for j in range(slots):
            prow=pl.ds((steps-1)*MINI,MINI)
            AQb=gelu1(ZQ[j]).astype(bf16)
            Q2=nt(AQb,W2[j])+B2[j]+nn(upper*(nt(AQb,AP[j])+1.0),EP[j])
            mq=rs(Q2); vq=rs(Q2*Q2)
            sq=lax.rsqrt(vq-mq*mq+EPS)
            Nq=sq*(Q2-mq)
            mix_ref[prow,64*j:64*j+64]=(q_ref[j,prow].astype(f32)+Nq*gain_ref[j]+shift_ref[j]).astype(bf16)
            nq_ref[j,prow]=(Q2-mq).astype(bf16)

def fwd_call(x,w1,b1,w2,b2,gain,shift,piece,tiles,block=256,unroll=2,**kw):
    slots=w1.shape[0]; length=x.shape[0]*piece
    count=block//MINI; nb=length//block; steps=length//MINI
    row=lambda w: pl.BlockSpec((slots,block,w),lambda i:(0,i,0))
    full=lambda s: pl.BlockSpec(s,lambda i:(0,)*len(s),pipeline_mode=pl.Buffered(1))
    r64=full((slots,length,64)); r1=full((slots,length,1)); rm_=full((length,64*slots))
    st=pl.BlockSpec((slots,count,64,256),lambda i:(0,i,0,0))
    S=jax.ShapeDtypeStruct
    return pl.pallas_call(functools.partial(fwd_kernel,slots,count,unroll,piece,tiles),
        grid=(nb,),
        in_specs=[full(a.shape) for a in (x,w1,b1,w2,b2,gain,shift)],
        out_specs=[rm_,r64,r64,r64,r1,st,st,row(256),row(256),row(256),r64,r64,r64],
        out_shape=[S((length,64*slots),bf16)]+[S((slots,length,64),bf16)]*3+[S((slots,length,1),f32)]+[S((slots,steps,64,256),bf16)]*2+[S((slots,length,256),bf16)]*3+[S((slots,length,64),bf16)]*3,
        scratch_shapes=[pltpu.VMEM((slots,64,256),f32),pltpu.VMEM((slots,1,256),f32),pltpu.VMEM((slots,64,256),f32),pltpu.VMEM((slots,1,64),f32),pltpu.VMEM((slots,MINI,256),f32),pltpu.VMEM((slots,MINI,256),f32),pltpu.VMEM((slots,MINI,256),bf16),pltpu.VMEM((slots,MINI,64),bf16)],
        compiler_params=pltpu.CompilerParams(dimension_semantics=("arbitrary",),vmem_limit_bytes=VMEM_BYTES),
        name="inner_forward",cost_estimate=pl.CostEstimate(flops=90_000_000_000,bytes_accessed=40_000_000,transcendentals=0),**kw)(x,w1,b1,w2,b2,gain,shift)


def bwd_kernel(slots,count,unroll,piece,tiles,q_ref,k_ref,v_ref,e_ref,dx_ref,n_ref,g_ref,nq_ref,w1s_ref,w2s_ref,z1_ref,h_ref,q1_ref,gain_ref,shift_ref,
    out_ref,dw1_ref,db1_ref,dw2_ref,db2_ref,dgn_ref,dsh_ref,
    do_ref,de_ref,    DW1,DB1,G2,DB2,KD,DGN,DSH,DGQ,DSQ,
    sA,sAd,sHA,sGZ,sE1,sE2,sW1,sW2,sR1,sR2,sDA,sQ1,sQ2,sAQ,sb1,sb2):
    lower,_=masks()
    steps=q_ref.shape[1]//MINI
    pid=pl.program_id(0); nb=pl.num_programs(0)
    @pl.when(pid==0)
    def _():
        @pl.loop(0,out_ref.shape[0])
        def _(src):
            rows=pl.ds(pl.multiple_of(src*piece,piece),piece)
            for j in range(slots):
                do_ref[j,rows]=dx_ref[rows,64*j:64*j+64]
        for r in (DW1,DB1,G2,DB2,KD,DGN,DSH,DGQ,DSQ):
            r[...]=jnp.zeros(r.shape,r.dtype)
        for r in (sA,sAd,sHA,sGZ,sE1,sE2,sW1,sW2,sR1,sR2,sDA,sQ1,sQ2,sAQ,sb1,sb2):
            r[0]=jnp.zeros(r.shape[1:],r.dtype)
    def put(j,index,t,value):
        t=jnp.minimum(t,steps-1)
        lane=(3*j+index)*64
        top=lane//128*piece
        part=piece//MINI
        rows=pl.ds(pl.multiple_of(top+lax.rem(t,part)*MINI,MINI),MINI)
        out_ref[lax.div(t,part),rows,lane%128:lane%128+64]=value.astype(bf16)
    def crit(j,p,t):
        rows=pl.ds(pl.multiple_of(jnp.minimum(t,steps-1)*MINI,MINI),MINI)
        prow=pl.ds(pl.multiple_of(jnp.maximum(t-1,0)*MINI,MINI),MINI)
        gain=gain_ref[j]; shift=shift_ref[j]; g2=gain*gain; mg=rs(g2)
        e=e_ref[j,rows]
        nE1=sR1[p,j]+KD[j]
        dgZ1=(-e)*nE1
        dH=dgZ1*sAd[p,j]
        dHb=dH.astype(bf16)
        w2b=sW2[p,j]
        G2f=G2[j]; G2b=G2f.astype(bf16)
        Ab=sA[p,j]; E2b=sE2[p,j]
        yield
        a1=nt(Ab,G2b)
        yP=nt(dHb,w2b)
        yield
        Zc=n_ref[j,rows].astype(f32); G=g_ref[j,rows].astype(f32)
        s=lax.rsqrt(rs(Zc*Zc)+EPS); N=s*Zc
        K=k_ref[j,rows]; Q=q_ref[j,rows]; Kp=k_ref[j,prow]
        T=shift-v_ref[j,rows].astype(f32)+K.astype(f32)
        U=gain*T
        gN=N*g2
        c1=rs(gN); c2=rs(gN*N); mU=rs(U); UN=rs(U*N)
        a=gN+U; ma=c1+mU; m2=c2+UN
        a2=nn(E2b,G2b)
        E1b=sE1[p,j]; dQ1b=sQ1[p,j]
        DW=DW1[j]; DWb=DW.astype(bf16)
        KDb=nn(Kp,DWb)+DB1[j]
        yield
        a3=nt(E1b,DWb)
        X1=(lower*nt(dQ1b,E1b)).astype(bf16)
        L2=cat((nt(Kp,cat(Q,K))+1.0).astype(bf16),cat(Q,K).T)
        yield
        nE2=sR2[p,j]+a1+DB2[j]
        y=yP-e*nE2
        yg=y*g2; yn=y*N
        ym=rs(y); yN=rs(yn); yG=rs(y*G); ygm=rs(yg); ygN=rs(yg*N)
        mdy=s*ym; mdyN=s*yN
        da=s*y-mdy-N*mdyN
        sN=s*ygN-mdy*c1-mdyN*c2-2.0*m2*mdyN
        mN=s*ygm-mdy*mg-mdyN*c1-ma*mdyN-m2*mdy
        kap=yG+sN
        dN=da*g2-a*mdyN-(s*m2)*y
        dZc=s*(dN-mN-N*kap)
        dZb=dZc.astype(bf16)
        dT=da*gain
        yield
        dA=nn(dZb,w2b)+sDA[p,j]-a2
        yield
        G2[j]=G2f+tn(cat(sQ2[p,j],g_ref[j,rows],dZb),cat(sAQ[p,j],dHb,Ab))
        DB2[j]=DB2[j]+sb2[p,j]+jnp.sum(dZc,0,keepdims=True)
        dQs=nn(X1,K); dKs=tn(X1,Q)
        put(j,2,t,-dT)
        dO=do_ref[j,rows].astype(f32)
        DGN[j]=DGN[j]+da*(2.0*gain*N+T)
        DSH[j]=DSH[j]+dT
        de_ref[j,rows]=-(jnp.sum(nE1*sGZ[p,j],-1,keepdims=True)+jnp.sum(nE2*G,-1,keepdims=True))
        yield
        dZ1=dA*sAd[p,j]+dgZ1*sHA[p,j]
        dZ1b=dZ1.astype(bf16)
        dd=cat(dQ1b,dZ1b)
        X=nn(L2,dd)
        KD[j]=KDb+X[:MINI]
        DW1[j]=DW+X[MINI:]
        DB1[j]=DB1[j]+sb1[p,j]+jnp.sum(dZ1,0,keepdims=True)
        yield
        qk=nt(dd,sW1[p,j])
        put(j,0,t,dO+qk[:MINI]-dQs)
        put(j,1,t,qk[MINI:]-dKs-a3+dT)
    def qside(j,p,t,i):
        rows=pl.ds(pl.multiple_of(t*MINI,MINI),MINI)
        brow=pl.ds(pl.multiple_of(i*MINI,MINI),MINI)
        gain=gain_ref[j]
        dO=do_ref[j,rows].astype(f32); Qc=nq_ref[j,rows].astype(f32)
        sq=lax.rsqrt(rs(Qc*Qc)+EPS); Nq=sq*Qc
        dNq=dO*gain
        dQ2=sq*(dNq-rs(dNq)-Nq*rs(dNq*Nq))
        dQ2b=dQ2.astype(bf16)
        A,Ad,Add=gelu3(z1_ref[j,brow].astype(f32))
        AQ,AQd=gelu2(q1_ref[j,brow].astype(f32))
        H=h_ref[j,brow].astype(f32); e=e_ref[j,rows]
        Ab=A.astype(bf16); AQb=AQ.astype(bf16)
        gZ1=H*Ad
        E1b=(e*gZ1).astype(bf16); E2b=(e*g_ref[j,rows].astype(f32)).astype(bf16)
        w1b=w1s_ref[j,i]; w2b=w2s_ref[j,i]
        yield
        sA[p,j]=Ab; sAd[p,j]=Ad; sHA[p,j]=H*Add; sGZ[p,j]=gZ1; sE1[p,j]=E1b; sE2[p,j]=E2b; sW1[p,j]=w1b; sW2[p,j]=w2b; sAQ[p,j]=AQb
        sQ2[p,j]=dQ2b; sb2[p,j]=jnp.sum(dQ2,0,keepdims=True)
        DGQ[j]=DGQ[j]+dO*Nq; DSQ[j]=DSQ[j]+dO
        Q=q_ref[j,rows]; K=k_ref[j,rows]
        P1=(lower*(nt(Q,K)+1.0)).astype(bf16)
        P2=(lower*(nt(AQb,Ab)+1.0)).astype(bf16)
        yield
        X2=(lower*nt(dQ2b,E2b)).astype(bf16)
        yield
        b1=nn(dQ2b,w2b)
        yield
        sR2[p,j]=tn(P2,dQ2b)
        yield
        dAQ=b1-nn(X2,Ab)
        sDA[p,j]=-tn(X2,AQb)
        yield
        yield
        dQ1=dAQ*AQd
        dQ1b=dQ1.astype(bf16)
        sQ1[p,j]=dQ1b; sb1[p,j]=jnp.sum(dQ1,0,keepdims=True)
        sR1[p,j]=tn(P1,dQ1b)
    @pl.loop(0,count//unroll)
    def _(i):
        for u in range(unroll):
            ii=count-1-(i*unroll+u)
            t=(nb-1-pid)*count+ii
            interleave([crit(j,u%2,t+1) for j in range(slots)]+[qside(j,(u+1)%2,t,ii) for j in range(slots)])
    @pl.when(pid==nb-1)
    def _():
        interleave([crit(j,0,jnp.int32(0)) for j in range(slots)])
        eye=lax.broadcasted_iota(jnp.int32,(128,128),0)==lax.broadcasted_iota(jnp.int32,(128,128),1)
        @pl.loop(0,out_ref.shape[0])
        def _(dst):
            base=pl.multiple_of(dst*piece,piece)
            rows=[jnp.sum(jnp.where(eye,de_ref[j,pl.ds(base+i*128,128)],0.0),0,keepdims=True) for j in range(slots) for i in range(piece//128)]
            rows.append(jnp.zeros((16-len(rows),128),f32))
            out_ref[dst,tiles*piece:tiles*piece+16]=cat(*rows).astype(bf16)
            if tiles*128>slots*192:
                out_ref[dst,(tiles-1)*piece:tiles*piece,(slots*192)%128:]=jnp.zeros((piece,128-(slots*192)%128),bf16)
        for j in range(slots):
            dw1_ref[j]=DW1[j]; db1_ref[j]=DB1[j]; dw2_ref[j]=G2[j]; db2_ref[j]=DB2[j]
            dgn_ref[j]=jnp.sum(DGN[j]+DGQ[j],0,keepdims=True); dsh_ref[j]=jnp.sum(DSH[j]+DSQ[j],0,keepdims=True)

def bwd_call(q,k,v,e,dO,n,g,nq,w1s,w2s,z1,h,q1,gain,shift,piece,tiles,block=256,unroll=2,**kw):
    slots,length,_=q.shape
    count=block//MINI; nb=length//block; steps=length//MINI
    row=lambda w: pl.BlockSpec((slots,block,w),lambda i:(0,nb-1-i,0))
    full=lambda s: pl.BlockSpec(s,lambda i:(0,)*len(s),pipeline_mode=pl.Buffered(1))
    r64=full((slots,length,64)); r1=full((slots,length,1))
    st=pl.BlockSpec((slots,count,64,256),lambda i:(0,nb-1-i,0,0))
    S=jax.ShapeDtypeStruct
    outs=[((length//piece,tiles*piece+16,128),bf16),((slots,64,256),f32),((slots,1,256),f32),((slots,64,256),f32),((slots,1,64),f32),((slots,1,64),f32),((slots,1,64),f32)]
    V=lambda *s,d=f32: pltpu.VMEM(s,d)
    return pl.pallas_call(functools.partial(bwd_kernel,slots,count,unroll,piece,tiles),
        grid=(nb,),
        in_specs=[r64]*3+[r1,full(dO.shape)]+[r64]*3+[st,st]+[row(256)]*3+[full(gain.shape)]*2,
        out_specs=[full(o[0]) for o in outs],
        out_shape=[S(*o) for o in outs],
        scratch_shapes=[V(slots,length,64,d=bf16),V(slots,length,1),V(slots,64,256),V(slots,1,256),V(slots,64,256),V(slots,1,64),V(slots,MINI,256),V(slots,MINI,64),V(slots,MINI,64),V(slots,MINI,64),V(slots,MINI,64),
          V(2,slots,MINI,256,d=bf16),V(2,slots,MINI,256),V(2,slots,MINI,256),V(2,slots,MINI,256),V(2,slots,MINI,256,d=bf16),V(2,slots,MINI,64,d=bf16),
          V(2,slots,64,256,d=bf16),V(2,slots,64,256,d=bf16),V(2,slots,MINI,256),V(2,slots,MINI,64),V(2,slots,MINI,256),V(2,slots,MINI,256,d=bf16),V(2,slots,MINI,64,d=bf16),V(2,slots,MINI,256,d=bf16),V(2,slots,1,256),V(2,slots,1,64)],
        compiler_params=pltpu.CompilerParams(dimension_semantics=("arbitrary",),vmem_limit_bytes=VMEM_BYTES),
        name="inner_backward",cost_estimate=pl.CostEstimate(flops=110_000_000_000,bytes_accessed=40_000_000,transcendentals=0),**kw)(q,k,v,e,dO,n,g,nq,w1s,w2s,z1,h,q1,gain,shift)


def rms_back(grad_scaled, inputs, scale):
    return scale * (
        grad_scaled - inputs * scale * scale * jnp.mean(grad_scaled * inputs, -1, keepdims=True)
    )


def gather(block):
    return lax.all_gather(block, "fsdp", axis=0, tiled=True)


def swap(block, axes):
    return lax.all_to_all(block, axes, split_axis=0, concat_axis=0, tiled=True)


def pad_to(array_in, size, dim):
    widths = [(0, 0)] * array_in.ndim
    widths[dim] = (0, size - array_in.shape[dim])
    return jnp.pad(array_in, widths)


def back_kernel(layout, piece, tiles, a_ref, slope_ref, front_ref, grad_ref, parts_ref):
    micro_step = pl.program_id(0)
    groups, slots, local, micro = layout["groups"], layout["slots"], layout["local"], layout["micro"]
    eye = lax.broadcasted_iota(jnp.int32, (128, 128), 0) == lax.broadcasted_iota(jnp.int32, (128, 128), 1)
    lanes = lax.broadcasted_iota(jnp.int32, (piece, 64), 1)
    rates = jnp.zeros((piece, 64), f32)
    for h, part in enumerate(layout["order"]):
        block = a_ref[h * micro + micro_step, tiles * piece : tiles * piece + 16].astype(f32)
        for j, g in enumerate(part):
            column = []
            for i in range(piece // 128):
                n = j * (piece // 128) + i
                column.append(jnp.sum(jnp.where(eye, block[n : n + 1], 0.0), 1, keepdims=True))
            rates = jnp.where(lanes == g, cat(*column), rates)
    slope = slope_ref[:, 0].reshape(piece, slope_ref.shape[-1])
    rates = rates * slope[:, :64]
    halves = []
    for h, part in enumerate(layout["order"]):
        for lane in range(0, len(part) * 192, 64):
            halves.append((h, lane))
    halves.append(None)
    chunks = []
    for n in range(0, len(halves), 2):
        pair = halves[n : n + 2]
        if pair[0] is not None and len(pair) == 2 and pair[1] is not None:
            (h, lane), (h2, lane2) = pair
            if h == h2 and lane % 128 == 0:
                top = lane // 128 * piece
                chunks.append(a_ref[h * micro + micro_step, top : top + piece])
                continue
        values = []
        for half in pair:
            if half is None:
                values.append(rates.astype(bf16))
            else:
                h, lane = half
                top = lane // 128 * piece
                values.append(a_ref[h * micro + micro_step, top : top + piece, lane % 128 : lane % 128 + 64])
        if len(values) == 1:
            values.append(jnp.zeros((piece, 64), bf16))
        chunks.append(jnp.concatenate(values, 1))
    grad = jnp.concatenate(chunks, 1)
    product = nt(grad, front_ref[...]).astype(bf16)
    rows = piece // grad_ref.shape[0]
    grad_ref[:, 0] = grad.reshape(grad_ref.shape[0], rows, grad.shape[1])
    parts_ref[:, 0] = product.reshape(parts_ref.shape[0], rows, product.shape[1])


def back_call(arrived, slope, front, layout, piece, tiles):
    Z, micro, rows, _ = slope.shape
    width = front.shape[0]
    packed = front.shape[1]
    full = lambda s: pl.BlockSpec(s, lambda i: (0,) * len(s), pipeline_mode=pl.Buffered(1))
    step = lambda w: pl.BlockSpec((Z, 1, rows, w), lambda i: (0, i, 0, 0))
    return pl.pallas_call(
        functools.partial(back_kernel, layout, piece, tiles),
        grid=(micro,),
        in_specs=[full(arrived.shape), step(slope.shape[-1]), full(front.shape)],
        out_specs=[step(packed), step(width)],
        out_shape=[
            jax.ShapeDtypeStruct((Z, micro, rows, packed), bf16),
            jax.ShapeDtypeStruct((Z, micro, rows, width), bf16),
        ],
        compiler_params=pltpu.CompilerParams(dimension_semantics=("arbitrary",), vmem_limit_bytes=VMEM_BYTES),
        name="projection_gradients",
        cost_estimate=pl.CostEstimate(flops=1_000_000_000, bytes_accessed=8_000_000, transcendentals=0),
    )(arrived, slope, front)


def finish_kernel(layout, all_ref, q_ref, k_ref, v_ref, r_ref, gate_ref, pre_ref, dq_ref, dk_ref, dv_ref, dr_ref, dot_ref):
    local = layout["local"]
    flat = layout["flat"]
    Z = all_ref.shape[0]
    own = dq_ref.shape[0]
    dot = jnp.zeros((own, 1), f32)
    rate = jnp.zeros((own, dr_ref.shape[1]), f32)
    lanes = lax.broadcasted_iota(jnp.int32, rate.shape, 1)
    for index, (weight, out) in enumerate(((q_ref, dq_ref), (k_ref, dk_ref), (v_ref, dv_ref))):
        for z in range(Z):
            for g in range(local):
                start = (flat.index(g) * 3 + index) * 64
                value = all_ref[z, :, start : start + 64].astype(f32)
                place = (z * local + g) * 64
                out[:, place : place + 64] = value
        dot = dot + jnp.sum(out[...] * weight[...].astype(f32), 1, keepdims=True)
    for z in range(Z):
        for g in range(local):
            n = local * 192 + g
            rate = jnp.where(lanes == z * local + g, all_ref[z, :, n : n + 1].astype(f32), rate)
    dr_ref[...] = rate
    dot = dot + jnp.sum(rate * r_ref[...].astype(f32), 1, keepdims=True) + gate_ref[...]
    dot_ref[...] = dot / pre_ref[...].astype(f32)


def finish_call(gathered, q_w, k_w, v_w, r_w, gate_dot, pre, layout):
    own, width = q_w.shape
    Z = gathered.shape[0]
    shapes = [(own, width)] * 3 + [(own, Z * layout["local"]), (own, 1)]
    return pl.pallas_call(
        functools.partial(finish_kernel, layout),
        out_shape=[jax.ShapeDtypeStruct(s, f32) for s in shapes],
        compiler_params=pltpu.CompilerParams(vmem_limit_bytes=VMEM_BYTES),
        name="weight_gradients",
        cost_estimate=pl.CostEstimate(flops=10_000_000, bytes_accessed=2_000_000, transcendentals=0),
    )(gathered, q_w, k_w, v_w, r_w, gate_dot, pre)


def rear_kernel(layout, got_ref, act_ref, slope_ref, tok_ref, w_ref, post_ref, gh_ref, go_ref,
                send_ref, lhs_ref, rhs_ref, hid_ref, gm_ref, mid_ref):
    groups, slots, local, micro = layout["groups"], layout["slots"], layout["local"], layout["micro"]
    Z, rows = got_ref.shape[1], got_ref.shape[2]
    total, width = act_ref.shape
    ff = hid_ref.shape[1]
    blocks = []
    for m in range(micro):
        pieces = []
        for z in range(Z):
            for g in range(local):
                h, j = g % groups, g // groups
                pieces.append(got_ref[h * micro + m, z, :, 64 * j : 64 * j + 64])
        blocks.append(jnp.concatenate(pieces, 1))
    mixed = cat(*blocks).astype(f32)
    gated = (act_ref[...] * mixed).astype(bf16)
    lhs_ref[0] = gated.T
    middle = tok_ref[...].astype(f32) + nn(gated, w_ref[:, :width])
    mid_ref[...] = middle
    scale = lax.rsqrt(jnp.mean(middle * middle, -1, keepdims=True) + EPS)
    post = post_ref[...]
    low = (middle * scale * post).astype(bf16)
    lhs_ref[1] = low.T
    gm_ref[...] = jnp.zeros((total, width), f32)
    step = 256

    @pl.loop(0, ff // step)
    def _(c):
        here = pl.ds(pl.multiple_of(c * step, step), step)
        gate_at = pl.ds(pl.multiple_of(2 * width + c * step, step), step)
        up_at = pl.ds(pl.multiple_of(2 * width + ff + c * step, step), step)
        gate_w, up_w = w_ref[:, gate_at], w_ref[:, up_at]
        gate_pre, up_pre = nn(low, gate_w), nn(low, up_w)
        sig = 0.5 + 0.5 * jnp.tanh(0.5 * gate_pre)
        silu = gate_pre * sig
        hid_ref[:, here] = (silu * up_pre).astype(bf16)
        grad = gh_ref[:, here]
        g_gate = (grad * up_pre * sig * (1.0 + gate_pre * (1.0 - sig))).astype(bf16)
        g_up = (grad * silu).astype(bf16)
        rhs_ref[:, gate_at] = g_gate
        rhs_ref[:, up_at] = g_up
        gm_ref[...] += nt(g_gate, gate_w) + nt(g_up, up_w)

    middle = mid_ref[...]
    grad_middle = go_ref[...].astype(f32) + rms_back(gm_ref[...] * post, middle, scale)
    gm_ref[...] = grad_middle
    branch = grad_middle.astype(bf16)
    rhs_ref[:, :width] = branch
    grad_gated = nt(branch, w_ref[:, :width])
    grad_mixed = (grad_gated * act_ref[...]).astype(bf16)
    rhs_ref[:, width : 2 * width] = (grad_gated * mixed * slope_ref[...]).astype(bf16)
    for m in range(micro):
        for z in range(Z):
            for h in range(groups):
                for j in range(slots):
                    g = h + j * groups
                    if g < local:
                        lane = (z * local + g) * 64
                        value = grad_mixed[m * rows : m * rows + rows, lane : lane + 64]
                    else:
                        value = jnp.zeros((rows, 64), bf16)
                    send_ref[h * micro + m, z, :, 64 * j : 64 * j + 64] = value


def rear_call(layout, got, act, slope, tok, weights, post, grad_hidden, grad_low):
    total, width = act.shape
    ff = grad_hidden.shape[1]
    S_ = jax.ShapeDtypeStruct
    return pl.pallas_call(
        functools.partial(rear_kernel, layout),
        out_shape=[
            S_(got.shape, bf16), S_((2, width, total), bf16), S_((total, weights.shape[1]), bf16),
            S_((total, ff), bf16), S_((total, width), f32), S_((total, width), f32),
        ],
        compiler_params=pltpu.CompilerParams(vmem_limit_bytes=VMEM_BYTES),
        name="rear",
        cost_estimate=pl.CostEstimate(flops=5_000_000_000, bytes_accessed=16_000_000, transcendentals=0),
    )(got, act, slope, tok, weights, post, grad_hidden, grad_low)


def rear_grad_kernel(starts, per_step, lhs_ref, normed_ref, low_ref, rhs_ref, hid_ref, out_ref):
    S = out_ref.shape[0]
    own = out_ref.shape[1] // per_step
    gate_at, ffn_at, down_at = starts

    def block(n, top):
        here = pl.ds(top * own, own)

        def write(left):
            right = rhs_ref[:, pl.ds(pl.multiple_of(n * 256, 256), 256)]
            out_ref[:, here] = nn(left, right).astype(bf16).reshape(S, own, 256)

        @pl.when(n < gate_at)
        def _():
            write(lhs_ref[0])

        @pl.when((n >= gate_at) & (n < ffn_at))
        def _():
            write(normed_ref[...])

        @pl.when((n >= ffn_at) & (n < down_at))
        def _():
            write(lhs_ref[1])

        @pl.when(n >= down_at)
        def _():
            i = n - down_at
            part = hid_ref.shape[1] // S
            k = 256 // part
            gap = low_ref.shape[0] // k
            left = [low_ref[pl.ds(pl.multiple_of(c * gap + i * own, 8), own)] for c in range(k)]
            product = nn(cat(*left), hid_ref[...]).astype(bf16)
            for d in range(S):
                parts = [product[c * own : c * own + own, part * d : part * d + part] for c in range(k)]
                out_ref[d, here] = parts[0] if k == 1 else jnp.concatenate(parts, 1)

    for u in range(per_step):
        block(pl.program_id(0) * per_step + u, u)


def rear_grad_call(lhs, normed_t, low_t, rhs, hidden, S):
    _, width, total = lhs.shape
    own = width // S
    starts = (width // 256, 2 * width // 256, rhs.shape[1] // 256)
    blocks = starts[2] + width * hidden.shape[1] // S // 256 // own
    per_step = 2 - blocks % 2
    full = lambda a: pl.BlockSpec(a.shape, lambda n: (0,) * a.ndim, pipeline_mode=pl.Buffered(1))
    return pl.pallas_call(
        functools.partial(rear_grad_kernel, starts, per_step),
        grid=(blocks // per_step,),
        in_specs=[full(a) for a in (lhs, normed_t, low_t, rhs, hidden)],
        out_specs=pl.BlockSpec((S, per_step * own, 256), lambda n: (0, n, 0)),
        out_shape=jax.ShapeDtypeStruct((S, blocks * own, 256), bf16),
        compiler_params=pltpu.CompilerParams(dimension_semantics=("arbitrary",), vmem_limit_bytes=VMEM_BYTES),
        name="rear_gradients",
        cost_estimate=pl.CostEstimate(flops=4_000_000_000, bytes_accessed=16_000_000, transcendentals=0),
    )(lhs, normed_t, low_t, rhs, hidden)


def unpack_kernel(down_at, part, sum_ref, gate_w, fgate_w, fup_w, post_ref,
                  out_ref, gate_ref, fgate_ref, fup_ref, down_ref, dot_ref, post_grad_ref):
    own = out_ref.shape[0]
    n = 0
    for ref in (out_ref, gate_ref, fgate_ref, fup_ref):
        for c in range(ref.shape[1] // 256):
            ref[:, c * 256 : c * 256 + 256] = sum_ref[n * own : n * own + own].astype(f32)
            n += 1
    gap = down_ref.shape[1] * part // 256
    for c in range(256 // part):
        block = sum_ref[down_at * own : down_at * own + gap, c * part : c * part + part].astype(f32)
        down_ref[:, c * gap : c * gap + gap] = block.T

    def row_dot(grad, weight):
        return jnp.sum(grad[...] * weight[...].astype(f32), 1, keepdims=True)

    dot_ref[...] = row_dot(gate_ref, gate_w)
    post_grad_ref[...] = (row_dot(fgate_ref, fgate_w) + row_dot(fup_ref, fup_w)) / post_ref[...].astype(f32)


def unpack_call(packed, gate_w, fgate_w, fup_w, post, ff_own):
    own, width = gate_w.shape
    ff = fgate_w.shape[1]
    shapes = [(own, width), (own, width), (own, ff), (own, ff), (ff_own, width), (own, 1), (own, 1)]
    return pl.pallas_call(
        functools.partial(unpack_kernel, (2 * width + 2 * ff) // 256, ff_own),
        out_shape=[jax.ShapeDtypeStruct(s, f32) for s in shapes],
        compiler_params=pltpu.CompilerParams(vmem_limit_bytes=VMEM_BYTES),
        name="rear_unpack",
        cost_estimate=pl.CostEstimate(flops=1_000_000, bytes_accessed=1_000_000, transcendentals=0),
    )(packed, gate_w, fgate_w, fup_w, post)


def token_kernel(parts_ref, gate_ref, tok_ref, gain_ref, middle_ref, out_ref):
    grad = gate_ref[...]
    for z in range(parts_ref.shape[0]):
        grad = grad + parts_ref[z].astype(f32)
    tok = tok_ref[...].astype(f32)
    scale = lax.rsqrt(jnp.mean(tok * tok, -1, keepdims=True) + EPS)
    out_ref[...] = (middle_ref[...] + rms_back(grad * gain_ref[...], tok, scale)).astype(bf16)


def token_call(parts, gate, tok, gain, middle):
    return pl.pallas_call(
        token_kernel,
        out_shape=jax.ShapeDtypeStruct(tok.shape, bf16),
        compiler_params=pltpu.CompilerParams(vmem_limit_bytes=VMEM_BYTES),
        name="token_gradients",
        cost_estimate=pl.CostEstimate(flops=10_000_000, bytes_accessed=4_000_000, transcendentals=0),
    )(parts, gate, tok, gain, middle)


def shards(
    tokens,
    lengths,
    cotangent,
    pre_gain,
    query_weight,
    key_weight,
    value_weight,
    gate_weight,
    rate_weight,
    out_weight,
    post_gain,
    ffn_gate,
    ffn_up,
    ffn_down,
    inner_first,
    inner_first_bias,
    inner_second,
    inner_second_bias,
    inner_gain,
    inner_shift,
):
    micro, _, rows, width = tokens.shape
    local, head, inner = inner_first.shape
    ff = ffn_gate.shape[1]
    Z = lax.axis_size("sp")
    S = lax.axis_size("fsdp")
    z = lax.axis_index("sp")
    d = lax.axis_index("fsdp")
    groups = S // micro
    slots = -(-local // groups)
    order = [[g for g in range(h, local, groups)] for h in range(groups)]
    flat = [g for part in order for g in part]
    span = 3 * head
    tiles = -(-slots * span // 128)
    piece = Z * rows
    length = S * piece
    total = micro * rows
    own = query_weight.shape[0]
    extra = local * span
    packed_width = -(-(extra + local + 2) // 128) * 128

    def columns(weight, count):
        return lax.dynamic_slice_in_dim(weight, z * count, count, 1)

    q_w, k_w, v_w = (
        columns(w, local * head).reshape(own, local, head)
        for w in (query_weight, key_weight, value_weight)
    )
    r_w = columns(rate_weight, local)
    parts = []
    for g in flat:
        parts += [q_w[:, g], k_w[:, g], v_w[:, g]]
    parts += [r_w, pre_gain[:, None], post_gain[:, None]]
    packed = pad_to(jnp.concatenate(parts, 1), packed_width, 1)
    front = gather(packed)
    all_tokens = lax.all_gather(tokens[:, 0], "sp", axis=0)
    rear_in = (out_weight, gate_weight, ffn_gate, ffn_up, ffn_down)
    rear_in, front, all_tokens = lax.optimization_barrier((rear_in, front, all_tokens))
    pre_full = front[:, extra + local].astype(f32)[None]
    post_full = front[:, extra + local + 1].astype(f32)[None]
    token_rows = all_tokens.reshape(Z * total, width).astype(f32)
    scale_one = lax.rsqrt(jnp.mean(token_rows * token_rows, -1, keepdims=True) + EPS)
    normed = (token_rows * scale_one * pre_full).astype(bf16)
    projected = nn(normed, front)
    rate_sig = jax.nn.sigmoid(projected[:, extra : extra + local])
    rate_rows = (RATE * rate_sig).astype(bf16).reshape(Z, micro, rows, local)
    rate_slope = pad_to(RATE * rate_sig * (1.0 - rate_sig), 128, 1).reshape(Z, micro, rows, 128)
    layout = dict(groups=groups, slots=slots, local=local, micro=micro, order=order, flat=flat)
    low = projected.astype(bf16).reshape(Z, micro, rows, packed_width)
    rate_tiles = slots * piece // 128

    def pack_tiles(pieces, rates):
        body = pieces.reshape(S, piece, tiles, 128).transpose(0, 2, 1, 3)
        tail = pad_to(rates.reshape(S, rate_tiles, 128), 16 * (-(-rate_tiles // 16)), 1)
        return jnp.concatenate([body.reshape(S, tiles * piece, 128), tail], 1)

    low_parts = []
    rate_parts = []
    start = 0
    for part in order:
        stop = min(start + tiles * 128, packed_width)
        low_parts.append(pad_to(low[..., start:stop], tiles * 128, 3))
        start += len(part) * span
        here = [rate_rows[..., g : g + 1] for g in part] + [jnp.zeros_like(rate_rows[..., :1])] * (slots - len(part))
        rate_parts.append(jnp.concatenate(here, 3))
    send_low = jnp.stack(low_parts).transpose(0, 2, 1, 3, 4).reshape(S, piece, tiles * 128)
    send_rate = jnp.stack(rate_parts).transpose(0, 2, 4, 1, 3).reshape(S, slots, piece)
    arrived = swap(pack_tiles(send_low, send_rate), "fsdp")

    half = d // micro
    heads_here = [jnp.minimum(half + j * groups, local - 1) for j in range(slots)]

    def of_slots(array_in):
        return jnp.stack([lax.dynamic_index_in_dim(array_in, g, 0, keepdims=False) for g in heads_here])

    w1 = of_slots(inner_first)
    b1 = of_slots(inner_first_bias)[:, None]
    w2 = of_slots(inner_second)
    w2 = (w2 - jnp.mean(w2, -1, keepdims=True)).transpose(0, 2, 1)
    b2 = of_slots(inner_second_bias)[:, None]
    b2 = b2 - jnp.mean(b2, -1, keepdims=True)
    gain = of_slots(inner_gain)[:, None]
    shift = of_slots(inner_shift)[:, None]
    mix, q, k, v, e, *saved = fwd_call(arrived, w1, b1, w2, b2, gain, shift, piece, tiles)
    w1s, w2s, z1, h, q1, n, g_, nq = saved

    out_in, gate_in, fgate_in, fup_in, down_in = rear_in
    rear = gather(jnp.concatenate([out_in, gate_in, fgate_in, fup_in], 1))
    out_full = rear[:, :width]
    gate_full = rear[:, width : 2 * width]
    fgate_full = rear[:, 2 * width : 2 * width + ff]
    fup_full = rear[:, 2 * width + ff :]
    down_full = gather(down_in)

    got = swap(mix.reshape(S * Z, rows, slots * head), ("fsdp", "sp"))
    own_tokens = tokens.reshape(total, width)
    own_normed = lax.dynamic_slice_in_dim(normed, z * total, total, 0)
    gate_act, gate_slope = gelu2(nn(own_normed, gate_full))
    position = d * piece + z * rows + lax.broadcasted_iota(jnp.int32, (micro, rows), 1)
    live = (position < lengths[:, None]).astype(f32).reshape(total, 1)
    grad_low = (cotangent.reshape(total, width).astype(f32) * live).astype(bf16)
    grad_hidden = nt(grad_low, down_full)
    got, gate_act, gate_slope, grad_hidden, normed_t, low_t = lax.optimization_barrier(
        (got, gate_act, gate_slope, grad_hidden, own_normed.T, grad_low.T)
    )
    sent, lhs, rhs, hidden, grad_middle, middle = rear_call(
        layout, got.reshape(S, Z, rows, slots * head), gate_act, gate_slope, own_tokens, rear, post_full,
        grad_hidden, grad_low,
    )
    d_mix = swap(sent.reshape(S * Z, rows, slots * head), ("fsdp", "sp")).reshape(length, slots * head)
    rear_grad = rear_grad_call(lhs, normed_t, low_t, rhs, hidden, S)
    d_mix, rear_grad = lax.optimization_barrier((d_mix, rear_grad))
    packed_rows = rear_grad.shape[1]
    rear_part = lax.psum_scatter(rear_grad.reshape(S * packed_rows, 256), "fsdp", scatter_dimension=0, tiled=True)
    output = (middle + nn(hidden, down_full)).astype(bf16)
    grad_normed_gate = nt(rhs[:, width : 2 * width], gate_full)

    packed_back, dw1, db1, dw2, db2, dgn, dsh = bwd_call(
        q, k, v, e, d_mix, n, g_, nq, w1s, w2s, z1, h, q1, gain, shift, piece, tiles
    )
    packed_back, rear_part = lax.optimization_barrier((packed_back, rear_part))
    rear_sum = lax.psum(rear_part, "sp")
    dw2 = dw2 - jnp.mean(dw2, 1, keepdims=True)
    db2 = db2 - jnp.mean(db2, -1, keepdims=True)
    small = jnp.concatenate([db1[:, 0], db2[:, 0], dgn[:, 0], dsh[:, 0], jnp.zeros((slots, head), f32)], 1)
    inner_rows = jnp.concatenate([dw1, dw2, pad_to(small.reshape(slots, 2, inner), -(-(2 * head + 2) // S) * S - 2 * head, 1)], 1)
    share = inner_rows.shape[1] // S
    inner_send = inner_rows.astype(bf16).reshape(slots, S, share, 2, 128).transpose(1, 0, 3, 2, 4)
    inner_send = inner_send.reshape(S, slots * 2 * share, 128)

    arrived = swap(packed_back, "fsdp")
    grad_packed, normed_parts = back_call(arrived, rate_slope, front, layout, piece, tiles)
    weight_parts = tn(normed, grad_packed.reshape(Z * total, packed_width)).astype(bf16)
    weight_parts = weight_parts.reshape(S, own, packed_width)
    extent = -(-inner_send.shape[1] * 128 // packed_width)
    inner_send = pad_to(inner_send.reshape(S, -1), extent * packed_width, 1).reshape(S, extent, packed_width)
    got = swap(jnp.concatenate([weight_parts, inner_send], 1), "fsdp")
    got, normed_parts, rear_sum = lax.optimization_barrier((got, normed_parts, rear_sum))
    normed_parts = swap(normed_parts.reshape(Z, total, width), "sp")
    got_sum = jnp.sum(got[:, :own].astype(f32), 0).astype(bf16)
    out_grad, gate_grad, fgate_grad, fup_grad, down_grad, gate_dot, post_grad = unpack_call(
        rear_sum, gate_weight, ffn_gate, ffn_up, post_gain[:, None], ff // S
    )
    post_grad = post_grad[:, 0]
    inner_part = got[:, own:].reshape(S, -1)[:, : slots * 2 * share * 128].astype(f32)
    inner_part = jnp.sum(inner_part.reshape(groups, micro, slots, 2, share, 128), 1)
    inner_part = inner_part.transpose(1, 0, 3, 2, 4).reshape(slots * groups, share, 2 * 128)[:local]
    rear_done = (out_grad, gate_grad, fgate_grad, fup_grad, down_grad, post_grad, gate_dot)
    rear_done, got_sum, inner_part = lax.optimization_barrier((rear_done, got_sum, inner_part.astype(bf16)))
    out_grad, gate_grad, fgate_grad, fup_grad, down_grad, post_grad, gate_dot = rear_done
    inner_sum = lax.all_gather(inner_part, "fsdp", axis=1, tiled=True)
    weight_all = lax.all_gather(got_sum, "sp", axis=0)
    inner_sum = inner_sum.astype(f32)
    query_grad, key_grad, value_grad, rate_grad, pre_grad = finish_call(
        weight_all, query_weight, key_weight, value_weight, rate_weight, gate_dot, pre_gain[:, None], layout
    )
    pre_grad = pre_grad[:, 0]
    tokens_grad = token_call(normed_parts, grad_normed_gate, own_tokens, pre_full, grad_middle)
    tail = inner_sum[:, 2 * head : 2 * head + 2].reshape(local, 2 * inner)
    return (
        output.reshape(tokens.shape),
        tokens_grad.reshape(tokens.shape),
        pre_grad,
        query_grad,
        key_grad,
        value_grad,
        gate_grad,
        rate_grad,
        out_grad,
        post_grad,
        fgate_grad,
        fup_grad,
        down_grad,
        inner_sum[:, :head],
        tail[:, :inner],
        inner_sum[:, head : 2 * head].transpose(0, 2, 1),
        tail[:, inner : inner + head],
        tail[:, inner + head : inner + 2 * head],
        tail[:, inner + 2 * head : inner + 3 * head],
    )


def solution(mesh):
    return jax.shard_map(
        shards,
        mesh=mesh,
        in_specs=(
            P(None, "fsdp", "sp", None),
            P(),
            P(None, "fsdp", "sp", None),
            P("fsdp"),
            P("fsdp", None),
            P("fsdp", None),
            P("fsdp", None),
            P("fsdp", None),
            P("fsdp", None),
            P("fsdp", None),
            P("fsdp"),
            P("fsdp", None),
            P("fsdp", None),
            P("fsdp", None),
            P("sp", None, None),
            P("sp", None),
            P("sp", None, None),
            P("sp", None),
            P("sp", None),
            P("sp", None),
        ),
        out_specs=(
            P(None, "fsdp", "sp", None),
            P(None, "fsdp", "sp", None),
            P("fsdp"),
            P("fsdp", None),
            P("fsdp", None),
            P("fsdp", None),
            P("fsdp", None),
            P("fsdp", None),
            P("fsdp", None),
            P("fsdp"),
            P("fsdp", None),
            P("fsdp", None),
            P("fsdp", None),
            P("sp", None, None),
            P("sp", None),
            P("sp", None, None),
            P("sp", None),
            P("sp", None),
            P("sp", None),
        ),
        check_vma=False,
    )
```

```python
import functools

import jax
import jax.numpy as jnp
from jax import lax
from jax.experimental import pallas as pl
from jax.experimental.pallas import tpu as pltpu
from jax.sharding import PartitionSpec as P

MINI = 16
EPS = 1e-06
RATE = 1.0 / 1024.0
GELU_C = 0.7978845608028654
GELU_K = 0.044715
VMEM_BYTES = 58 * 1024 * 1024
f32 = jnp.float32
bf16 = jnp.bfloat16

def nn(x,y): return lax.dot_general(x.astype(bf16),y.astype(bf16),(((1,),(0,)),((),())),preferred_element_type=f32)
def nt(x,y): return lax.dot_general(x.astype(bf16),y.astype(bf16),(((1,),(1,)),((),())),preferred_element_type=f32)
def tn(x,y): return lax.dot_general(x.astype(bf16),y.astype(bf16),(((0,),(0,)),((),())),preferred_element_type=f32)
def gelu1(z):
    t=jnp.tanh(GELU_C*z*(1.0+GELU_K*(z*z)))
    return 0.5*z*(1.0+t)
def gelu2(z):
    z2=z*z
    t=jnp.tanh(z*(GELU_C+(GELU_C*GELU_K)*z2))
    h=0.5+0.5*t
    return z*h, h+0.5*z*(1.0-t*t)*(GELU_C+(3.0*GELU_C*GELU_K)*z2)
def gelu3(z):
    z2=z*z
    t=jnp.tanh(z*(GELU_C+(GELU_C*GELU_K)*z2))
    h=0.5+0.5*t
    u=GELU_C+(3.0*GELU_C*GELU_K)*z2
    c=1.0-t*t
    return z*h, h+0.5*z*c*u, c*(u+z*((3.0*GELU_C*GELU_K)*z-t*u*u))

def cat(*xs): return jnp.concatenate(xs,0)
def rs(x): return jnp.sum(x,-1,keepdims=True)*(1.0/64)

def interleave(gens):
    gens=list(gens)
    while gens:
        alive=[]
        for g in gens:
            try:
                next(g); alive.append(g)
            except StopIteration: pass
        gens=alive

def masks():
    lower=lax.broadcasted_iota(jnp.int32,(MINI,MINI),0)>=lax.broadcasted_iota(jnp.int32,(MINI,MINI),1)
    return lower.astype(f32), jnp.where(lower,0.0,1.0)

def fwd_kernel(slots,count,unroll,piece,tiles,x_ref,w1_ref,b1_ref,w2_ref,b2_ref,gain_ref,shift_ref,
    mix_ref,q_ref,k_ref,v_ref,e_ref,w1s_ref,w2s_ref,z1_ref,h_ref,q1_ref,n_ref,g_ref,nq_ref,
    W1,B1,W2,B2,Z,ZQ,AP,EP):
    lower,upper=masks()
    steps=q_ref.shape[1]//MINI
    pid=pl.program_id(0)
    @pl.when(pid==0)
    def _():
        eye=lax.broadcasted_iota(jnp.int32,(128,128),0)==lax.broadcasted_iota(jnp.int32,(128,128),1)
        @pl.loop(0,x_ref.shape[0])
        def _(src):
            base=pl.multiple_of(src*piece,piece)
            for j in range(slots):
                for index,ref in enumerate((q_ref,k_ref,v_ref)):
                    lane=(3*j+index)*64
                    top=lane//128*piece
                    ref[j,pl.ds(base,piece)]=x_ref[src,top:top+piece,lane%128:lane%128+64]
            rates=x_ref[src,tiles*piece:tiles*piece+16].astype(f32)
            for j in range(slots):
                for i in range(piece//128):
                    n=j*(piece//128)+i
                    column=jnp.sum(jnp.where(eye,rates[n:n+1],0.0),1,keepdims=True)
                    e_ref[j,pl.ds(base+i*128,128)]=jnp.broadcast_to(column,(128,128))
        for j in range(slots):
            W1[j]=w1_ref[j]; B1[j]=b1_ref[j]; W2[j]=w2_ref[j]; B2[j]=b2_ref[j]
            Z[j]=nn(k_ref[j,:MINI],w1_ref[j])+b1_ref[j]
            ZQ[j]=jnp.zeros((MINI,256),f32); AP[j]=jnp.zeros((MINI,256),bf16); EP[j]=jnp.zeros((MINI,64),bf16)
    def chain(j,i):
        t=pid*count+i
        rows=pl.ds(pl.multiple_of(t*MINI,MINI),MINI)
        prow=pl.ds(pl.multiple_of(jnp.maximum(t-1,0)*MINI,MINI),MINI)
        nrow=pl.ds(pl.multiple_of(jnp.minimum(t+1,steps-1)*MINI,MINI),MINI)
        brow=pl.ds(pl.multiple_of(i*MINI,MINI),MINI)
        gain=gain_ref[j]; shift=shift_ref[j]; g2=gain*gain; mg=rs(g2)
        z1=Z[j]; q1=ZQ[j]; w2=W2[j]; b2=B2[j]
        w2b=w2.astype(bf16)
        Ap=AP[j]; Ep=EP[j]
        A,Ad=gelu2(z1); AQ=gelu1(q1)
        Ab=A.astype(bf16); AQb=AQ.astype(bf16)
        z1_ref[j,brow]=z1.astype(bf16)
        yield
        zz=nt(cat(Ab,AQb),w2b)
        z=zz[:MINI]+b2; qb=zz[MINI:]+b2
        yield
        P2=upper*(nt(AQb,Ap)+1.0)
        K=k_ref[j,rows]; Q=q_ref[j,rows]; Kn=k_ref[j,nrow]
        w1=W1[j]; w1b=w1.astype(bf16); b1=B1[j]
        w1s_ref[j,i]=w1b; w2s_ref[j,i]=w2b
        KQ=cat(Kn,Q)
        KK=nt(KQ,K)+1.0
        L=cat(KK[:MINI].astype(bf16),(lower*KK[MINI:]).astype(bf16),K.T)
        base=nn(KQ,w1b)+b1
        U=gain*(shift-v_ref[j,rows].astype(f32)+K.astype(f32)); mU=rs(U)
        e=e_ref[j,rows]; e64=e[:,:64]; e256=jnp.concatenate([e,e],1)
        yield
        Q2=qb+nn(P2,Ep)
        yield
        zg=z*g2
        mz=rs(z); p0=rs(z*z); p1=rs(zg); p2=rs(z*zg); p3=rs(z*U)
        s=lax.rsqrt(p0-mz*mz+EPS)
        m1=s*(p1-mz*mg)+mU
        m2=s*(s*(p2-2.0*mz*p1+mz*mz*mg)+(p3-mz*mU))
        N=s*(z-mz)
        G=s*(N*(g2-m2)+(U-m1))
        Gb=G.astype(bf16)
        yield
        H=nn(Gb,w2b)
        E2=e64*G; E2b=E2.astype(bf16)
        n_ref[j,rows]=(z-mz).astype(bf16); g_ref[j,rows]=Gb
        EP[j]=E2b; AP[j]=Ab
        yield
        W2[j]=w2-tn(E2b,Ab)
        B2[j]=b2-jnp.sum(E2,0,keepdims=True)
        yield
        E1=(e256*Ad)*H; E1b=E1.astype(bf16)
        X=nn(L,E1b)
        Z[j]=base[:MINI]-X[:MINI]
        Q1=base[MINI:]-X[MINI:2*MINI]
        ZQ[j]=Q1
        W1[j]=w1-X[2*MINI:]
        B1[j]=b1-jnp.sum(E1,0,keepdims=True)
        h_ref[j,brow]=H.astype(bf16); q1_ref[j,brow]=Q1.astype(bf16)
        yield
        mq=rs(Q2); vq=rs(Q2*Q2)
        sq=lax.rsqrt(vq-mq*mq+EPS)
        Nq=sq*(Q2-mq)
        Qp=q_ref[j,prow].astype(f32)
        mix_ref[prow,64*j:64*j+64]=(Qp+Nq*gain+shift).astype(bf16)
        nq_ref[j,prow]=(Q2-mq).astype(bf16)
    @pl.loop(0,count//unroll)
    def _(i):
        for u in range(unroll):
            interleave(chain(j,i*unroll+u) for j in range(slots))
    @pl.when(pid==pl.num_programs(0)-1)
    def _():
        for j in range(slots):
            prow=pl.ds((steps-1)*MINI,MINI)
            AQb=gelu1(ZQ[j]).astype(bf16)
            Q2=nt(AQb,W2[j])+B2[j]+nn(upper*(nt(AQb,AP[j])+1.0),EP[j])
            mq=rs(Q2); vq=rs(Q2*Q2)
            sq=lax.rsqrt(vq-mq*mq+EPS)
            Nq=sq*(Q2-mq)
            mix_ref[prow,64*j:64*j+64]=(q_ref[j,prow].astype(f32)+Nq*gain_ref[j]+shift_ref[j]).astype(bf16)
            nq_ref[j,prow]=(Q2-mq).astype(bf16)

def fwd_call(x,w1,b1,w2,b2,gain,shift,piece,tiles,block=256,unroll=2,**kw):
    slots=w1.shape[0]; length=x.shape[0]*piece
    count=block//MINI; nb=length//block; steps=length//MINI
    row=lambda w: pl.BlockSpec((slots,block,w),lambda i:(0,i,0))
    full=lambda s: pl.BlockSpec(s,lambda i:(0,)*len(s),pipeline_mode=pl.Buffered(1))
    r64=full((slots,length,64)); r1=full((slots,length,128)); rm_=full((length,64*slots))
    st=pl.BlockSpec((slots,count,64,256),lambda i:(0,i,0,0))
    S=jax.ShapeDtypeStruct
    return pl.pallas_call(functools.partial(fwd_kernel,slots,count,unroll,piece,tiles),
        grid=(nb,),
        in_specs=[full(a.shape) for a in (x,w1,b1,w2,b2,gain,shift)],
        out_specs=[rm_,r64,r64,r64,r1,st,st,row(256),row(256),row(256),r64,r64,r64],
        out_shape=[S((length,64*slots),bf16)]+[S((slots,length,64),bf16)]*3+[S((slots,length,128),f32)]+[S((slots,steps,64,256),bf16)]*2+[S((slots,length,256),bf16)]*3+[S((slots,length,64),bf16)]*3,
        scratch_shapes=[pltpu.VMEM((slots,64,256),f32),pltpu.VMEM((slots,1,256),f32),pltpu.VMEM((slots,64,256),f32),pltpu.VMEM((slots,1,64),f32),pltpu.VMEM((slots,MINI,256),f32),pltpu.VMEM((slots,MINI,256),f32),pltpu.VMEM((slots,MINI,256),bf16),pltpu.VMEM((slots,MINI,64),bf16)],
        compiler_params=pltpu.CompilerParams(dimension_semantics=("arbitrary",),vmem_limit_bytes=VMEM_BYTES),
        name="inner_forward",cost_estimate=pl.CostEstimate(flops=90_000_000_000,bytes_accessed=40_000_000,transcendentals=0),**kw)(x,w1,b1,w2,b2,gain,shift)


def bwd_kernel(slots,count,unroll,piece,tiles,q_ref,k_ref,v_ref,e_ref,dx_ref,n_ref,g_ref,nq_ref,w1s_ref,w2s_ref,z1_ref,h_ref,q1_ref,gain_ref,shift_ref,
    out_ref,dw1_ref,db1_ref,dw2_ref,db2_ref,dgn_ref,dsh_ref,
    do_ref,de_ref,    DW1,DB1,G2,DB2,KD,DGN,DSH,DGQ,DSQ,
    sA,sAd,sHA,sGZ,sE1,sE2,sW1,sW2,sR1,sR2,sDA,sQ1,sQ2,sAQ,sb1,sb2):
    lower,_=masks()
    steps=q_ref.shape[1]//MINI
    pid=pl.program_id(0); nb=pl.num_programs(0)
    @pl.when(pid==0)
    def _():
        @pl.loop(0,out_ref.shape[0])
        def _(src):
            rows=pl.ds(pl.multiple_of(src*piece,piece),piece)
            for j in range(slots):
                do_ref[j,rows]=dx_ref[rows,64*j:64*j+64]
        for r in (DW1,DB1,G2,DB2,KD,DGN,DSH,DGQ,DSQ):
            r[...]=jnp.zeros(r.shape,r.dtype)
        for r in (sA,sAd,sHA,sGZ,sE1,sE2,sW1,sW2,sR1,sR2,sDA,sQ1,sQ2,sAQ,sb1,sb2):
            r[0]=jnp.zeros(r.shape[1:],r.dtype)
    def put(j,index,t,value):
        t=jnp.minimum(t,steps-1)
        lane=(3*j+index)*64
        top=lane//128*piece
        part=piece//MINI
        rows=pl.ds(pl.multiple_of(top+lax.rem(t,part)*MINI,MINI),MINI)
        out_ref[lax.div(t,part),rows,lane%128:lane%128+64]=value.astype(bf16)
    def crit(j,p,t):
        rows=pl.ds(pl.multiple_of(jnp.minimum(t,steps-1)*MINI,MINI),MINI)
        prow=pl.ds(pl.multiple_of(jnp.maximum(t-1,0)*MINI,MINI),MINI)
        gain=gain_ref[j]; shift=shift_ref[j]; g2=gain*gain; mg=rs(g2)
        e=e_ref[j,rows]; e64=e[:,:64]; e=jnp.concatenate([e,e],1)
        nE1=sR1[p,j]+KD[j]
        dgZ1=(-e)*nE1
        dH=dgZ1*sAd[p,j]
        dHb=dH.astype(bf16)
        w2b=sW2[p,j]
        G2f=G2[j]; G2b=G2f.astype(bf16)
        Ab=sA[p,j]; E2b=sE2[p,j]
        yield
        a1=nt(Ab,G2b)
        yP=nt(dHb,w2b)
        yield
        Zc=n_ref[j,rows].astype(f32); G=g_ref[j,rows].astype(f32)
        s=lax.rsqrt(rs(Zc*Zc)+EPS); N=s*Zc
        K=k_ref[j,rows]; Q=q_ref[j,rows]; Kp=k_ref[j,prow]
        T=shift-v_ref[j,rows].astype(f32)+K.astype(f32)
        U=gain*T
        gN=N*g2
        c1=rs(gN); c2=rs(gN*N); mU=rs(U); UN=rs(U*N)
        a=gN+U; ma=c1+mU; m2=c2+UN
        a2=nn(E2b,G2b)
        E1b=sE1[p,j]; dQ1b=sQ1[p,j]
        DW=DW1[j]; DWb=DW.astype(bf16)
        KDb=nn(Kp,DWb)+DB1[j]
        yield
        a3=nt(E1b,DWb)
        X1=(lower*nt(dQ1b,E1b)).astype(bf16)
        L2=cat((nt(Kp,cat(Q,K))+1.0).astype(bf16),cat(Q,K).T)
        yield
        nE2=sR2[p,j]+a1+DB2[j]
        y=yP-e64*nE2
        yg=y*g2; yn=y*N
        ym=rs(y); yN=rs(yn); yG=rs(y*G); ygm=rs(yg); ygN=rs(yg*N)
        mdy=s*ym; mdyN=s*yN
        da=s*y-mdy-N*mdyN
        sN=s*ygN-mdy*c1-mdyN*c2-2.0*m2*mdyN
        mN=s*ygm-mdy*mg-mdyN*c1-ma*mdyN-m2*mdy
        kap=yG+sN
        dN=da*g2-a*mdyN-(s*m2)*y
        dZc=s*(dN-mN-N*kap)
        dZb=dZc.astype(bf16)
        dT=da*gain
        yield
        dA=nn(dZb,w2b)+sDA[p,j]-a2
        yield
        G2[j]=G2f+tn(cat(sQ2[p,j],g_ref[j,rows],dZb),cat(sAQ[p,j],dHb,Ab))
        DB2[j]=DB2[j]+sb2[p,j]+jnp.sum(dZc,0,keepdims=True)
        dQs=nn(X1,K); dKs=tn(X1,Q)
        put(j,2,t,-dT)
        dO=do_ref[j,rows].astype(f32)
        DGN[j]=DGN[j]+da*(2.0*gain*N+T)
        DSH[j]=DSH[j]+dT
        de_ref[j,rows]=-(jnp.sum(nE1*sGZ[p,j],-1,keepdims=True)+jnp.sum(nE2*G,-1,keepdims=True))
        yield
        dZ1=dA*sAd[p,j]+dgZ1*sHA[p,j]
        dZ1b=dZ1.astype(bf16)
        dd=cat(dQ1b,dZ1b)
        X=nn(L2,dd)
        KD[j]=KDb+X[:MINI]
        DW1[j]=DW+X[MINI:]
        DB1[j]=DB1[j]+sb1[p,j]+jnp.sum(dZ1,0,keepdims=True)
        yield
        qk=nt(dd,sW1[p,j])
        put(j,0,t,dO+qk[:MINI]-dQs)
        put(j,1,t,qk[MINI:]-dKs-a3+dT)
    def qside(j,p,t,i):
        rows=pl.ds(pl.multiple_of(t*MINI,MINI),MINI)
        brow=pl.ds(pl.multiple_of(i*MINI,MINI),MINI)
        gain=gain_ref[j]
        dO=do_ref[j,rows].astype(f32); Qc=nq_ref[j,rows].astype(f32)
        sq=lax.rsqrt(rs(Qc*Qc)+EPS); Nq=sq*Qc
        dNq=dO*gain
        dQ2=sq*(dNq-rs(dNq)-Nq*rs(dNq*Nq))
        dQ2b=dQ2.astype(bf16)
        A,Ad,Add=gelu3(z1_ref[j,brow].astype(f32))
        AQ,AQd=gelu2(q1_ref[j,brow].astype(f32))
        H=h_ref[j,brow].astype(f32); e=e_ref[j,rows]; e64=e[:,:64]; e=jnp.concatenate([e,e],1)
        Ab=A.astype(bf16); AQb=AQ.astype(bf16)
        gZ1=H*Ad
        E1b=(e*gZ1).astype(bf16); E2b=(e64*g_ref[j,rows].astype(f32)).astype(bf16)
        w1b=w1s_ref[j,i]; w2b=w2s_ref[j,i]
        yield
        sA[p,j]=Ab; sAd[p,j]=Ad; sHA[p,j]=H*Add; sGZ[p,j]=gZ1; sE1[p,j]=E1b; sE2[p,j]=E2b; sW1[p,j]=w1b; sW2[p,j]=w2b; sAQ[p,j]=AQb
        sQ2[p,j]=dQ2b; sb2[p,j]=jnp.sum(dQ2,0,keepdims=True)
        DGQ[j]=DGQ[j]+dO*Nq; DSQ[j]=DSQ[j]+dO
        Q=q_ref[j,rows]; K=k_ref[j,rows]
        P1=(lower*(nt(Q,K)+1.0)).astype(bf16)
        P2=(lower*(nt(AQb,Ab)+1.0)).astype(bf16)
        yield
        X2=(lower*nt(dQ2b,E2b)).astype(bf16)
        yield
        b1=nn(dQ2b,w2b)
        yield
        sR2[p,j]=tn(P2,dQ2b)
        yield
        dAQ=b1-nn(X2,Ab)
        sDA[p,j]=-tn(X2,AQb)
        yield
        yield
        dQ1=dAQ*AQd
        dQ1b=dQ1.astype(bf16)
        sQ1[p,j]=dQ1b; sb1[p,j]=jnp.sum(dQ1,0,keepdims=True)
        sR1[p,j]=tn(P1,dQ1b)
    @pl.loop(0,count//unroll)
    def _(i):
        for u in range(unroll):
            ii=count-1-(i*unroll+u)
            t=(nb-1-pid)*count+ii
            interleave([crit(j,u%2,t+1) for j in range(slots)]+[qside(j,(u+1)%2,t,ii) for j in range(slots)])
    @pl.when(pid==nb-1)
    def _():
        interleave([crit(j,0,jnp.int32(0)) for j in range(slots)])
        eye=lax.broadcasted_iota(jnp.int32,(128,128),0)==lax.broadcasted_iota(jnp.int32,(128,128),1)
        @pl.loop(0,out_ref.shape[0])
        def _(dst):
            base=pl.multiple_of(dst*piece,piece)
            rows=[jnp.sum(jnp.where(eye,de_ref[j,pl.ds(base+i*128,128)],0.0),0,keepdims=True) for j in range(slots) for i in range(piece//128)]
            rows.append(jnp.zeros((16-len(rows),128),f32))
            out_ref[dst,tiles*piece:tiles*piece+16]=cat(*rows).astype(bf16)
            if tiles*128>slots*192:
                out_ref[dst,(tiles-1)*piece:tiles*piece,(slots*192)%128:]=jnp.zeros((piece,128-(slots*192)%128),bf16)
        for j in range(slots):
            dw1_ref[j]=DW1[j]; db1_ref[j]=DB1[j]; dw2_ref[j]=G2[j]; db2_ref[j]=DB2[j]
            dgn_ref[j]=jnp.sum(DGN[j]+DGQ[j],0,keepdims=True); dsh_ref[j]=jnp.sum(DSH[j]+DSQ[j],0,keepdims=True)

def bwd_call(q,k,v,e,dO,n,g,nq,w1s,w2s,z1,h,q1,gain,shift,piece,tiles,block=256,unroll=2,**kw):
    slots,length,_=q.shape
    count=block//MINI; nb=length//block; steps=length//MINI
    row=lambda w: pl.BlockSpec((slots,block,w),lambda i:(0,nb-1-i,0))
    full=lambda s: pl.BlockSpec(s,lambda i:(0,)*len(s),pipeline_mode=pl.Buffered(1))
    r64=full((slots,length,64)); r1=full((slots,length,128))
    st=pl.BlockSpec((slots,count,64,256),lambda i:(0,nb-1-i,0,0))
    S=jax.ShapeDtypeStruct
    outs=[((length//piece,tiles*piece+16,128),bf16),((slots,64,256),f32),((slots,1,256),f32),((slots,64,256),f32),((slots,1,64),f32),((slots,1,64),f32),((slots,1,64),f32)]
    V=lambda *s,d=f32: pltpu.VMEM(s,d)
    return pl.pallas_call(functools.partial(bwd_kernel,slots,count,unroll,piece,tiles),
        grid=(nb,),
        in_specs=[r64]*3+[r1,full(dO.shape)]+[r64]*3+[st,st]+[row(256)]*3+[full(gain.shape)]*2,
        out_specs=[full(o[0]) for o in outs],
        out_shape=[S(*o) for o in outs],
        scratch_shapes=[V(slots,length,64,d=bf16),V(slots,length,1),V(slots,64,256),V(slots,1,256),V(slots,64,256),V(slots,1,64),V(slots,MINI,256),V(slots,MINI,64),V(slots,MINI,64),V(slots,MINI,64),V(slots,MINI,64),
          V(2,slots,MINI,256,d=bf16),V(2,slots,MINI,256),V(2,slots,MINI,256),V(2,slots,MINI,256),V(2,slots,MINI,256,d=bf16),V(2,slots,MINI,64,d=bf16),
          V(2,slots,64,256,d=bf16),V(2,slots,64,256,d=bf16),V(2,slots,MINI,256),V(2,slots,MINI,64),V(2,slots,MINI,256),V(2,slots,MINI,256,d=bf16),V(2,slots,MINI,64,d=bf16),V(2,slots,MINI,256,d=bf16),V(2,slots,1,256),V(2,slots,1,64)],
        compiler_params=pltpu.CompilerParams(dimension_semantics=("arbitrary",),vmem_limit_bytes=VMEM_BYTES),
        name="inner_backward",cost_estimate=pl.CostEstimate(flops=110_000_000_000,bytes_accessed=40_000_000,transcendentals=0),**kw)(q,k,v,e,dO,n,g,nq,w1s,w2s,z1,h,q1,gain,shift)


def rms_back(grad_scaled, inputs, scale):
    return scale * (
        grad_scaled - inputs * scale * scale * jnp.mean(grad_scaled * inputs, -1, keepdims=True)
    )


def gather(block):
    return lax.all_gather(block, "fsdp", axis=0, tiled=True)


def swap(block, axes):
    return lax.all_to_all(block, axes, split_axis=0, concat_axis=0, tiled=True)


def pad_to(array_in, size, dim):
    widths = [(0, 0)] * array_in.ndim
    widths[dim] = (0, size - array_in.shape[dim])
    return jnp.pad(array_in, widths)


def back_kernel(layout, piece, tiles, a_ref, slope_ref, front_ref, grad_ref, parts_ref):
    micro_step = pl.program_id(0)
    groups, slots, local, micro = layout["groups"], layout["slots"], layout["local"], layout["micro"]
    eye = lax.broadcasted_iota(jnp.int32, (128, 128), 0) == lax.broadcasted_iota(jnp.int32, (128, 128), 1)
    lanes = lax.broadcasted_iota(jnp.int32, (piece, 64), 1)
    rates = jnp.zeros((piece, 64), f32)
    for h, part in enumerate(layout["order"]):
        block = a_ref[h * micro + micro_step, tiles * piece : tiles * piece + 16].astype(f32)
        for j, g in enumerate(part):
            column = []
            for i in range(piece // 128):
                n = j * (piece // 128) + i
                column.append(jnp.sum(jnp.where(eye, block[n : n + 1], 0.0), 1, keepdims=True))
            rates = jnp.where(lanes == g, cat(*column), rates)
    slope = slope_ref[:, 0].reshape(piece, slope_ref.shape[-1])
    rates = rates * slope[:, :64]
    halves = []
    for h, part in enumerate(layout["order"]):
        for lane in range(0, len(part) * 192, 64):
            halves.append((h, lane))
    halves.append(None)
    chunks = []
    for n in range(0, len(halves), 2):
        pair = halves[n : n + 2]
        if pair[0] is not None and len(pair) == 2 and pair[1] is not None:
            (h, lane), (h2, lane2) = pair
            if h == h2 and lane % 128 == 0:
                top = lane // 128 * piece
                chunks.append(a_ref[h * micro + micro_step, top : top + piece])
                continue
        values = []
        for half in pair:
            if half is None:
                values.append(rates.astype(bf16))
            else:
                h, lane = half
                top = lane // 128 * piece
                values.append(a_ref[h * micro + micro_step, top : top + piece, lane % 128 : lane % 128 + 64])
        if len(values) == 1:
            values.append(jnp.zeros((piece, 64), bf16))
        chunks.append(jnp.concatenate(values, 1))
    grad = jnp.concatenate(chunks, 1)
    product = nt(grad, front_ref[...]).astype(bf16)
    rows = piece // grad_ref.shape[0]
    grad_ref[:, 0] = grad.reshape(grad_ref.shape[0], rows, grad.shape[1])
    parts_ref[:, 0] = product.reshape(parts_ref.shape[0], rows, product.shape[1])


def back_call(arrived, slope, front, layout, piece, tiles):
    Z, micro, rows, _ = slope.shape
    width = front.shape[0]
    packed = front.shape[1]
    full = lambda s: pl.BlockSpec(s, lambda i: (0,) * len(s), pipeline_mode=pl.Buffered(1))
    step = lambda w: pl.BlockSpec((Z, 1, rows, w), lambda i: (0, i, 0, 0))
    return pl.pallas_call(
        functools.partial(back_kernel, layout, piece, tiles),
        grid=(micro,),
        in_specs=[full(arrived.shape), step(slope.shape[-1]), full(front.shape)],
        out_specs=[step(packed), step(width)],
        out_shape=[
            jax.ShapeDtypeStruct((Z, micro, rows, packed), bf16),
            jax.ShapeDtypeStruct((Z, micro, rows, width), bf16),
        ],
        compiler_params=pltpu.CompilerParams(dimension_semantics=("arbitrary",), vmem_limit_bytes=VMEM_BYTES),
        name="projection_gradients",
        cost_estimate=pl.CostEstimate(flops=1_000_000_000, bytes_accessed=8_000_000, transcendentals=0),
    )(arrived, slope, front)


def finish_kernel(layout, all_ref, q_ref, k_ref, v_ref, r_ref, gate_ref, pre_ref, dq_ref, dk_ref, dv_ref, dr_ref, dot_ref):
    local = layout["local"]
    flat = layout["flat"]
    Z = all_ref.shape[0]
    own = dq_ref.shape[0]
    dot = jnp.zeros((own, 1), f32)
    rate = jnp.zeros((own, dr_ref.shape[1]), f32)
    lanes = lax.broadcasted_iota(jnp.int32, rate.shape, 1)
    for index, (weight, out) in enumerate(((q_ref, dq_ref), (k_ref, dk_ref), (v_ref, dv_ref))):
        for z in range(Z):
            for g in range(local):
                start = (flat.index(g) * 3 + index) * 64
                value = all_ref[z, :, start : start + 64].astype(f32)
                place = (z * local + g) * 64
                out[:, place : place + 64] = value
        dot = dot + jnp.sum(out[...] * weight[...].astype(f32), 1, keepdims=True)
    for z in range(Z):
        for g in range(local):
            n = local * 192 + g
            rate = jnp.where(lanes == z * local + g, all_ref[z, :, n : n + 1].astype(f32), rate)
    dr_ref[...] = rate
    dot = dot + jnp.sum(rate * r_ref[...].astype(f32), 1, keepdims=True) + gate_ref[...]
    dot_ref[...] = dot / pre_ref[...].astype(f32)


def finish_call(gathered, q_w, k_w, v_w, r_w, gate_dot, pre, layout):
    own, width = q_w.shape
    Z = gathered.shape[0]
    shapes = [(own, width)] * 3 + [(own, Z * layout["local"]), (own, 1)]
    return pl.pallas_call(
        functools.partial(finish_kernel, layout),
        out_shape=[jax.ShapeDtypeStruct(s, f32) for s in shapes],
        compiler_params=pltpu.CompilerParams(vmem_limit_bytes=VMEM_BYTES),
        name="weight_gradients",
        cost_estimate=pl.CostEstimate(flops=10_000_000, bytes_accessed=2_000_000, transcendentals=0),
    )(gathered, q_w, k_w, v_w, r_w, gate_dot, pre)


def rear_kernel(layout, got_ref, act_ref, slope_ref, tok_ref, w_ref, post_ref, gh_ref, go_ref,
                send_ref, lhs_ref, rhs_ref, hid_ref, gm_ref, mid_ref):
    groups, slots, local, micro = layout["groups"], layout["slots"], layout["local"], layout["micro"]
    Z, rows = got_ref.shape[1], got_ref.shape[2]
    total, width = act_ref.shape
    ff = hid_ref.shape[1]
    blocks = []
    for m in range(micro):
        pieces = []
        for z in range(Z):
            for g in range(local):
                h, j = g % groups, g // groups
                pieces.append(got_ref[h * micro + m, z, :, 64 * j : 64 * j + 64])
        blocks.append(jnp.concatenate(pieces, 1))
    mixed = cat(*blocks).astype(f32)
    gated = (act_ref[...] * mixed).astype(bf16)
    lhs_ref[0] = gated.T
    middle = tok_ref[...].astype(f32) + nn(gated, w_ref[:, :width])
    mid_ref[...] = middle
    scale = lax.rsqrt(jnp.mean(middle * middle, -1, keepdims=True) + EPS)
    post = post_ref[...]
    low = (middle * scale * post).astype(bf16)
    lhs_ref[1] = low.T
    gm_ref[...] = jnp.zeros((total, width), f32)
    step = 256

    @pl.loop(0, ff // step)
    def _(c):
        here = pl.ds(pl.multiple_of(c * step, step), step)
        gate_at = pl.ds(pl.multiple_of(2 * width + c * step, step), step)
        up_at = pl.ds(pl.multiple_of(2 * width + ff + c * step, step), step)
        gate_w, up_w = w_ref[:, gate_at], w_ref[:, up_at]
        gate_pre, up_pre = nn(low, gate_w), nn(low, up_w)
        sig = 0.5 + 0.5 * jnp.tanh(0.5 * gate_pre)
        silu = gate_pre * sig
        hid_ref[:, here] = (silu * up_pre).astype(bf16)
        grad = gh_ref[:, here]
        g_gate = (grad * up_pre * sig * (1.0 + gate_pre * (1.0 - sig))).astype(bf16)
        g_up = (grad * silu).astype(bf16)
        rhs_ref[:, gate_at] = g_gate
        rhs_ref[:, up_at] = g_up
        gm_ref[...] += nt(g_gate, gate_w) + nt(g_up, up_w)

    middle = mid_ref[...]
    grad_middle = go_ref[...].astype(f32) + rms_back(gm_ref[...] * post, middle, scale)
    gm_ref[...] = grad_middle
    branch = grad_middle.astype(bf16)
    rhs_ref[:, :width] = branch
    grad_gated = nt(branch, w_ref[:, :width])
    grad_mixed = (grad_gated * act_ref[...]).astype(bf16)
    rhs_ref[:, width : 2 * width] = (grad_gated * mixed * slope_ref[...]).astype(bf16)
    for m in range(micro):
        for z in range(Z):
            for h in range(groups):
                for j in range(slots):
                    g = h + j * groups
                    if g < local:
                        lane = (z * local + g) * 64
                        value = grad_mixed[m * rows : m * rows + rows, lane : lane + 64]
                    else:
                        value = jnp.zeros((rows, 64), bf16)
                    send_ref[h * micro + m, z, :, 64 * j : 64 * j + 64] = value


def rear_call(layout, got, act, slope, tok, weights, post, grad_hidden, grad_low):
    total, width = act.shape
    ff = grad_hidden.shape[1]
    S_ = jax.ShapeDtypeStruct
    return pl.pallas_call(
        functools.partial(rear_kernel, layout),
        out_shape=[
            S_(got.shape, bf16), S_((2, width, total), bf16), S_((total, weights.shape[1]), bf16),
            S_((total, ff), bf16), S_((total, width), f32), S_((total, width), f32),
        ],
        compiler_params=pltpu.CompilerParams(vmem_limit_bytes=VMEM_BYTES),
        name="rear",
        cost_estimate=pl.CostEstimate(flops=5_000_000_000, bytes_accessed=16_000_000, transcendentals=0),
    )(got, act, slope, tok, weights, post, grad_hidden, grad_low)


def rear_grad_kernel(starts, per_step, lhs_ref, normed_ref, low_ref, rhs_ref, hid_ref, out_ref):
    S = out_ref.shape[0]
    own = out_ref.shape[1] // per_step
    gate_at, ffn_at, down_at = starts

    def block(n, top):
        here = pl.ds(top * own, own)

        def write(left):
            right = rhs_ref[:, pl.ds(pl.multiple_of(n * 256, 256), 256)]
            out_ref[:, here] = nn(left, right).astype(bf16).reshape(S, own, 256)

        @pl.when(n < gate_at)
        def _():
            write(lhs_ref[0])

        @pl.when((n >= gate_at) & (n < ffn_at))
        def _():
            write(normed_ref[...])

        @pl.when((n >= ffn_at) & (n < down_at))
        def _():
            write(lhs_ref[1])

        @pl.when(n >= down_at)
        def _():
            i = n - down_at
            part = hid_ref.shape[1] // S
            k = 256 // part
            gap = low_ref.shape[0] // k
            left = [low_ref[pl.ds(pl.multiple_of(c * gap + i * own, 8), own)] for c in range(k)]
            product = nn(cat(*left), hid_ref[...]).astype(bf16)
            for d in range(S):
                parts = [product[c * own : c * own + own, part * d : part * d + part] for c in range(k)]
                out_ref[d, here] = parts[0] if k == 1 else jnp.concatenate(parts, 1)

    for u in range(per_step):
        block(pl.program_id(0) * per_step + u, u)


def rear_grad_call(lhs, normed_t, low_t, rhs, hidden, S):
    _, width, total = lhs.shape
    own = width // S
    starts = (width // 256, 2 * width // 256, rhs.shape[1] // 256)
    blocks = starts[2] + width * hidden.shape[1] // S // 256 // own
    per_step = 2 - blocks % 2
    full = lambda a: pl.BlockSpec(a.shape, lambda n: (0,) * a.ndim, pipeline_mode=pl.Buffered(1))
    return pl.pallas_call(
        functools.partial(rear_grad_kernel, starts, per_step),
        grid=(blocks // per_step,),
        in_specs=[full(a) for a in (lhs, normed_t, low_t, rhs, hidden)],
        out_specs=pl.BlockSpec((S, per_step * own, 256), lambda n: (0, n, 0)),
        out_shape=jax.ShapeDtypeStruct((S, blocks * own, 256), bf16),
        compiler_params=pltpu.CompilerParams(dimension_semantics=("arbitrary",), vmem_limit_bytes=VMEM_BYTES),
        name="rear_gradients",
        cost_estimate=pl.CostEstimate(flops=4_000_000_000, bytes_accessed=16_000_000, transcendentals=0),
    )(lhs, normed_t, low_t, rhs, hidden)


def unpack_kernel(down_at, part, sum_ref, gate_w, fgate_w, fup_w, post_ref,
                  out_ref, gate_ref, fgate_ref, fup_ref, down_ref, dot_ref, post_grad_ref):
    own = out_ref.shape[0]
    n = 0
    for ref in (out_ref, gate_ref, fgate_ref, fup_ref):
        for c in range(ref.shape[1] // 256):
            ref[:, c * 256 : c * 256 + 256] = sum_ref[n * own : n * own + own].astype(f32)
            n += 1
    gap = down_ref.shape[1] * part // 256
    for c in range(256 // part):
        block = sum_ref[down_at * own : down_at * own + gap, c * part : c * part + part].astype(f32)
        down_ref[:, c * gap : c * gap + gap] = block.T

    def row_dot(grad, weight):
        return jnp.sum(grad[...] * weight[...].astype(f32), 1, keepdims=True)

    dot_ref[...] = row_dot(gate_ref, gate_w)
    post_grad_ref[...] = (row_dot(fgate_ref, fgate_w) + row_dot(fup_ref, fup_w)) / post_ref[...].astype(f32)


def unpack_call(packed, gate_w, fgate_w, fup_w, post, ff_own):
    own, width = gate_w.shape
    ff = fgate_w.shape[1]
    shapes = [(own, width), (own, width), (own, ff), (own, ff), (ff_own, width), (own, 1), (own, 1)]
    return pl.pallas_call(
        functools.partial(unpack_kernel, (2 * width + 2 * ff) // 256, ff_own),
        out_shape=[jax.ShapeDtypeStruct(s, f32) for s in shapes],
        compiler_params=pltpu.CompilerParams(vmem_limit_bytes=VMEM_BYTES),
        name="rear_unpack",
        cost_estimate=pl.CostEstimate(flops=1_000_000, bytes_accessed=1_000_000, transcendentals=0),
    )(packed, gate_w, fgate_w, fup_w, post)


def token_kernel(parts_ref, gate_ref, tok_ref, gain_ref, middle_ref, out_ref):
    grad = gate_ref[...]
    for z in range(parts_ref.shape[0]):
        grad = grad + parts_ref[z].astype(f32)
    tok = tok_ref[...].astype(f32)
    scale = lax.rsqrt(jnp.mean(tok * tok, -1, keepdims=True) + EPS)
    out_ref[...] = (middle_ref[...] + rms_back(grad * gain_ref[...], tok, scale)).astype(bf16)


def token_call(parts, gate, tok, gain, middle):
    return pl.pallas_call(
        token_kernel,
        out_shape=jax.ShapeDtypeStruct(tok.shape, bf16),
        compiler_params=pltpu.CompilerParams(vmem_limit_bytes=VMEM_BYTES),
        name="token_gradients",
        cost_estimate=pl.CostEstimate(flops=10_000_000, bytes_accessed=4_000_000, transcendentals=0),
    )(parts, gate, tok, gain, middle)


def front_kernel(layout, piece, tiles, tok_ref, w_ref, normed_ref, slope_ref, send_ref, gains_ref):
    local, order = layout["local"], layout["order"]
    width, packed = w_ref.shape
    extra = local * 192
    eye = lax.broadcasted_iota(jnp.int32, (128, 128), 0) == lax.broadcasted_iota(jnp.int32, (128, 128), 1)

    def to_row(column):
        return jnp.sum(jnp.where(eye, column, 0.0), 0, keepdims=True)

    @pl.when(pl.program_id(0) == 0)
    def _():
        for n in range(2):
            lane = extra + local + n
            for c in range(width // 128):
                column = w_ref[c * 128 : c * 128 + 128, lane : lane + 1].astype(f32)
                gains_ref[n : n + 1, c * 128 : c * 128 + 128] = to_row(column)

    tok = tok_ref[:, 0].reshape(piece, width).astype(f32)
    scale = lax.rsqrt(jnp.mean(tok * tok, -1, keepdims=True) + EPS)
    normed = (tok * scale * gains_ref[0:1]).astype(bf16)
    normed_ref[:, 0] = normed.reshape(normed_ref.shape[0], -1, width)
    projected = nn(normed, w_ref[...])
    sig = 0.5 + 0.5 * jnp.tanh(0.5 * projected[:, extra : extra + local])
    slope = jnp.concatenate([RATE * sig * (1.0 - sig), jnp.zeros((piece, 128 - local), f32)], 1)
    slope_ref[:, 0] = slope.reshape(slope_ref.shape[0], -1, 128)
    rates = (RATE * sig).astype(bf16).astype(f32)
    low = projected.astype(bf16)
    start = 0
    for h, part in enumerate(order):
        for t in range(tiles):
            first, stop = start + t * 128, min(start + t * 128 + 128, packed)
            if first >= packed:
                value = jnp.zeros((piece, 128), bf16)
            else:
                value = low[:, first:stop]
                if stop - first < 128:
                    value = jnp.concatenate([value, jnp.zeros((piece, 128 - stop + first), bf16)], 1)
            send_ref[h, 0, t * piece : t * piece + piece] = value
        start += len(part) * 192
        rows = []
        for j in range(layout["slots"]):
            for i in range(piece // 128):
                if j < len(part):
                    g = part[j]
                    rows.append(to_row(rates[i * 128 : i * 128 + 128, g : g + 1]))
                else:
                    rows.append(jnp.zeros((1, 128), f32))
        rows.append(jnp.zeros((16 - len(rows), 128), f32))
        send_ref[h, 0, tiles * piece : tiles * piece + 16] = cat(*rows).astype(bf16)


def front_call(tokens, weights, layout, piece, tiles):
    Z, micro, rows, width = tokens.shape
    groups = layout["groups"]
    extent = tiles * piece + 16
    step = lambda w: pl.BlockSpec((Z, 1, rows, w), lambda m: (0, m, 0, 0))
    full = lambda s: pl.BlockSpec(s, lambda m: (0,) * len(s), pipeline_mode=pl.Buffered(1))
    S_ = jax.ShapeDtypeStruct
    return pl.pallas_call(
        functools.partial(front_kernel, layout, piece, tiles),
        grid=(micro,),
        in_specs=[step(width), full(weights.shape)],
        out_specs=[step(width), step(128), pl.BlockSpec((groups, 1, extent, 128), lambda m: (0, m, 0, 0)), full((2, width))],
        out_shape=[
            S_((Z, micro, rows, width), bf16), S_((Z, micro, rows, 128), f32),
            S_((groups, micro, extent, 128), bf16), S_((2, width), f32),
        ],
        compiler_params=pltpu.CompilerParams(dimension_semantics=("arbitrary",), vmem_limit_bytes=VMEM_BYTES),
        name="front",
        cost_estimate=pl.CostEstimate(flops=1_000_000_000, bytes_accessed=7_000_000, transcendentals=0),
    )(tokens, weights)


def shards(
    tokens,
    lengths,
    cotangent,
    pre_gain,
    query_weight,
    key_weight,
    value_weight,
    gate_weight,
    rate_weight,
    out_weight,
    post_gain,
    ffn_gate,
    ffn_up,
    ffn_down,
    inner_first,
    inner_first_bias,
    inner_second,
    inner_second_bias,
    inner_gain,
    inner_shift,
):
    micro, _, rows, width = tokens.shape
    local, head, inner = inner_first.shape
    ff = ffn_gate.shape[1]
    Z = lax.axis_size("sp")
    S = lax.axis_size("fsdp")
    z = lax.axis_index("sp")
    d = lax.axis_index("fsdp")
    groups = S // micro
    slots = -(-local // groups)
    order = [[g for g in range(h, local, groups)] for h in range(groups)]
    flat = [g for part in order for g in part]
    span = 3 * head
    tiles = -(-slots * span // 128)
    piece = Z * rows
    length = S * piece
    total = micro * rows
    own = query_weight.shape[0]
    extra = local * span
    packed_width = -(-(extra + local + 2) // 128) * 128

    def columns(weight, count):
        return lax.dynamic_slice_in_dim(weight, z * count, count, 1)

    q_w, k_w, v_w = (
        columns(w, local * head).reshape(own, local, head)
        for w in (query_weight, key_weight, value_weight)
    )
    r_w = columns(rate_weight, local)
    parts = []
    for g in flat:
        parts += [q_w[:, g], k_w[:, g], v_w[:, g]]
    parts += [r_w, pre_gain[:, None], post_gain[:, None]]
    packed = pad_to(jnp.concatenate(parts, 1), packed_width, 1)
    front = gather(packed)
    all_tokens = lax.all_gather(tokens[:, 0], "sp", axis=0)
    rear_in = (out_weight, gate_weight, ffn_gate, ffn_up, ffn_down)
    rear_in, front, all_tokens = lax.optimization_barrier((rear_in, front, all_tokens))
    layout = dict(groups=groups, slots=slots, local=local, micro=micro, order=order, flat=flat)
    normed, rate_slope, send, gains = front_call(all_tokens, front, layout, piece, tiles)
    normed = normed.reshape(Z * total, width)
    pre_full, post_full = gains[:1], gains[1:]
    arrived = swap(send.reshape(S, tiles * piece + 16, 128), "fsdp")

    half = d // micro
    heads_here = [jnp.minimum(half + j * groups, local - 1) for j in range(slots)]

    def of_slots(array_in):
        return jnp.stack([lax.dynamic_index_in_dim(array_in, g, 0, keepdims=False) for g in heads_here])

    w1 = of_slots(inner_first)
    b1 = of_slots(inner_first_bias)[:, None]
    w2 = of_slots(inner_second)
    w2 = (w2 - jnp.mean(w2, -1, keepdims=True)).transpose(0, 2, 1)
    b2 = of_slots(inner_second_bias)[:, None]
    b2 = b2 - jnp.mean(b2, -1, keepdims=True)
    gain = of_slots(inner_gain)[:, None]
    shift = of_slots(inner_shift)[:, None]
    mix, q, k, v, e, *saved = fwd_call(arrived, w1, b1, w2, b2, gain, shift, piece, tiles)
    w1s, w2s, z1, h, q1, n, g_, nq = saved

    out_in, gate_in, fgate_in, fup_in, down_in = rear_in
    rear = gather(jnp.concatenate([out_in, gate_in, fgate_in, fup_in], 1))
    out_full = rear[:, :width]
    gate_full = rear[:, width : 2 * width]
    fgate_full = rear[:, 2 * width : 2 * width + ff]
    fup_full = rear[:, 2 * width + ff :]
    down_full = gather(down_in)

    got = swap(mix.reshape(S * Z, rows, slots * head), ("fsdp", "sp"))
    own_tokens = tokens.reshape(total, width)
    own_normed = lax.dynamic_slice_in_dim(normed, z * total, total, 0)
    gate_act, gate_slope = gelu2(nn(own_normed, gate_full))
    position = d * piece + z * rows + lax.broadcasted_iota(jnp.int32, (micro, rows), 1)
    live = (position < lengths[:, None]).astype(f32).reshape(total, 1)
    grad_low = (cotangent.reshape(total, width).astype(f32) * live).astype(bf16)
    grad_hidden = nt(grad_low, down_full)
    got, gate_act, gate_slope, grad_hidden, normed_t, low_t = lax.optimization_barrier(
        (got, gate_act, gate_slope, grad_hidden, own_normed.T, grad_low.T)
    )
    sent, lhs, rhs, hidden, grad_middle, middle = rear_call(
        layout, got.reshape(S, Z, rows, slots * head), gate_act, gate_slope, own_tokens, rear, post_full,
        grad_hidden, grad_low,
    )
    d_mix = swap(sent.reshape(S * Z, rows, slots * head), ("fsdp", "sp")).reshape(length, slots * head)
    rear_grad = rear_grad_call(lhs, normed_t, low_t, rhs, hidden, S)
    d_mix, rear_grad = lax.optimization_barrier((d_mix, rear_grad))
    packed_rows = rear_grad.shape[1]
    rear_part = lax.psum_scatter(rear_grad.reshape(S * packed_rows, 256), "fsdp", scatter_dimension=0, tiled=True)
    output = (middle + nn(hidden, down_full)).astype(bf16)
    grad_normed_gate = nt(rhs[:, width : 2 * width], gate_full)

    packed_back, dw1, db1, dw2, db2, dgn, dsh = bwd_call(
        q, k, v, e, d_mix, n, g_, nq, w1s, w2s, z1, h, q1, gain, shift, piece, tiles
    )
    packed_back, rear_part = lax.optimization_barrier((packed_back, rear_part))
    rear_sum = lax.psum(rear_part, "sp")
    dw2 = dw2 - jnp.mean(dw2, 1, keepdims=True)
    db2 = db2 - jnp.mean(db2, -1, keepdims=True)
    small = jnp.concatenate([db1[:, 0], db2[:, 0], dgn[:, 0], dsh[:, 0], jnp.zeros((slots, head), f32)], 1)
    inner_rows = jnp.concatenate([dw1, dw2, pad_to(small.reshape(slots, 2, inner), -(-(2 * head + 2) // S) * S - 2 * head, 1)], 1)
    share = inner_rows.shape[1] // S
    inner_send = inner_rows.astype(bf16).reshape(slots, S, share, 2, 128).transpose(1, 0, 3, 2, 4)
    inner_send = inner_send.reshape(S, slots * 2 * share, 128)

    arrived = swap(packed_back, "fsdp")
    grad_packed, normed_parts = back_call(arrived, rate_slope, front, layout, piece, tiles)
    weight_parts = tn(normed, grad_packed.reshape(Z * total, packed_width)).astype(bf16)
    weight_parts = weight_parts.reshape(S, own, packed_width)
    extent = -(-inner_send.shape[1] * 128 // packed_width)
    inner_send = pad_to(inner_send.reshape(S, -1), extent * packed_width, 1).reshape(S, extent, packed_width)
    got = swap(jnp.concatenate([weight_parts, inner_send], 1), "fsdp")
    got, normed_parts, rear_sum = lax.optimization_barrier((got, normed_parts, rear_sum))
    normed_parts = swap(normed_parts.reshape(Z, total, width), "sp")
    got_sum = jnp.sum(got[:, :own].astype(f32), 0).astype(bf16)
    out_grad, gate_grad, fgate_grad, fup_grad, down_grad, gate_dot, post_grad = unpack_call(
        rear_sum, gate_weight, ffn_gate, ffn_up, post_gain[:, None], ff // S
    )
    post_grad = post_grad[:, 0]
    inner_part = got[:, own:].reshape(S, -1)[:, : slots * 2 * share * 128].astype(f32)
    inner_part = jnp.sum(inner_part.reshape(groups, micro, slots, 2, share, 128), 1)
    inner_part = inner_part.transpose(1, 0, 3, 2, 4).reshape(slots * groups, share, 2 * 128)[:local]
    rear_done = (out_grad, gate_grad, fgate_grad, fup_grad, down_grad, post_grad, gate_dot)
    rear_done, got_sum, inner_part = lax.optimization_barrier((rear_done, got_sum, inner_part.astype(bf16)))
    out_grad, gate_grad, fgate_grad, fup_grad, down_grad, post_grad, gate_dot = rear_done
    inner_sum = lax.all_gather(inner_part, "fsdp", axis=1, tiled=True)
    weight_all = lax.all_gather(got_sum, "sp", axis=0)
    inner_sum = inner_sum.astype(f32)
    query_grad, key_grad, value_grad, rate_grad, pre_grad = finish_call(
        weight_all, query_weight, key_weight, value_weight, rate_weight, gate_dot, pre_gain[:, None], layout
    )
    pre_grad = pre_grad[:, 0]
    tokens_grad = token_call(normed_parts, grad_normed_gate, own_tokens, pre_full, grad_middle)
    tail = inner_sum[:, 2 * head : 2 * head + 2].reshape(local, 2 * inner)
    return (
        output.reshape(tokens.shape),
        tokens_grad.reshape(tokens.shape),
        pre_grad,
        query_grad,
        key_grad,
        value_grad,
        gate_grad,
        rate_grad,
        out_grad,
        post_grad,
        fgate_grad,
        fup_grad,
        down_grad,
        inner_sum[:, :head],
        tail[:, :inner],
        inner_sum[:, head : 2 * head].transpose(0, 2, 1),
        tail[:, inner : inner + head],
        tail[:, inner + head : inner + 2 * head],
        tail[:, inner + 2 * head : inner + 3 * head],
    )


def solution(mesh):
    return jax.shard_map(
        shards,
        mesh=mesh,
        in_specs=(
            P(None, "fsdp", "sp", None),
            P(),
            P(None, "fsdp", "sp", None),
            P("fsdp"),
            P("fsdp", None),
            P("fsdp", None),
            P("fsdp", None),
            P("fsdp", None),
            P("fsdp", None),
            P("fsdp", None),
            P("fsdp"),
            P("fsdp", None),
            P("fsdp", None),
            P("fsdp", None),
            P("sp", None, None),
            P("sp", None),
            P("sp", None, None),
            P("sp", None),
            P("sp", None),
            P("sp", None),
        ),
        out_specs=(
            P(None, "fsdp", "sp", None),
            P(None, "fsdp", "sp", None),
            P("fsdp"),
            P("fsdp", None),
            P("fsdp", None),
            P("fsdp", None),
            P("fsdp", None),
            P("fsdp", None),
            P("fsdp", None),
            P("fsdp"),
            P("fsdp", None),
            P("fsdp", None),
            P("fsdp", None),
            P("sp", None, None),
            P("sp", None),
            P("sp", None, None),
            P("sp", None),
            P("sp", None),
            P("sp", None),
        ),
        check_vma=False,
    )
```

```python
import functools

import jax
import jax.numpy as jnp
from jax import lax
from jax.experimental import pallas as pl
from jax.experimental.pallas import tpu as pltpu
from jax.sharding import PartitionSpec as P

MINI = 16
EPS = 1e-06
RATE = 1.0 / 1024.0
GELU_C = 0.7978845608028654
GELU_K = 0.044715
VMEM_BYTES = 58 * 1024 * 1024
f32 = jnp.float32
bf16 = jnp.bfloat16

def nn(x,y): return lax.dot_general(x.astype(bf16),y.astype(bf16),(((1,),(0,)),((),())),preferred_element_type=f32)
def nt(x,y): return lax.dot_general(x.astype(bf16),y.astype(bf16),(((1,),(1,)),((),())),preferred_element_type=f32)
def tn(x,y): return lax.dot_general(x.astype(bf16),y.astype(bf16),(((0,),(0,)),((),())),preferred_element_type=f32)
def gelu1(z):
    t=jnp.tanh(GELU_C*z*(1.0+GELU_K*(z*z)))
    return 0.5*z*(1.0+t)
def gelu2(z):
    z2=z*z
    t=jnp.tanh(z*(GELU_C+(GELU_C*GELU_K)*z2))
    h=0.5+0.5*t
    return z*h, h+0.5*z*(1.0-t*t)*(GELU_C+(3.0*GELU_C*GELU_K)*z2)
def gelu3(z):
    z2=z*z
    t=jnp.tanh(z*(GELU_C+(GELU_C*GELU_K)*z2))
    h=0.5+0.5*t
    u=GELU_C+(3.0*GELU_C*GELU_K)*z2
    c=1.0-t*t
    return z*h, h+0.5*z*c*u, c*(u+z*((3.0*GELU_C*GELU_K)*z-t*u*u))

def cat(*xs): return jnp.concatenate(xs,0)
def rs(x): return jnp.sum(x,-1,keepdims=True)*(1.0/64)

def interleave(gens):
    gens=list(gens)
    while gens:
        alive=[]
        for g in gens:
            try:
                next(g); alive.append(g)
            except StopIteration: pass
        gens=alive

def masks():
    lower=lax.broadcasted_iota(jnp.int32,(MINI,MINI),0)>=lax.broadcasted_iota(jnp.int32,(MINI,MINI),1)
    return lower.astype(f32), jnp.where(lower,0.0,1.0)

def fwd_kernel(slots,count,unroll,piece,tiles,x_ref,w1_ref,b1_ref,w2_ref,b2_ref,gain_ref,shift_ref,
    mix_ref,q_ref,k_ref,v_ref,e_ref,w1s_ref,w2s_ref,z1_ref,h_ref,q1_ref,n_ref,g_ref,nq_ref,
    W1,B1,W2,B2,Z,ZQ,AP,EP):
    lower,upper=masks()
    steps=q_ref.shape[1]//MINI
    pid=pl.program_id(0)
    @pl.when(pid==0)
    def _():
        eye=lax.broadcasted_iota(jnp.int32,(128,128),0)==lax.broadcasted_iota(jnp.int32,(128,128),1)
        @pl.loop(0,x_ref.shape[0])
        def _(src):
            base=pl.multiple_of(src*piece,piece)
            for j in range(slots):
                for index,ref in enumerate((q_ref,k_ref,v_ref)):
                    lane=(3*j+index)*64
                    top=lane//128*piece
                    ref[j,pl.ds(base,piece)]=x_ref[src,top:top+piece,lane%128:lane%128+64]
            rates=x_ref[src,tiles*piece:tiles*piece+16].astype(f32)
            for j in range(slots):
                for i in range(piece//128):
                    n=j*(piece//128)+i
                    column=jnp.sum(jnp.where(eye,rates[n:n+1],0.0),1,keepdims=True)
                    e_ref[j,pl.ds(base+i*128,128)]=jnp.broadcast_to(column,(128,128))
        for j in range(slots):
            W1[j]=w1_ref[j]; B1[j]=b1_ref[j]; W2[j]=w2_ref[j]; B2[j]=b2_ref[j]
            Z[j]=nn(k_ref[j,:MINI],w1_ref[j])+b1_ref[j]
            ZQ[j]=jnp.zeros((MINI,256),f32); AP[j]=jnp.zeros((MINI,256),bf16); EP[j]=jnp.zeros((MINI,64),bf16)
    def chain(j,i):
        t=pid*count+i
        rows=pl.ds(pl.multiple_of(t*MINI,MINI),MINI)
        prow=pl.ds(pl.multiple_of(jnp.maximum(t-1,0)*MINI,MINI),MINI)
        nrow=pl.ds(pl.multiple_of(jnp.minimum(t+1,steps-1)*MINI,MINI),MINI)
        brow=pl.ds(pl.multiple_of(i*MINI,MINI),MINI)
        gain=gain_ref[j]; shift=shift_ref[j]; g2=gain*gain; mg=rs(g2)
        z1=Z[j]; q1=ZQ[j]; w2=W2[j]; b2=B2[j]
        w2b=w2.astype(bf16)
        Ap=AP[j]; Ep=EP[j]
        A,Ad=gelu2(z1); AQ=gelu1(q1)
        Ab=A.astype(bf16); AQb=AQ.astype(bf16)
        z1_ref[j,brow]=z1.astype(bf16)
        yield
        zz=nt(cat(Ab,AQb),w2b)
        z=zz[:MINI]+b2; qb=zz[MINI:]+b2
        yield
        P2=upper*(nt(AQb,Ap)+1.0)
        K=k_ref[j,rows]; Q=q_ref[j,rows]; Kn=k_ref[j,nrow]
        w1=W1[j]; w1b=w1.astype(bf16); b1=B1[j]
        w1s_ref[j,i]=w1b; w2s_ref[j,i]=w2b
        KQ=cat(Kn,Q)
        KK=nt(KQ,K)+1.0
        L=cat(KK[:MINI].astype(bf16),(lower*KK[MINI:]).astype(bf16),K.T)
        base=nn(KQ,w1b)+b1
        U=gain*(shift-v_ref[j,rows].astype(f32)+K.astype(f32)); mU=rs(U)
        e=e_ref[j,rows]; e64=e[:,:64]; e256=jnp.concatenate([e,e],1)
        yield
        Q2=qb+nn(P2,Ep)
        yield
        zg=z*g2
        mz=rs(z); p0=rs(z*z); p1=rs(zg); p2=rs(z*zg); p3=rs(z*U)
        s=lax.rsqrt(p0-mz*mz+EPS)
        m1=s*(p1-mz*mg)+mU
        m2=s*(s*(p2-2.0*mz*p1+mz*mz*mg)+(p3-mz*mU))
        N=s*(z-mz)
        G=s*(N*(g2-m2)+(U-m1))
        Gb=G.astype(bf16)
        yield
        H=nn(Gb,w2b)
        E2=e64*G; E2b=E2.astype(bf16)
        n_ref[j,rows]=(z-mz).astype(bf16); g_ref[j,rows]=Gb
        EP[j]=E2b; AP[j]=Ab
        yield
        W2[j]=w2-tn(E2b,Ab)
        B2[j]=b2-jnp.sum(E2,0,keepdims=True)
        yield
        E1=(e256*Ad)*H; E1b=E1.astype(bf16)
        X=nn(L,E1b)
        Z[j]=base[:MINI]-X[:MINI]
        Q1=base[MINI:]-X[MINI:2*MINI]
        ZQ[j]=Q1
        W1[j]=w1-X[2*MINI:]
        B1[j]=b1-jnp.sum(E1,0,keepdims=True)
        h_ref[j,brow]=H.astype(bf16); q1_ref[j,brow]=Q1.astype(bf16)
        yield
        mq=rs(Q2); vq=rs(Q2*Q2)
        sq=lax.rsqrt(vq-mq*mq+EPS)
        Nq=sq*(Q2-mq)
        Qp=q_ref[j,prow].astype(f32)
        mix_ref[prow,64*j:64*j+64]=(Qp+Nq*gain+shift).astype(bf16)
        nq_ref[j,prow]=(Q2-mq).astype(bf16)
    @pl.loop(0,count//unroll)
    def _(i):
        for u in range(unroll):
            interleave(chain(j,i*unroll+u) for j in range(slots))
    @pl.when(pid==pl.num_programs(0)-1)
    def _():
        for j in range(slots):
            prow=pl.ds((steps-1)*MINI,MINI)
            AQb=gelu1(ZQ[j]).astype(bf16)
            Q2=nt(AQb,W2[j])+B2[j]+nn(upper*(nt(AQb,AP[j])+1.0),EP[j])
            mq=rs(Q2); vq=rs(Q2*Q2)
            sq=lax.rsqrt(vq-mq*mq+EPS)
            Nq=sq*(Q2-mq)
            mix_ref[prow,64*j:64*j+64]=(q_ref[j,prow].astype(f32)+Nq*gain_ref[j]+shift_ref[j]).astype(bf16)
            nq_ref[j,prow]=(Q2-mq).astype(bf16)

def fwd_call(x,w1,b1,w2,b2,gain,shift,piece,tiles,block=256,unroll=2,**kw):
    slots=w1.shape[0]; length=x.shape[0]*piece
    count=block//MINI; nb=length//block; steps=length//MINI
    row=lambda w: pl.BlockSpec((slots,block,w),lambda i:(0,i,0))
    full=lambda s: pl.BlockSpec(s,lambda i:(0,)*len(s),pipeline_mode=pl.Buffered(1))
    r64=full((slots,length,64)); r1=full((slots,length,128)); rm_=full((length,64*slots))
    st=pl.BlockSpec((slots,count,64,256),lambda i:(0,i,0,0))
    S=jax.ShapeDtypeStruct
    return pl.pallas_call(functools.partial(fwd_kernel,slots,count,unroll,piece,tiles),
        grid=(nb,),
        in_specs=[full(a.shape) for a in (x,w1,b1,w2,b2,gain,shift)],
        out_specs=[rm_,r64,r64,r64,r1,st,st,row(256),row(256),row(256),r64,r64,r64],
        out_shape=[S((length,64*slots),bf16)]+[S((slots,length,64),bf16)]*3+[S((slots,length,128),f32)]+[S((slots,steps,64,256),bf16)]*2+[S((slots,length,256),bf16)]*3+[S((slots,length,64),bf16)]*3,
        scratch_shapes=[pltpu.VMEM((slots,64,256),f32),pltpu.VMEM((slots,1,256),f32),pltpu.VMEM((slots,64,256),f32),pltpu.VMEM((slots,1,64),f32),pltpu.VMEM((slots,MINI,256),f32),pltpu.VMEM((slots,MINI,256),f32),pltpu.VMEM((slots,MINI,256),bf16),pltpu.VMEM((slots,MINI,64),bf16)],
        compiler_params=pltpu.CompilerParams(dimension_semantics=("arbitrary",),vmem_limit_bytes=VMEM_BYTES),
        name="inner_forward",cost_estimate=pl.CostEstimate(flops=90_000_000_000,bytes_accessed=40_000_000,transcendentals=0),**kw)(x,w1,b1,w2,b2,gain,shift)


def bwd_kernel(slots,count,unroll,piece,tiles,q_ref,k_ref,v_ref,e_ref,dx_ref,n_ref,g_ref,nq_ref,w1s_ref,w2s_ref,z1_ref,h_ref,q1_ref,gain_ref,shift_ref,
    out_ref,dw1_ref,db1_ref,dw2_ref,db2_ref,dgn_ref,dsh_ref,
    do_ref,de_ref,    DW1,DB1,G2,DB2,KD,DGN,DSH,DGQ,DSQ,
    sA,sAd,sHA,sGZ,sE1,sE2,sW1,sW2,sR1,sR2,sDA,sQ1,sQ2,sAQ,sb1,sb2):
    lower,_=masks()
    steps=q_ref.shape[1]//MINI
    pid=pl.program_id(0); nb=pl.num_programs(0)
    @pl.when(pid==0)
    def _():
        @pl.loop(0,out_ref.shape[0])
        def _(src):
            rows=pl.ds(pl.multiple_of(src*piece,piece),piece)
            for j in range(slots):
                do_ref[j,rows]=dx_ref[rows,64*j:64*j+64]
        for r in (DW1,DB1,G2,DB2,KD,DGN,DSH,DGQ,DSQ):
            r[...]=jnp.zeros(r.shape,r.dtype)
        for r in (sA,sAd,sHA,sGZ,sE1,sE2,sW1,sW2,sR1,sR2,sDA,sQ1,sQ2,sAQ,sb1,sb2):
            r[0]=jnp.zeros(r.shape[1:],r.dtype)
    def put(j,index,t,value):
        t=jnp.minimum(t,steps-1)
        lane=(3*j+index)*64
        top=lane//128*piece
        part=piece//MINI
        rows=pl.ds(pl.multiple_of(top+lax.rem(t,part)*MINI,MINI),MINI)
        out_ref[lax.div(t,part),rows,lane%128:lane%128+64]=value.astype(bf16)
    def crit(j,p,t):
        rows=pl.ds(pl.multiple_of(jnp.minimum(t,steps-1)*MINI,MINI),MINI)
        prow=pl.ds(pl.multiple_of(jnp.maximum(t-1,0)*MINI,MINI),MINI)
        gain=gain_ref[j]; shift=shift_ref[j]; g2=gain*gain; mg=rs(g2)
        e=e_ref[j,rows]; e64=e[:,:64]; e=jnp.concatenate([e,e],1)
        nE1=sR1[p,j]+KD[j]
        dgZ1=(-e)*nE1
        dH=dgZ1*sAd[p,j]
        dHb=dH.astype(bf16)
        w2b=sW2[p,j]
        G2f=G2[j]; G2b=G2f.astype(bf16)
        Ab=sA[p,j]; E2b=sE2[p,j]
        yield
        a1=nt(Ab,G2b)
        yP=nt(dHb,w2b)
        yield
        Zc=n_ref[j,rows].astype(f32); G=g_ref[j,rows].astype(f32)
        s=lax.rsqrt(rs(Zc*Zc)+EPS); N=s*Zc
        K=k_ref[j,rows]; Q=q_ref[j,rows]; Kp=k_ref[j,prow]
        T=shift-v_ref[j,rows].astype(f32)+K.astype(f32)
        U=gain*T
        gN=N*g2
        c1=rs(gN); c2=rs(gN*N); mU=rs(U); UN=rs(U*N)
        a=gN+U; ma=c1+mU; m2=c2+UN
        a2=nn(E2b,G2b)
        E1b=sE1[p,j]; dQ1b=sQ1[p,j]
        DW=DW1[j]; DWb=DW.astype(bf16)
        KDb=nn(Kp,DWb)+DB1[j]
        yield
        a3=nt(E1b,DWb)
        X1=(lower*nt(dQ1b,E1b)).astype(bf16)
        L2=cat((nt(Kp,cat(Q,K))+1.0).astype(bf16),cat(Q,K).T)
        yield
        nE2=sR2[p,j]+a1+DB2[j]
        y=yP-e64*nE2
        yg=y*g2; yn=y*N
        ym=rs(y); yN=rs(yn); yG=rs(y*G); ygm=rs(yg); ygN=rs(yg*N)
        mdy=s*ym; mdyN=s*yN
        da=s*y-mdy-N*mdyN
        sN=s*ygN-mdy*c1-mdyN*c2-2.0*m2*mdyN
        mN=s*ygm-mdy*mg-mdyN*c1-ma*mdyN-m2*mdy
        kap=yG+sN
        dN=da*g2-a*mdyN-(s*m2)*y
        dZc=s*(dN-mN-N*kap)
        dZb=dZc.astype(bf16)
        dT=da*gain
        yield
        dA=nn(dZb,w2b)+sDA[p,j]-a2
        yield
        G2[j]=G2f+tn(cat(sQ2[p,j],g_ref[j,rows],dZb),cat(sAQ[p,j],dHb,Ab))
        DB2[j]=DB2[j]+sb2[p,j]+jnp.sum(dZc,0,keepdims=True)
        dQs=nn(X1,K); dKs=tn(X1,Q)
        put(j,2,t,-dT)
        dO=do_ref[j,rows].astype(f32)
        DGN[j]=DGN[j]+da*(2.0*gain*N+T)
        DSH[j]=DSH[j]+dT
        de_ref[j,rows]=-(jnp.sum(nE1*sGZ[p,j],-1,keepdims=True)+jnp.sum(nE2*G,-1,keepdims=True))
        yield
        dZ1=dA*sAd[p,j]+dgZ1*sHA[p,j]
        dZ1b=dZ1.astype(bf16)
        dd=cat(dQ1b,dZ1b)
        X=nn(L2,dd)
        KD[j]=KDb+X[:MINI]
        DW1[j]=DW+X[MINI:]
        DB1[j]=DB1[j]+sb1[p,j]+jnp.sum(dZ1,0,keepdims=True)
        yield
        qk=nt(dd,sW1[p,j])
        put(j,0,t,dO+qk[:MINI]-dQs)
        put(j,1,t,qk[MINI:]-dKs-a3+dT)
    def qside(j,p,t,i):
        rows=pl.ds(pl.multiple_of(t*MINI,MINI),MINI)
        brow=pl.ds(pl.multiple_of(i*MINI,MINI),MINI)
        gain=gain_ref[j]
        dO=do_ref[j,rows].astype(f32); Qc=nq_ref[j,rows].astype(f32)
        sq=lax.rsqrt(rs(Qc*Qc)+EPS); Nq=sq*Qc
        dNq=dO*gain
        dQ2=sq*(dNq-rs(dNq)-Nq*rs(dNq*Nq))
        dQ2b=dQ2.astype(bf16)
        A,Ad,Add=gelu3(z1_ref[j,brow].astype(f32))
        AQ,AQd=gelu2(q1_ref[j,brow].astype(f32))
        H=h_ref[j,brow].astype(f32); e=e_ref[j,rows]; e64=e[:,:64]; e=jnp.concatenate([e,e],1)
        Ab=A.astype(bf16); AQb=AQ.astype(bf16)
        gZ1=H*Ad
        E1b=(e*gZ1).astype(bf16); E2b=(e64*g_ref[j,rows].astype(f32)).astype(bf16)
        w1b=w1s_ref[j,i]; w2b=w2s_ref[j,i]
        yield
        sA[p,j]=Ab; sAd[p,j]=Ad; sHA[p,j]=H*Add; sGZ[p,j]=gZ1; sE1[p,j]=E1b; sE2[p,j]=E2b; sW1[p,j]=w1b; sW2[p,j]=w2b; sAQ[p,j]=AQb
        sQ2[p,j]=dQ2b; sb2[p,j]=jnp.sum(dQ2,0,keepdims=True)
        DGQ[j]=DGQ[j]+dO*Nq; DSQ[j]=DSQ[j]+dO
        Q=q_ref[j,rows]; K=k_ref[j,rows]
        P1=(lower*(nt(Q,K)+1.0)).astype(bf16)
        P2=(lower*(nt(AQb,Ab)+1.0)).astype(bf16)
        yield
        X2=(lower*nt(dQ2b,E2b)).astype(bf16)
        yield
        b1=nn(dQ2b,w2b)
        yield
        sR2[p,j]=tn(P2,dQ2b)
        yield
        dAQ=b1-nn(X2,Ab)
        sDA[p,j]=-tn(X2,AQb)
        yield
        yield
        dQ1=dAQ*AQd
        dQ1b=dQ1.astype(bf16)
        sQ1[p,j]=dQ1b; sb1[p,j]=jnp.sum(dQ1,0,keepdims=True)
        sR1[p,j]=tn(P1,dQ1b)
    @pl.loop(0,count//unroll)
    def _(i):
        for u in range(unroll):
            ii=count-1-(i*unroll+u)
            t=(nb-1-pid)*count+ii
            interleave([crit(j,u%2,t+1) for j in range(slots)]+[qside(j,(u+1)%2,t,ii) for j in range(slots)])
    @pl.when(pid==nb-1)
    def _():
        interleave([crit(j,0,jnp.int32(0)) for j in range(slots)])
        eye=lax.broadcasted_iota(jnp.int32,(128,128),0)==lax.broadcasted_iota(jnp.int32,(128,128),1)
        @pl.loop(0,out_ref.shape[0])
        def _(dst):
            base=pl.multiple_of(dst*piece,piece)
            rows=[jnp.sum(jnp.where(eye,de_ref[j,pl.ds(base+i*128,128)],0.0),0,keepdims=True) for j in range(slots) for i in range(piece//128)]
            rows.append(jnp.zeros((16-len(rows),128),f32))
            out_ref[dst,tiles*piece:tiles*piece+16]=cat(*rows).astype(bf16)
            if tiles*128>slots*192:
                out_ref[dst,(tiles-1)*piece:tiles*piece,(slots*192)%128:]=jnp.zeros((piece,128-(slots*192)%128),bf16)
        for j in range(slots):
            dw1_ref[j]=DW1[j]; db1_ref[j]=DB1[j]; dw2_ref[j]=G2[j]; db2_ref[j]=DB2[j]
            dgn_ref[j]=jnp.sum(DGN[j]+DGQ[j],0,keepdims=True); dsh_ref[j]=jnp.sum(DSH[j]+DSQ[j],0,keepdims=True)

def bwd_call(q,k,v,e,dO,n,g,nq,w1s,w2s,z1,h,q1,gain,shift,piece,tiles,block=256,unroll=2,**kw):
    slots,length,_=q.shape
    count=block//MINI; nb=length//block; steps=length//MINI
    row=lambda w: pl.BlockSpec((slots,block,w),lambda i:(0,nb-1-i,0))
    full=lambda s: pl.BlockSpec(s,lambda i:(0,)*len(s),pipeline_mode=pl.Buffered(1))
    r64=full((slots,length,64)); r1=full((slots,length,128))
    st=pl.BlockSpec((slots,count,64,256),lambda i:(0,nb-1-i,0,0))
    S=jax.ShapeDtypeStruct
    outs=[((length//piece,tiles*piece+16,128),bf16),((slots,64,256),f32),((slots,1,256),f32),((slots,64,256),f32),((slots,1,64),f32),((slots,1,64),f32),((slots,1,64),f32)]
    V=lambda *s,d=f32: pltpu.VMEM(s,d)
    return pl.pallas_call(functools.partial(bwd_kernel,slots,count,unroll,piece,tiles),
        grid=(nb,),
        in_specs=[r64]*3+[r1,full(dO.shape)]+[r64]*3+[st,st]+[row(256)]*3+[full(gain.shape)]*2,
        out_specs=[full(o[0]) for o in outs],
        out_shape=[S(*o) for o in outs],
        scratch_shapes=[V(slots,length,64,d=bf16),V(slots,length,1),V(slots,64,256),V(slots,1,256),V(slots,64,256),V(slots,1,64),V(slots,MINI,256),V(slots,MINI,64),V(slots,MINI,64),V(slots,MINI,64),V(slots,MINI,64),
          V(2,slots,MINI,256,d=bf16),V(2,slots,MINI,256),V(2,slots,MINI,256),V(2,slots,MINI,256),V(2,slots,MINI,256,d=bf16),V(2,slots,MINI,64,d=bf16),
          V(2,slots,64,256,d=bf16),V(2,slots,64,256,d=bf16),V(2,slots,MINI,256),V(2,slots,MINI,64),V(2,slots,MINI,256),V(2,slots,MINI,256,d=bf16),V(2,slots,MINI,64,d=bf16),V(2,slots,MINI,256,d=bf16),V(2,slots,1,256),V(2,slots,1,64)],
        compiler_params=pltpu.CompilerParams(dimension_semantics=("arbitrary",),vmem_limit_bytes=VMEM_BYTES),
        name="inner_backward",cost_estimate=pl.CostEstimate(flops=110_000_000_000,bytes_accessed=40_000_000,transcendentals=0),**kw)(q,k,v,e,dO,n,g,nq,w1s,w2s,z1,h,q1,gain,shift)


def rms_back(grad_scaled, inputs, scale):
    return scale * (
        grad_scaled - inputs * scale * scale * jnp.mean(grad_scaled * inputs, -1, keepdims=True)
    )


def gather(block):
    return lax.all_gather(block, "fsdp", axis=0, tiled=True)


def swap(block, axes):
    return lax.all_to_all(block, axes, split_axis=0, concat_axis=0, tiled=True)


def pad_to(array_in, size, dim):
    widths = [(0, 0)] * array_in.ndim
    widths[dim] = (0, size - array_in.shape[dim])
    return jnp.pad(array_in, widths)


def back_kernel(layout, piece, tiles, a_ref, slope_ref, front_ref, grad_ref, parts_ref):
    micro_step = pl.program_id(0)
    groups, slots, local, micro = layout["groups"], layout["slots"], layout["local"], layout["micro"]
    eye = lax.broadcasted_iota(jnp.int32, (128, 128), 0) == lax.broadcasted_iota(jnp.int32, (128, 128), 1)
    lanes = lax.broadcasted_iota(jnp.int32, (piece, 64), 1)
    rates = jnp.zeros((piece, 64), f32)
    for h, part in enumerate(layout["order"]):
        block = a_ref[h * micro + micro_step, tiles * piece : tiles * piece + 16].astype(f32)
        for j, g in enumerate(part):
            column = []
            for i in range(piece // 128):
                n = j * (piece // 128) + i
                column.append(jnp.sum(jnp.where(eye, block[n : n + 1], 0.0), 1, keepdims=True))
            rates = jnp.where(lanes == g, cat(*column), rates)
    slope = slope_ref[:, 0].reshape(piece, slope_ref.shape[-1])
    rates = rates * slope[:, :64]
    halves = []
    for h, part in enumerate(layout["order"]):
        for lane in range(0, len(part) * 192, 64):
            halves.append((h, lane))
    halves.append(None)
    chunks = []
    for n in range(0, len(halves), 2):
        pair = halves[n : n + 2]
        if pair[0] is not None and len(pair) == 2 and pair[1] is not None:
            (h, lane), (h2, lane2) = pair
            if h == h2 and lane % 128 == 0:
                top = lane // 128 * piece
                chunks.append(a_ref[h * micro + micro_step, top : top + piece])
                continue
        values = []
        for half in pair:
            if half is None:
                values.append(rates.astype(bf16))
            else:
                h, lane = half
                top = lane // 128 * piece
                values.append(a_ref[h * micro + micro_step, top : top + piece, lane % 128 : lane % 128 + 64])
        if len(values) == 1:
            values.append(jnp.zeros((piece, 64), bf16))
        chunks.append(jnp.concatenate(values, 1))
    grad = jnp.concatenate(chunks, 1)
    product = nt(grad, front_ref[...]).astype(bf16)
    rows = piece // grad_ref.shape[0]
    grad_ref[:, 0] = grad.reshape(grad_ref.shape[0], rows, grad.shape[1])
    parts_ref[:, 0] = product.reshape(parts_ref.shape[0], rows, product.shape[1])


def back_call(arrived, slope, front, layout, piece, tiles):
    Z, micro, rows, _ = slope.shape
    width = front.shape[0]
    packed = front.shape[1]
    full = lambda s: pl.BlockSpec(s, lambda i: (0,) * len(s), pipeline_mode=pl.Buffered(1))
    step = lambda w: pl.BlockSpec((Z, 1, rows, w), lambda i: (0, i, 0, 0))
    return pl.pallas_call(
        functools.partial(back_kernel, layout, piece, tiles),
        grid=(micro,),
        in_specs=[full(arrived.shape), step(slope.shape[-1]), full(front.shape)],
        out_specs=[step(packed), step(width)],
        out_shape=[
            jax.ShapeDtypeStruct((Z, micro, rows, packed), bf16),
            jax.ShapeDtypeStruct((Z, micro, rows, width), bf16),
        ],
        compiler_params=pltpu.CompilerParams(dimension_semantics=("arbitrary",), vmem_limit_bytes=VMEM_BYTES),
        name="projection_gradients",
        cost_estimate=pl.CostEstimate(flops=1_000_000_000, bytes_accessed=8_000_000, transcendentals=0),
    )(arrived, slope, front)


def finish_kernel(layout, all_ref, q_ref, k_ref, v_ref, r_ref, gate_ref, pre_ref, dq_ref, dk_ref, dv_ref, dr_ref, dot_ref):
    local = layout["local"]
    flat = layout["flat"]
    Z = all_ref.shape[0]
    own = dq_ref.shape[0]
    dot = jnp.zeros((own, 1), f32)
    rate = jnp.zeros((own, dr_ref.shape[1]), f32)
    lanes = lax.broadcasted_iota(jnp.int32, rate.shape, 1)
    for index, (weight, out) in enumerate(((q_ref, dq_ref), (k_ref, dk_ref), (v_ref, dv_ref))):
        for z in range(Z):
            for g in range(local):
                start = (flat.index(g) * 3 + index) * 64
                value = all_ref[z, :, start : start + 64].astype(f32)
                place = (z * local + g) * 64
                out[:, place : place + 64] = value
        dot = dot + jnp.sum(out[...] * weight[...].astype(f32), 1, keepdims=True)
    for z in range(Z):
        for g in range(local):
            n = local * 192 + g
            rate = jnp.where(lanes == z * local + g, all_ref[z, :, n : n + 1].astype(f32), rate)
    dr_ref[...] = rate
    dot = dot + jnp.sum(rate * r_ref[...].astype(f32), 1, keepdims=True) + gate_ref[...]
    dot_ref[...] = dot / pre_ref[...].astype(f32)


def finish_call(gathered, q_w, k_w, v_w, r_w, gate_dot, pre, layout):
    own, width = q_w.shape
    Z = gathered.shape[0]
    shapes = [(own, width)] * 3 + [(own, Z * layout["local"]), (own, 1)]
    return pl.pallas_call(
        functools.partial(finish_kernel, layout),
        out_shape=[jax.ShapeDtypeStruct(s, f32) for s in shapes],
        compiler_params=pltpu.CompilerParams(vmem_limit_bytes=VMEM_BYTES),
        name="weight_gradients",
        cost_estimate=pl.CostEstimate(flops=10_000_000, bytes_accessed=2_000_000, transcendentals=0),
    )(gathered, q_w, k_w, v_w, r_w, gate_dot, pre)


def rear_kernel(layout, got_ref, act_ref, slope_ref, tok_ref, w_ref, post_ref, gh_ref, go_ref,
                send_ref, lhs_ref, rhs_ref, hid_ref, gm_ref, mid_ref):
    groups, slots, local, micro = layout["groups"], layout["slots"], layout["local"], layout["micro"]
    Z, rows = got_ref.shape[1], got_ref.shape[2]
    total, width = act_ref.shape
    ff = hid_ref.shape[1]
    blocks = []
    for m in range(micro):
        pieces = []
        for z in range(Z):
            for g in range(local):
                h, j = g % groups, g // groups
                pieces.append(got_ref[h * micro + m, z, :, 64 * j : 64 * j + 64])
        blocks.append(jnp.concatenate(pieces, 1))
    mixed = cat(*blocks).astype(f32)
    gated = (act_ref[...] * mixed).astype(bf16)
    lhs_ref[0] = gated.T
    middle = tok_ref[...].astype(f32) + nn(gated, w_ref[:, :width])
    mid_ref[...] = middle
    scale = lax.rsqrt(jnp.mean(middle * middle, -1, keepdims=True) + EPS)
    post = post_ref[...]
    low = (middle * scale * post).astype(bf16)
    lhs_ref[1] = low.T
    gm_ref[...] = jnp.zeros((total, width), f32)
    step = 256

    @pl.loop(0, ff // step)
    def _(c):
        here = pl.ds(pl.multiple_of(c * step, step), step)
        gate_at = pl.ds(pl.multiple_of(2 * width + c * step, step), step)
        up_at = pl.ds(pl.multiple_of(2 * width + ff + c * step, step), step)
        gate_w, up_w = w_ref[:, gate_at], w_ref[:, up_at]
        gate_pre, up_pre = nn(low, gate_w), nn(low, up_w)
        sig = 0.5 + 0.5 * jnp.tanh(0.5 * gate_pre)
        silu = gate_pre * sig
        hid_ref[:, here] = (silu * up_pre).astype(bf16)
        grad = gh_ref[:, here]
        g_gate = (grad * up_pre * sig * (1.0 + gate_pre * (1.0 - sig))).astype(bf16)
        g_up = (grad * silu).astype(bf16)
        rhs_ref[:, gate_at] = g_gate
        rhs_ref[:, up_at] = g_up
        gm_ref[...] += nt(g_gate, gate_w) + nt(g_up, up_w)

    middle = mid_ref[...]
    grad_middle = go_ref[...].astype(f32) + rms_back(gm_ref[...] * post, middle, scale)
    gm_ref[...] = grad_middle
    branch = grad_middle.astype(bf16)
    rhs_ref[:, :width] = branch
    grad_gated = nt(branch, w_ref[:, :width])
    grad_mixed = (grad_gated * act_ref[...]).astype(bf16)
    rhs_ref[:, width : 2 * width] = (grad_gated * mixed * slope_ref[...]).astype(bf16)
    for m in range(micro):
        for z in range(Z):
            for h in range(groups):
                for j in range(slots):
                    g = h + j * groups
                    if g < local:
                        lane = (z * local + g) * 64
                        value = grad_mixed[m * rows : m * rows + rows, lane : lane + 64]
                    else:
                        value = jnp.zeros((rows, 64), bf16)
                    send_ref[h * micro + m, z, :, 64 * j : 64 * j + 64] = value


def rear_call(layout, got, act, slope, tok, weights, post, grad_hidden, grad_low):
    total, width = act.shape
    ff = grad_hidden.shape[1]
    S_ = jax.ShapeDtypeStruct
    return pl.pallas_call(
        functools.partial(rear_kernel, layout),
        out_shape=[
            S_(got.shape, bf16), S_((2, width, total), bf16), S_((total, weights.shape[1]), bf16),
            S_((total, ff), bf16), S_((total, width), f32), S_((total, width), f32),
        ],
        compiler_params=pltpu.CompilerParams(vmem_limit_bytes=VMEM_BYTES),
        name="rear",
        cost_estimate=pl.CostEstimate(flops=5_000_000_000, bytes_accessed=16_000_000, transcendentals=0),
    )(got, act, slope, tok, weights, post, grad_hidden, grad_low)


def rear_grad_kernel(starts, per_step, lhs_ref, normed_ref, low_ref, rhs_ref, hid_ref, out_ref):
    S = out_ref.shape[0]
    own = out_ref.shape[1] // per_step
    gate_at, ffn_at, down_at = starts

    def block(n, top):
        here = pl.ds(top * own, own)

        def write(left):
            right = rhs_ref[:, pl.ds(pl.multiple_of(n * 256, 256), 256)]
            out_ref[:, here] = nn(left, right).astype(bf16).reshape(S, own, 256)

        @pl.when(n < gate_at)
        def _():
            write(lhs_ref[0])

        @pl.when((n >= gate_at) & (n < ffn_at))
        def _():
            write(normed_ref[...])

        @pl.when((n >= ffn_at) & (n < down_at))
        def _():
            write(lhs_ref[1])

        @pl.when(n >= down_at)
        def _():
            i = n - down_at
            part = hid_ref.shape[1] // S
            k = 256 // part
            gap = low_ref.shape[0] // k
            left = [low_ref[pl.ds(pl.multiple_of(c * gap + i * own, 8), own)] for c in range(k)]
            product = nn(cat(*left), hid_ref[...]).astype(bf16)
            for d in range(S):
                parts = [product[c * own : c * own + own, part * d : part * d + part] for c in range(k)]
                out_ref[d, here] = parts[0] if k == 1 else jnp.concatenate(parts, 1)

    for u in range(per_step):
        block(pl.program_id(0) * per_step + u, u)


def rear_grad_call(lhs, normed_t, low_t, rhs, hidden, S):
    _, width, total = lhs.shape
    own = width // S
    starts = (width // 256, 2 * width // 256, rhs.shape[1] // 256)
    blocks = starts[2] + width * hidden.shape[1] // S // 256 // own
    per_step = 2 - blocks % 2
    full = lambda a: pl.BlockSpec(a.shape, lambda n: (0,) * a.ndim, pipeline_mode=pl.Buffered(1))
    return pl.pallas_call(
        functools.partial(rear_grad_kernel, starts, per_step),
        grid=(blocks // per_step,),
        in_specs=[full(a) for a in (lhs, normed_t, low_t, rhs, hidden)],
        out_specs=pl.BlockSpec((S, per_step * own, 256), lambda n: (0, n, 0)),
        out_shape=jax.ShapeDtypeStruct((S, blocks * own, 256), bf16),
        compiler_params=pltpu.CompilerParams(dimension_semantics=("arbitrary",), vmem_limit_bytes=VMEM_BYTES),
        name="rear_gradients",
        cost_estimate=pl.CostEstimate(flops=4_000_000_000, bytes_accessed=16_000_000, transcendentals=0),
    )(lhs, normed_t, low_t, rhs, hidden)


def unpack_kernel(down_at, part, sum_ref, gate_w, fgate_w, fup_w, post_ref,
                  out_ref, gate_ref, fgate_ref, fup_ref, down_ref, dot_ref, post_grad_ref):
    own = out_ref.shape[0]
    n = 0
    for ref in (out_ref, gate_ref, fgate_ref, fup_ref):
        for c in range(ref.shape[1] // 256):
            ref[:, c * 256 : c * 256 + 256] = sum_ref[n * own : n * own + own].astype(f32)
            n += 1
    gap = down_ref.shape[1] * part // 256
    for c in range(256 // part):
        block = sum_ref[down_at * own : down_at * own + gap, c * part : c * part + part].astype(f32)
        down_ref[:, c * gap : c * gap + gap] = block.T

    def row_dot(grad, weight):
        return jnp.sum(grad[...] * weight[...].astype(f32), 1, keepdims=True)

    dot_ref[...] = row_dot(gate_ref, gate_w)
    post_grad_ref[...] = (row_dot(fgate_ref, fgate_w) + row_dot(fup_ref, fup_w)) / post_ref[...].astype(f32)


def unpack_call(packed, gate_w, fgate_w, fup_w, post, ff_own):
    own, width = gate_w.shape
    ff = fgate_w.shape[1]
    shapes = [(own, width), (own, width), (own, ff), (own, ff), (ff_own, width), (own, 1), (own, 1)]
    return pl.pallas_call(
        functools.partial(unpack_kernel, (2 * width + 2 * ff) // 256, ff_own),
        out_shape=[jax.ShapeDtypeStruct(s, f32) for s in shapes],
        compiler_params=pltpu.CompilerParams(vmem_limit_bytes=VMEM_BYTES),
        name="rear_unpack",
        cost_estimate=pl.CostEstimate(flops=1_000_000, bytes_accessed=1_000_000, transcendentals=0),
    )(packed, gate_w, fgate_w, fup_w, post)


def token_kernel(parts_ref, gate_ref, tok_ref, gain_ref, middle_ref, out_ref):
    grad = gate_ref[...]
    for z in range(parts_ref.shape[0]):
        grad = grad + parts_ref[z].astype(f32)
    tok = tok_ref[...].astype(f32)
    scale = lax.rsqrt(jnp.mean(tok * tok, -1, keepdims=True) + EPS)
    out_ref[...] = (middle_ref[...] + rms_back(grad * gain_ref[...], tok, scale)).astype(bf16)


def token_call(parts, gate, tok, gain, middle):
    return pl.pallas_call(
        token_kernel,
        out_shape=jax.ShapeDtypeStruct(tok.shape, bf16),
        compiler_params=pltpu.CompilerParams(vmem_limit_bytes=VMEM_BYTES),
        name="token_gradients",
        cost_estimate=pl.CostEstimate(flops=10_000_000, bytes_accessed=4_000_000, transcendentals=0),
    )(parts, gate, tok, gain, middle)


def front_kernel(layout, piece, tiles, tok_ref, w_ref, normed_ref, slope_ref, send_ref, gains_ref):
    local, order = layout["local"], layout["order"]
    width, packed = w_ref.shape
    extra = local * 192
    eye = lax.broadcasted_iota(jnp.int32, (128, 128), 0) == lax.broadcasted_iota(jnp.int32, (128, 128), 1)

    def to_row(column):
        return jnp.sum(jnp.where(eye, column, 0.0), 0, keepdims=True)

    @pl.when(pl.program_id(0) == 0)
    def _():
        for n in range(2):
            lane = extra + local + n
            for c in range(width // 128):
                column = w_ref[c * 128 : c * 128 + 128, lane : lane + 1].astype(f32)
                gains_ref[n : n + 1, c * 128 : c * 128 + 128] = to_row(column)

    tok = tok_ref[:, 0].reshape(piece, width).astype(f32)
    scale = lax.rsqrt(jnp.mean(tok * tok, -1, keepdims=True) + EPS)
    normed = (tok * scale * gains_ref[0:1]).astype(bf16)
    normed_ref[:, 0] = normed.reshape(normed_ref.shape[0], -1, width)
    projected = nn(normed, w_ref[...])
    sig = 0.5 + 0.5 * jnp.tanh(0.5 * projected[:, extra : extra + local])
    slope = jnp.concatenate([RATE * sig * (1.0 - sig), jnp.zeros((piece, 128 - local), f32)], 1)
    slope_ref[:, 0] = slope.reshape(slope_ref.shape[0], -1, 128)
    rates = (RATE * sig).astype(bf16).astype(f32)
    low = projected.astype(bf16)
    start = 0
    for h, part in enumerate(order):
        for t in range(tiles):
            first, stop = start + t * 128, min(start + t * 128 + 128, packed)
            if first >= packed:
                value = jnp.zeros((piece, 128), bf16)
            else:
                value = low[:, first:stop]
                if stop - first < 128:
                    value = jnp.concatenate([value, jnp.zeros((piece, 128 - stop + first), bf16)], 1)
            send_ref[h, 0, t * piece : t * piece + piece] = value
        start += len(part) * 192
        rows = []
        for j in range(layout["slots"]):
            for i in range(piece // 128):
                if j < len(part):
                    g = part[j]
                    rows.append(to_row(rates[i * 128 : i * 128 + 128, g : g + 1]))
                else:
                    rows.append(jnp.zeros((1, 128), f32))
        rows.append(jnp.zeros((16 - len(rows), 128), f32))
        send_ref[h, 0, tiles * piece : tiles * piece + 16] = cat(*rows).astype(bf16)


def front_call(tokens, weights, layout, piece, tiles):
    Z, micro, rows, width = tokens.shape
    groups = layout["groups"]
    extent = tiles * piece + 16
    step = lambda w: pl.BlockSpec((Z, 1, rows, w), lambda m: (0, m, 0, 0))
    full = lambda s: pl.BlockSpec(s, lambda m: (0,) * len(s), pipeline_mode=pl.Buffered(1))
    S_ = jax.ShapeDtypeStruct
    return pl.pallas_call(
        functools.partial(front_kernel, layout, piece, tiles),
        grid=(micro,),
        in_specs=[step(width), full(weights.shape)],
        out_specs=[step(width), step(128), pl.BlockSpec((groups, 1, extent, 128), lambda m: (0, m, 0, 0)), full((2, width))],
        out_shape=[
            S_((Z, micro, rows, width), bf16), S_((Z, micro, rows, 128), f32),
            S_((groups, micro, extent, 128), bf16), S_((2, width), f32),
        ],
        compiler_params=pltpu.CompilerParams(dimension_semantics=("arbitrary",), vmem_limit_bytes=VMEM_BYTES),
        name="front",
        cost_estimate=pl.CostEstimate(flops=1_000_000_000, bytes_accessed=7_000_000, transcendentals=0),
    )(tokens, weights)


def shards(
    tokens,
    lengths,
    cotangent,
    pre_gain,
    query_weight,
    key_weight,
    value_weight,
    gate_weight,
    rate_weight,
    out_weight,
    post_gain,
    ffn_gate,
    ffn_up,
    ffn_down,
    inner_first,
    inner_first_bias,
    inner_second,
    inner_second_bias,
    inner_gain,
    inner_shift,
):
    micro, _, rows, width = tokens.shape
    local, head, inner = inner_first.shape
    ff = ffn_gate.shape[1]
    Z = lax.axis_size("sp")
    S = lax.axis_size("fsdp")
    z = lax.axis_index("sp")
    d = lax.axis_index("fsdp")
    groups = S // micro
    slots = -(-local // groups)
    order = [[g for g in range(h, local, groups)] for h in range(groups)]
    flat = [g for part in order for g in part]
    span = 3 * head
    tiles = -(-slots * span // 128)
    piece = Z * rows
    length = S * piece
    total = micro * rows
    own = query_weight.shape[0]
    extra = local * span
    packed_width = -(-(extra + local + 2) // 128) * 128

    def columns(weight, count):
        return lax.dynamic_slice_in_dim(weight, z * count, count, 1)

    q_w, k_w, v_w = (
        columns(w, local * head).reshape(own, local, head)
        for w in (query_weight, key_weight, value_weight)
    )
    r_w = columns(rate_weight, local)
    parts = []
    for g in flat:
        parts += [q_w[:, g], k_w[:, g], v_w[:, g]]
    parts += [r_w, pre_gain[:, None], post_gain[:, None]]
    packed = pad_to(jnp.concatenate(parts, 1), packed_width, 1)
    front = gather(packed)
    all_tokens = lax.all_gather(tokens[:, 0], "sp", axis=0)
    rear_in = (jnp.concatenate([out_weight, gate_weight, ffn_gate, ffn_up], 1), ffn_down)
    rear_in, front, all_tokens = lax.optimization_barrier((rear_in, front, all_tokens))
    layout = dict(groups=groups, slots=slots, local=local, micro=micro, order=order, flat=flat)
    normed, rate_slope, send, gains = front_call(all_tokens, front, layout, piece, tiles)
    normed = normed.reshape(Z * total, width)
    pre_full, post_full = gains[:1], gains[1:]
    arrived = swap(send.reshape(S, tiles * piece + 16, 128), "fsdp")

    half = d // micro
    heads_here = [jnp.minimum(half + j * groups, local - 1) for j in range(slots)]

    def of_slots(array_in):
        return jnp.stack([lax.dynamic_index_in_dim(array_in, g, 0, keepdims=False) for g in heads_here])

    w1 = of_slots(inner_first)
    b1 = of_slots(inner_first_bias)[:, None]
    w2 = of_slots(inner_second)
    w2 = (w2 - jnp.mean(w2, -1, keepdims=True)).transpose(0, 2, 1)
    b2 = of_slots(inner_second_bias)[:, None]
    b2 = b2 - jnp.mean(b2, -1, keepdims=True)
    gain = of_slots(inner_gain)[:, None]
    shift = of_slots(inner_shift)[:, None]
    mix, q, k, v, e, *saved = fwd_call(arrived, w1, b1, w2, b2, gain, shift, piece, tiles)
    w1s, w2s, z1, h, q1, n, g_, nq = saved

    rear_own, down_in = rear_in
    rear = gather(rear_own)
    out_full = rear[:, :width]
    gate_full = rear[:, width : 2 * width]
    fgate_full = rear[:, 2 * width : 2 * width + ff]
    fup_full = rear[:, 2 * width + ff :]
    down_full = gather(down_in)

    got = swap(mix.reshape(S * Z, rows, slots * head), ("fsdp", "sp"))
    own_tokens = tokens.reshape(total, width)
    own_normed = lax.dynamic_slice_in_dim(normed, z * total, total, 0)
    gate_act, gate_slope = gelu2(nn(own_normed, gate_full))
    position = d * piece + z * rows + lax.broadcasted_iota(jnp.int32, (micro, rows), 1)
    live = (position < lengths[:, None]).astype(f32).reshape(total, 1)
    grad_low = (cotangent.reshape(total, width).astype(f32) * live).astype(bf16)
    grad_hidden = nt(grad_low, down_full)
    got, gate_act, gate_slope, grad_hidden, normed_t, low_t = lax.optimization_barrier(
        (got, gate_act, gate_slope, grad_hidden, own_normed.T, grad_low.T)
    )
    sent, lhs, rhs, hidden, grad_middle, middle = rear_call(
        layout, got.reshape(S, Z, rows, slots * head), gate_act, gate_slope, own_tokens, rear, post_full,
        grad_hidden, grad_low,
    )
    d_mix = swap(sent.reshape(S * Z, rows, slots * head), ("fsdp", "sp")).reshape(length, slots * head)
    rear_grad = rear_grad_call(lhs, normed_t, low_t, rhs, hidden, S)
    d_mix, rear_grad = lax.optimization_barrier((d_mix, rear_grad))
    packed_rows = rear_grad.shape[1]
    rear_part = lax.psum_scatter(rear_grad.reshape(S * packed_rows, 256), "fsdp", scatter_dimension=0, tiled=True)
    output = (middle + nn(hidden, down_full)).astype(bf16)
    grad_normed_gate = nt(rhs[:, width : 2 * width], gate_full)

    packed_back, dw1, db1, dw2, db2, dgn, dsh = bwd_call(
        q, k, v, e, d_mix, n, g_, nq, w1s, w2s, z1, h, q1, gain, shift, piece, tiles
    )
    packed_back, rear_part = lax.optimization_barrier((packed_back, rear_part))
    rear_sum = lax.psum(rear_part, "sp")
    dw2 = dw2 - jnp.mean(dw2, 1, keepdims=True)
    db2 = db2 - jnp.mean(db2, -1, keepdims=True)
    small = jnp.concatenate([db1[:, 0], db2[:, 0], dgn[:, 0], dsh[:, 0], jnp.zeros((slots, head), f32)], 1)
    inner_rows = jnp.concatenate([dw1, dw2, pad_to(small.reshape(slots, 2, inner), -(-(2 * head + 2) // S) * S - 2 * head, 1)], 1)
    share = inner_rows.shape[1] // S
    inner_send = inner_rows.astype(bf16).reshape(slots, S, share, 2, 128).transpose(1, 0, 3, 2, 4)
    inner_send = inner_send.reshape(S, slots * 2 * share, 128)

    arrived = swap(packed_back, "fsdp")
    grad_packed, normed_parts = back_call(arrived, rate_slope, front, layout, piece, tiles)
    weight_parts = tn(normed, grad_packed.reshape(Z * total, packed_width)).astype(bf16)
    weight_parts = weight_parts.reshape(S, own, packed_width)
    extent = -(-inner_send.shape[1] * 128 // packed_width)
    inner_send = pad_to(inner_send.reshape(S, -1), extent * packed_width, 1).reshape(S, extent, packed_width)
    got = swap(jnp.concatenate([weight_parts, inner_send], 1), "fsdp")
    got, normed_parts = lax.optimization_barrier((got, normed_parts))
    got_sum = jnp.sum(got[:, :own].astype(f32), 0).astype(bf16)
    weight_all = lax.all_gather(got_sum, "sp", axis=0)
    normed_parts, rear_sum, weight_all = lax.optimization_barrier((normed_parts, rear_sum, weight_all))
    normed_parts = swap(normed_parts.reshape(Z, total, width), "sp")
    out_grad, gate_grad, fgate_grad, fup_grad, down_grad, gate_dot, post_grad = unpack_call(
        rear_sum, gate_weight, ffn_gate, ffn_up, post_gain[:, None], ff // S
    )
    post_grad = post_grad[:, 0]
    inner_part = got[:, own:].reshape(S, -1)[:, : slots * 2 * share * 128].astype(f32)
    inner_part = jnp.sum(inner_part.reshape(groups, micro, slots, 2, share, 128), 1)
    inner_part = inner_part.transpose(1, 0, 3, 2, 4).reshape(slots * groups, share, 2 * 128)[:local]
    query_grad, key_grad, value_grad, rate_grad, pre_grad = finish_call(
        weight_all, query_weight, key_weight, value_weight, rate_weight, gate_dot, pre_gain[:, None], layout
    )
    pre_grad = pre_grad[:, 0]
    rear_done = (out_grad, gate_grad, fgate_grad, fup_grad, down_grad, post_grad, pre_grad)
    rear_done, inner_part = lax.optimization_barrier((rear_done, inner_part.astype(bf16)))
    out_grad, gate_grad, fgate_grad, fup_grad, down_grad, post_grad, pre_grad = rear_done
    inner_sum = lax.all_gather(inner_part, "fsdp", axis=1, tiled=True).astype(f32)
    tokens_grad = token_call(normed_parts, grad_normed_gate, own_tokens, pre_full, grad_middle)
    tail = inner_sum[:, 2 * head : 2 * head + 2].reshape(local, 2 * inner)
    return (
        output.reshape(tokens.shape),
        tokens_grad.reshape(tokens.shape),
        pre_grad,
        query_grad,
        key_grad,
        value_grad,
        gate_grad,
        rate_grad,
        out_grad,
        post_grad,
        fgate_grad,
        fup_grad,
        down_grad,
        inner_sum[:, :head],
        tail[:, :inner],
        inner_sum[:, head : 2 * head].transpose(0, 2, 1),
        tail[:, inner : inner + head],
        tail[:, inner + head : inner + 2 * head],
        tail[:, inner + 2 * head : inner + 3 * head],
    )


def solution(mesh):
    return jax.shard_map(
        shards,
        mesh=mesh,
        in_specs=(
            P(None, "fsdp", "sp", None),
            P(),
            P(None, "fsdp", "sp", None),
            P("fsdp"),
            P("fsdp", None),
            P("fsdp", None),
            P("fsdp", None),
            P("fsdp", None),
            P("fsdp", None),
            P("fsdp", None),
            P("fsdp"),
            P("fsdp", None),
            P("fsdp", None),
            P("fsdp", None),
            P("sp", None, None),
            P("sp", None),
            P("sp", None, None),
            P("sp", None),
            P("sp", None),
            P("sp", None),
        ),
        out_specs=(
            P(None, "fsdp", "sp", None),
            P(None, "fsdp", "sp", None),
            P("fsdp"),
            P("fsdp", None),
            P("fsdp", None),
            P("fsdp", None),
            P("fsdp", None),
            P("fsdp", None),
            P("fsdp", None),
            P("fsdp"),
            P("fsdp", None),
            P("fsdp", None),
            P("fsdp", None),
            P("sp", None, None),
            P("sp", None),
            P("sp", None, None),
            P("sp", None),
            P("sp", None),
            P("sp", None),
        ),
        check_vma=False,
    )
```

```python
import functools

import jax
import jax.numpy as jnp
from jax import lax
from jax.experimental import pallas as pl
from jax.experimental.pallas import tpu as pltpu
from jax.sharding import PartitionSpec as P

MINI = 16
EPS = 1e-06
RATE = 1.0 / 1024.0
GELU_C = 0.7978845608028654
GELU_K = 0.044715
VMEM_BYTES = 58 * 1024 * 1024
f32 = jnp.float32
bf16 = jnp.bfloat16

def nn(x,y): return lax.dot_general(x.astype(bf16),y.astype(bf16),(((1,),(0,)),((),())),preferred_element_type=f32)
def nt(x,y): return lax.dot_general(x.astype(bf16),y.astype(bf16),(((1,),(1,)),((),())),preferred_element_type=f32)
def tn(x,y): return lax.dot_general(x.astype(bf16),y.astype(bf16),(((0,),(0,)),((),())),preferred_element_type=f32)
def gelu1(z):
    t=jnp.tanh(GELU_C*z*(1.0+GELU_K*(z*z)))
    return 0.5*z*(1.0+t)
def gelu2(z):
    z2=z*z
    t=jnp.tanh(z*(GELU_C+(GELU_C*GELU_K)*z2))
    h=0.5+0.5*t
    return z*h, h+0.5*z*(1.0-t*t)*(GELU_C+(3.0*GELU_C*GELU_K)*z2)
def gelu3(z):
    z2=z*z
    t=jnp.tanh(z*(GELU_C+(GELU_C*GELU_K)*z2))
    h=0.5+0.5*t
    u=GELU_C+(3.0*GELU_C*GELU_K)*z2
    c=1.0-t*t
    return z*h, h+0.5*z*c*u, c*(u+z*((3.0*GELU_C*GELU_K)*z-t*u*u))

def cat(*xs): return jnp.concatenate(xs,0)
def rs(x): return jnp.sum(x,-1,keepdims=True)*(1.0/64)

def interleave(gens):
    gens=list(gens)
    while gens:
        alive=[]
        for g in gens:
            try:
                next(g); alive.append(g)
            except StopIteration: pass
        gens=alive

def masks():
    lower=lax.broadcasted_iota(jnp.int32,(MINI,MINI),0)>=lax.broadcasted_iota(jnp.int32,(MINI,MINI),1)
    return lower.astype(f32), jnp.where(lower,0.0,1.0)

def split_rows(slots,piece,tiles,x_ref,q_ref,k_ref,v_ref,e_ref):
    eye=lax.broadcasted_iota(jnp.int32,(128,128),0)==lax.broadcasted_iota(jnp.int32,(128,128),1)
    @pl.loop(0,x_ref.shape[0])
    def _(src):
        base=pl.multiple_of(src*piece,piece)
        for j in range(slots):
            for index,ref in enumerate((q_ref,k_ref,v_ref)):
                lane=(3*j+index)*64
                top=lane//128*piece
                ref[j,pl.ds(base,piece)]=x_ref[src,top:top+piece,lane%128:lane%128+64]
        rates=x_ref[src,tiles*piece:tiles*piece+16].astype(f32)
        for j in range(slots):
            for i in range(piece//128):
                n=j*(piece//128)+i
                column=jnp.sum(jnp.where(eye,rates[n:n+1],0.0),1,keepdims=True)
                e_ref[j,pl.ds(base+i*128,128)]=jnp.broadcast_to(column,(128,128))

def fwd_kernel(slots,count,unroll,piece,tiles,x_ref,w1_ref,b1_ref,w2_ref,b2_ref,gain_ref,shift_ref,
    mix_ref,w1s_ref,w2s_ref,z1_ref,h_ref,q1_ref,n_ref,g_ref,nq_ref,
    q_ref,k_ref,v_ref,e_ref,W1,B1,W2,B2,Z,ZQ,AP,EP):
    lower,upper=masks()
    steps=q_ref.shape[1]//MINI
    pid=pl.program_id(0)
    @pl.when(pid==0)
    def _():
        split_rows(slots,piece,tiles,x_ref,q_ref,k_ref,v_ref,e_ref)
        for j in range(slots):
            W1[j]=w1_ref[j]; B1[j]=b1_ref[j]; W2[j]=w2_ref[j]; B2[j]=b2_ref[j]
            Z[j]=nn(k_ref[j,:MINI],w1_ref[j])+b1_ref[j]
            ZQ[j]=jnp.zeros((MINI,256),f32); AP[j]=jnp.zeros((MINI,256),bf16); EP[j]=jnp.zeros((MINI,64),bf16)
    def chain(j,i):
        t=pid*count+i
        rows=pl.ds(pl.multiple_of(t*MINI,MINI),MINI)
        prow=pl.ds(pl.multiple_of(jnp.maximum(t-1,0)*MINI,MINI),MINI)
        nrow=pl.ds(pl.multiple_of(jnp.minimum(t+1,steps-1)*MINI,MINI),MINI)
        brow=pl.ds(pl.multiple_of(i*MINI,MINI),MINI)
        gain=gain_ref[j]; shift=shift_ref[j]; g2=gain*gain; mg=rs(g2)
        z1=Z[j]; q1=ZQ[j]; w2=W2[j]; b2=B2[j]
        w2b=w2.astype(bf16)
        Ap=AP[j]; Ep=EP[j]
        A,Ad=gelu2(z1); AQ=gelu1(q1)
        Ab=A.astype(bf16); AQb=AQ.astype(bf16)
        z1_ref[j,brow]=z1.astype(bf16)
        yield
        zz=nt(cat(Ab,AQb),w2b)
        z=zz[:MINI]+b2; qb=zz[MINI:]+b2
        yield
        P2=upper*(nt(AQb,Ap)+1.0)
        K=k_ref[j,rows]; Q=q_ref[j,rows]; Kn=k_ref[j,nrow]
        w1=W1[j]; w1b=w1.astype(bf16); b1=B1[j]
        w1s_ref[j,i]=w1b; w2s_ref[j,i]=w2b
        KQ=cat(Kn,Q)
        KK=nt(KQ,K)+1.0
        L=cat(KK[:MINI].astype(bf16),(lower*KK[MINI:]).astype(bf16),K.T)
        base=nn(KQ,w1b)+b1
        U=gain*(shift-v_ref[j,rows].astype(f32)+K.astype(f32)); mU=rs(U)
        e=e_ref[j,rows]; e64=e[:,:64]; e256=jnp.concatenate([e,e],1)
        yield
        Q2=qb+nn(P2,Ep)
        yield
        zg=z*g2
        mz=rs(z); p0=rs(z*z); p1=rs(zg); p2=rs(z*zg); p3=rs(z*U)
        s=lax.rsqrt(p0-mz*mz+EPS)
        m1=s*(p1-mz*mg)+mU
        m2=s*(s*(p2-2.0*mz*p1+mz*mz*mg)+(p3-mz*mU))
        N=s*(z-mz)
        G=s*(N*(g2-m2)+(U-m1))
        Gb=G.astype(bf16)
        yield
        H=nn(Gb,w2b)
        E2=e64*G; E2b=E2.astype(bf16)
        n_ref[j,brow]=(z-mz).astype(bf16); g_ref[j,brow]=Gb
        EP[j]=E2b; AP[j]=Ab
        yield
        W2[j]=w2-tn(E2b,Ab)
        B2[j]=b2-jnp.sum(E2,0,keepdims=True)
        yield
        E1=(e256*Ad)*H; E1b=E1.astype(bf16)
        X=nn(L,E1b)
        Z[j]=base[:MINI]-X[:MINI]
        Q1=base[MINI:]-X[MINI:2*MINI]
        ZQ[j]=Q1
        W1[j]=w1-X[2*MINI:]
        B1[j]=b1-jnp.sum(E1,0,keepdims=True)
        h_ref[j,brow]=H.astype(bf16); q1_ref[j,brow]=Q1.astype(bf16)
        yield
        mq=rs(Q2); vq=rs(Q2*Q2)
        sq=lax.rsqrt(vq-mq*mq+EPS)
        Nq=sq*(Q2-mq)
        Qp=q_ref[j,prow].astype(f32)
        mix_ref[prow,64*j:64*j+64]=(Qp+Nq*gain+shift).astype(bf16)
        nq_ref[j,prow]=(Q2-mq).astype(bf16)
    @pl.loop(0,count//unroll)
    def _(i):
        for u in range(unroll):
            interleave(chain(j,i*unroll+u) for j in range(slots))
    @pl.when(pid==pl.num_programs(0)-1)
    def _():
        for j in range(slots):
            prow=pl.ds((steps-1)*MINI,MINI)
            AQb=gelu1(ZQ[j]).astype(bf16)
            Q2=nt(AQb,W2[j])+B2[j]+nn(upper*(nt(AQb,AP[j])+1.0),EP[j])
            mq=rs(Q2); vq=rs(Q2*Q2)
            sq=lax.rsqrt(vq-mq*mq+EPS)
            Nq=sq*(Q2-mq)
            mix_ref[prow,64*j:64*j+64]=(q_ref[j,prow].astype(f32)+Nq*gain_ref[j]+shift_ref[j]).astype(bf16)
            nq_ref[j,prow]=(Q2-mq).astype(bf16)

def fwd_call(x,w1,b1,w2,b2,gain,shift,piece,tiles,block=256,unroll=2,**kw):
    slots=w1.shape[0]; length=x.shape[0]*piece
    count=block//MINI; nb=length//block; steps=length//MINI
    row=lambda w: pl.BlockSpec((slots,block,w),lambda i:(0,i,0))
    full=lambda s: pl.BlockSpec(s,lambda i:(0,)*len(s),pipeline_mode=pl.Buffered(1))
    r64=full((slots,length,64)); r1=full((slots,length,128)); rm_=full((length,64*slots))
    st=pl.BlockSpec((slots,count,64,256),lambda i:(0,i,0,0))
    S=jax.ShapeDtypeStruct
    return pl.pallas_call(functools.partial(fwd_kernel,slots,count,unroll,piece,tiles),
        grid=(nb,),
        in_specs=[full(a.shape) for a in (x,w1,b1,w2,b2,gain,shift)],
        out_specs=[rm_,st,st,row(256),row(256),row(256),row(64),row(64),r64],
        out_shape=[S((length,64*slots),bf16)]+[S((slots,steps,64,256),bf16)]*2+[S((slots,length,256),bf16)]*3+[S((slots,length,64),bf16)]*3,
        scratch_shapes=[pltpu.VMEM((slots,length,64),bf16)]*3+[pltpu.VMEM((slots,length,128),f32)]+[pltpu.VMEM((slots,64,256),f32),pltpu.VMEM((slots,1,256),f32),pltpu.VMEM((slots,64,256),f32),pltpu.VMEM((slots,1,64),f32),pltpu.VMEM((slots,MINI,256),f32),pltpu.VMEM((slots,MINI,256),f32),pltpu.VMEM((slots,MINI,256),bf16),pltpu.VMEM((slots,MINI,64),bf16)],
        compiler_params=pltpu.CompilerParams(dimension_semantics=("arbitrary",),vmem_limit_bytes=VMEM_BYTES),
        name="inner_forward",cost_estimate=pl.CostEstimate(flops=90_000_000_000,bytes_accessed=40_000_000,transcendentals=0),**kw)(x,w1,b1,w2,b2,gain,shift)


def bwd_kernel(slots,count,unroll,piece,tiles,x_ref,dx_ref,n_ref,g_ref,nq_ref,w1s_ref,w2s_ref,z1_ref,h_ref,q1_ref,gain_ref,shift_ref,
    out_ref,dw1_ref,db1_ref,dw2_ref,db2_ref,dgn_ref,dsh_ref,
    q_ref,k_ref,v_ref,e_ref,do_ref,de_ref,    DW1,DB1,G2,DB2,KD,DGN,DSH,DGQ,DSQ,
    sA,sAd,sHA,sGZ,sE1,sE2,sW1,sW2,sR1,sR2,sDA,sQ1,sQ2,sAQ,sb1,sb2):
    lower,_=masks()
    steps=q_ref.shape[1]//MINI
    pid=pl.program_id(0); nb=pl.num_programs(0)
    @pl.when(pid==0)
    def _():
        split_rows(slots,piece,tiles,x_ref,q_ref,k_ref,v_ref,e_ref)
        @pl.loop(0,out_ref.shape[0])
        def _(src):
            rows=pl.ds(pl.multiple_of(src*piece,piece),piece)
            for j in range(slots):
                do_ref[j,rows]=dx_ref[rows,64*j:64*j+64]
        for r in (DW1,DB1,G2,DB2,KD,DGN,DSH,DGQ,DSQ):
            r[...]=jnp.zeros(r.shape,r.dtype)
        for r in (sA,sAd,sHA,sGZ,sE1,sE2,sW1,sW2,sR1,sR2,sDA,sQ1,sQ2,sAQ,sb1,sb2):
            r[0]=jnp.zeros(r.shape[1:],r.dtype)
    def put(j,index,t,value):
        t=jnp.minimum(t,steps-1)
        lane=(3*j+index)*64
        top=lane//128*piece
        part=piece//MINI
        rows=pl.ds(pl.multiple_of(top+lax.rem(t,part)*MINI,MINI),MINI)
        out_ref[lax.div(t,part),rows,lane%128:lane%128+64]=value.astype(bf16)
    def crit(j,p,t):
        rows=pl.ds(pl.multiple_of(jnp.minimum(t,steps-1)*MINI,MINI),MINI)
        prow=pl.ds(pl.multiple_of(jnp.maximum(t-1,0)*MINI,MINI),MINI)
        gain=gain_ref[j]; shift=shift_ref[j]; g2=gain*gain; mg=rs(g2)
        e=e_ref[j,rows]; e64=e[:,:64]; e=jnp.concatenate([e,e],1)
        nE1=sR1[p,j]+KD[j]
        dgZ1=(-e)*nE1
        dH=dgZ1*sAd[p,j]
        dHb=dH.astype(bf16)
        w2b=sW2[p,j]
        G2f=G2[j]; G2b=G2f.astype(bf16)
        Ab=sA[p,j]; E2b=sE2[p,j]
        yield
        a1=nt(Ab,G2b)
        yP=nt(dHb,w2b)
        yield
        Zc=n_ref[j,rows].astype(f32); G=g_ref[j,rows].astype(f32)
        s=lax.rsqrt(rs(Zc*Zc)+EPS); N=s*Zc
        K=k_ref[j,rows]; Q=q_ref[j,rows]; Kp=k_ref[j,prow]
        T=shift-v_ref[j,rows].astype(f32)+K.astype(f32)
        U=gain*T
        gN=N*g2
        c1=rs(gN); c2=rs(gN*N); mU=rs(U); UN=rs(U*N)
        a=gN+U; ma=c1+mU; m2=c2+UN
        a2=nn(E2b,G2b)
        E1b=sE1[p,j]; dQ1b=sQ1[p,j]
        DW=DW1[j]; DWb=DW.astype(bf16)
        KDb=nn(Kp,DWb)+DB1[j]
        yield
        a3=nt(E1b,DWb)
        X1=(lower*nt(dQ1b,E1b)).astype(bf16)
        L2=cat((nt(Kp,cat(Q,K))+1.0).astype(bf16),cat(Q,K).T)
        yield
        nE2=sR2[p,j]+a1+DB2[j]
        y=yP-e64*nE2
        yg=y*g2; yn=y*N
        ym=rs(y); yN=rs(yn); yG=rs(y*G); ygm=rs(yg); ygN=rs(yg*N)
        mdy=s*ym; mdyN=s*yN
        da=s*y-mdy-N*mdyN
        sN=s*ygN-mdy*c1-mdyN*c2-2.0*m2*mdyN
        mN=s*ygm-mdy*mg-mdyN*c1-ma*mdyN-m2*mdy
        kap=yG+sN
        dN=da*g2-a*mdyN-(s*m2)*y
        dZc=s*(dN-mN-N*kap)
        dZb=dZc.astype(bf16)
        dT=da*gain
        yield
        dA=nn(dZb,w2b)+sDA[p,j]-a2
        yield
        G2[j]=G2f+tn(cat(sQ2[p,j],g_ref[j,rows],dZb),cat(sAQ[p,j],dHb,Ab))
        DB2[j]=DB2[j]+sb2[p,j]+jnp.sum(dZc,0,keepdims=True)
        dQs=nn(X1,K); dKs=tn(X1,Q)
        put(j,2,t,-dT)
        dO=do_ref[j,rows].astype(f32)
        DGN[j]=DGN[j]+da*(2.0*gain*N+T)
        DSH[j]=DSH[j]+dT
        de_ref[j,rows]=-(jnp.sum(nE1*sGZ[p,j],-1,keepdims=True)+jnp.sum(nE2*G,-1,keepdims=True))
        yield
        dZ1=dA*sAd[p,j]+dgZ1*sHA[p,j]
        dZ1b=dZ1.astype(bf16)
        dd=cat(dQ1b,dZ1b)
        X=nn(L2,dd)
        KD[j]=KDb+X[:MINI]
        DW1[j]=DW+X[MINI:]
        DB1[j]=DB1[j]+sb1[p,j]+jnp.sum(dZ1,0,keepdims=True)
        yield
        qk=nt(dd,sW1[p,j])
        put(j,0,t,dO+qk[:MINI]-dQs)
        put(j,1,t,qk[MINI:]-dKs-a3+dT)
    def qside(j,p,t,i):
        rows=pl.ds(pl.multiple_of(t*MINI,MINI),MINI)
        brow=pl.ds(pl.multiple_of(i*MINI,MINI),MINI)
        gain=gain_ref[j]
        dO=do_ref[j,rows].astype(f32); Qc=nq_ref[j,rows].astype(f32)
        sq=lax.rsqrt(rs(Qc*Qc)+EPS); Nq=sq*Qc
        dNq=dO*gain
        dQ2=sq*(dNq-rs(dNq)-Nq*rs(dNq*Nq))
        dQ2b=dQ2.astype(bf16)
        A,Ad,Add=gelu3(z1_ref[j,brow].astype(f32))
        AQ,AQd=gelu2(q1_ref[j,brow].astype(f32))
        H=h_ref[j,brow].astype(f32); e=e_ref[j,rows]; e64=e[:,:64]; e=jnp.concatenate([e,e],1)
        Ab=A.astype(bf16); AQb=AQ.astype(bf16)
        gZ1=H*Ad
        E1b=(e*gZ1).astype(bf16); E2b=(e64*g_ref[j,rows].astype(f32)).astype(bf16)
        w1b=w1s_ref[j,i]; w2b=w2s_ref[j,i]
        yield
        sA[p,j]=Ab; sAd[p,j]=Ad; sHA[p,j]=H*Add; sGZ[p,j]=gZ1; sE1[p,j]=E1b; sE2[p,j]=E2b; sW1[p,j]=w1b; sW2[p,j]=w2b; sAQ[p,j]=AQb
        sQ2[p,j]=dQ2b; sb2[p,j]=jnp.sum(dQ2,0,keepdims=True)
        DGQ[j]=DGQ[j]+dO*Nq; DSQ[j]=DSQ[j]+dO
        Q=q_ref[j,rows]; K=k_ref[j,rows]
        P1=(lower*(nt(Q,K)+1.0)).astype(bf16)
        P2=(lower*(nt(AQb,Ab)+1.0)).astype(bf16)
        yield
        X2=(lower*nt(dQ2b,E2b)).astype(bf16)
        yield
        b1=nn(dQ2b,w2b)
        yield
        sR2[p,j]=tn(P2,dQ2b)
        yield
        dAQ=b1-nn(X2,Ab)
        sDA[p,j]=-tn(X2,AQb)
        yield
        yield
        dQ1=dAQ*AQd
        dQ1b=dQ1.astype(bf16)
        sQ1[p,j]=dQ1b; sb1[p,j]=jnp.sum(dQ1,0,keepdims=True)
        sR1[p,j]=tn(P1,dQ1b)
    @pl.loop(0,count//unroll)
    def _(i):
        for u in range(unroll):
            ii=count-1-(i*unroll+u)
            t=(nb-1-pid)*count+ii
            interleave([crit(j,u%2,t+1) for j in range(slots)]+[qside(j,(u+1)%2,t,ii) for j in range(slots)])
    @pl.when(pid==nb-1)
    def _():
        interleave([crit(j,0,jnp.int32(0)) for j in range(slots)])
        eye=lax.broadcasted_iota(jnp.int32,(128,128),0)==lax.broadcasted_iota(jnp.int32,(128,128),1)
        @pl.loop(0,out_ref.shape[0])
        def _(dst):
            base=pl.multiple_of(dst*piece,piece)
            rows=[jnp.sum(jnp.where(eye,de_ref[j,pl.ds(base+i*128,128)],0.0),0,keepdims=True) for j in range(slots) for i in range(piece//128)]
            rows.append(jnp.zeros((16-len(rows),128),f32))
            out_ref[dst,tiles*piece:tiles*piece+16]=cat(*rows).astype(bf16)
            if tiles*128>slots*192:
                out_ref[dst,(tiles-1)*piece:tiles*piece,(slots*192)%128:]=jnp.zeros((piece,128-(slots*192)%128),bf16)
        for j in range(slots):
            dw1_ref[j]=DW1[j]; db1_ref[j]=DB1[j]; dw2_ref[j]=G2[j]; db2_ref[j]=DB2[j]
            dgn_ref[j]=jnp.sum(DGN[j]+DGQ[j],0,keepdims=True); dsh_ref[j]=jnp.sum(DSH[j]+DSQ[j],0,keepdims=True)

def bwd_call(x,dO,n,g,nq,w1s,w2s,z1,h,q1,gain,shift,piece,tiles,block=256,unroll=2,**kw):
    slots,length,_=n.shape
    count=block//MINI; nb=length//block; steps=length//MINI
    row=lambda w: pl.BlockSpec((slots,block,w),lambda i:(0,nb-1-i,0))
    full=lambda s: pl.BlockSpec(s,lambda i:(0,)*len(s),pipeline_mode=pl.Buffered(1))
    r64=full((slots,length,64)); r1=full((slots,length,128))
    st=pl.BlockSpec((slots,count,64,256),lambda i:(0,nb-1-i,0,0))
    S=jax.ShapeDtypeStruct
    outs=[((length//piece,tiles*piece+16,128),bf16),((slots,64,256),f32),((slots,1,256),f32),((slots,64,256),f32),((slots,1,64),f32),((slots,1,64),f32),((slots,1,64),f32)]
    V=lambda *s,d=f32: pltpu.VMEM(s,d)
    return pl.pallas_call(functools.partial(bwd_kernel,slots,count,unroll,piece,tiles),
        grid=(nb,),
        in_specs=[full(x.shape),full(dO.shape)]+[r64]*3+[st,st]+[row(256)]*3+[full(gain.shape)]*2,
        out_specs=[full(o[0]) for o in outs],
        out_shape=[S(*o) for o in outs],
        scratch_shapes=[V(slots,length,64,d=bf16)]*3+[V(slots,length,128)]+[V(slots,length,64,d=bf16),V(slots,length,1),V(slots,64,256),V(slots,1,256),V(slots,64,256),V(slots,1,64),V(slots,MINI,256),V(slots,MINI,64),V(slots,MINI,64),V(slots,MINI,64),V(slots,MINI,64),
          V(2,slots,MINI,256,d=bf16),V(2,slots,MINI,256),V(2,slots,MINI,256),V(2,slots,MINI,256),V(2,slots,MINI,256,d=bf16),V(2,slots,MINI,64,d=bf16),
          V(2,slots,64,256,d=bf16),V(2,slots,64,256,d=bf16),V(2,slots,MINI,256),V(2,slots,MINI,64),V(2,slots,MINI,256),V(2,slots,MINI,256,d=bf16),V(2,slots,MINI,64,d=bf16),V(2,slots,MINI,256,d=bf16),V(2,slots,1,256),V(2,slots,1,64)],
        compiler_params=pltpu.CompilerParams(dimension_semantics=("arbitrary",),vmem_limit_bytes=VMEM_BYTES),
        name="inner_backward",cost_estimate=pl.CostEstimate(flops=110_000_000_000,bytes_accessed=40_000_000,transcendentals=0),**kw)(x,dO,n,g,nq,w1s,w2s,z1,h,q1,gain,shift)


def rms_back(grad_scaled, inputs, scale):
    return scale * (
        grad_scaled - inputs * scale * scale * jnp.mean(grad_scaled * inputs, -1, keepdims=True)
    )


def gather(block):
    return lax.all_gather(block, "fsdp", axis=0, tiled=True)


def swap(block, axes):
    return lax.all_to_all(block, axes, split_axis=0, concat_axis=0, tiled=True)


def pad_to(array_in, size, dim):
    widths = [(0, 0)] * array_in.ndim
    widths[dim] = (0, size - array_in.shape[dim])
    return jnp.pad(array_in, widths)


def back_kernel(layout, piece, tiles, a_ref, slope_ref, front_ref, grad_ref, parts_ref):
    micro_step = pl.program_id(0)
    groups, slots, local, micro = layout["groups"], layout["slots"], layout["local"], layout["micro"]
    eye = lax.broadcasted_iota(jnp.int32, (128, 128), 0) == lax.broadcasted_iota(jnp.int32, (128, 128), 1)
    lanes = lax.broadcasted_iota(jnp.int32, (piece, 64), 1)
    rates = jnp.zeros((piece, 64), f32)
    for h, part in enumerate(layout["order"]):
        block = a_ref[h * micro + micro_step, tiles * piece : tiles * piece + 16].astype(f32)
        for j, g in enumerate(part):
            column = []
            for i in range(piece // 128):
                n = j * (piece // 128) + i
                column.append(jnp.sum(jnp.where(eye, block[n : n + 1], 0.0), 1, keepdims=True))
            rates = jnp.where(lanes == g, cat(*column), rates)
    slope = slope_ref[:, 0].reshape(piece, slope_ref.shape[-1])
    rates = rates * slope[:, :64]
    halves = []
    for h, part in enumerate(layout["order"]):
        for lane in range(0, len(part) * 192, 64):
            halves.append((h, lane))
    halves.append(None)
    chunks = []
    for n in range(0, len(halves), 2):
        pair = halves[n : n + 2]
        if pair[0] is not None and len(pair) == 2 and pair[1] is not None:
            (h, lane), (h2, lane2) = pair
            if h == h2 and lane % 128 == 0:
                top = lane // 128 * piece
                chunks.append(a_ref[h * micro + micro_step, top : top + piece])
                continue
        values = []
        for half in pair:
            if half is None:
                values.append(rates.astype(bf16))
            else:
                h, lane = half
                top = lane // 128 * piece
                values.append(a_ref[h * micro + micro_step, top : top + piece, lane % 128 : lane % 128 + 64])
        if len(values) == 1:
            values.append(jnp.zeros((piece, 64), bf16))
        chunks.append(jnp.concatenate(values, 1))
    grad = jnp.concatenate(chunks, 1)
    product = nt(grad, front_ref[...]).astype(bf16)
    rows = piece // grad_ref.shape[0]
    grad_ref[:, 0] = grad.reshape(grad_ref.shape[0], rows, grad.shape[1])
    parts_ref[:, 0] = product.reshape(parts_ref.shape[0], rows, product.shape[1])


def back_call(arrived, slope, front, layout, piece, tiles):
    Z, micro, rows, _ = slope.shape
    width = front.shape[0]
    packed = front.shape[1]
    full = lambda s: pl.BlockSpec(s, lambda i: (0,) * len(s), pipeline_mode=pl.Buffered(1))
    step = lambda w: pl.BlockSpec((Z, 1, rows, w), lambda i: (0, i, 0, 0))
    return pl.pallas_call(
        functools.partial(back_kernel, layout, piece, tiles),
        grid=(micro,),
        in_specs=[full(arrived.shape), step(slope.shape[-1]), full(front.shape)],
        out_specs=[step(packed), step(width)],
        out_shape=[
            jax.ShapeDtypeStruct((Z, micro, rows, packed), bf16),
            jax.ShapeDtypeStruct((Z, micro, rows, width), bf16),
        ],
        compiler_params=pltpu.CompilerParams(dimension_semantics=("arbitrary",), vmem_limit_bytes=VMEM_BYTES),
        name="projection_gradients",
        cost_estimate=pl.CostEstimate(flops=1_000_000_000, bytes_accessed=8_000_000, transcendentals=0),
    )(arrived, slope, front)


def finish_kernel(layout, all_ref, q_ref, k_ref, v_ref, r_ref, gate_ref, pre_ref, dq_ref, dk_ref, dv_ref, dr_ref, dot_ref):
    local = layout["local"]
    flat = layout["flat"]
    Z = all_ref.shape[0]
    own = dq_ref.shape[0]
    dot = jnp.zeros((own, 1), f32)
    rate = jnp.zeros((own, dr_ref.shape[1]), f32)
    lanes = lax.broadcasted_iota(jnp.int32, rate.shape, 1)
    for index, (weight, out) in enumerate(((q_ref, dq_ref), (k_ref, dk_ref), (v_ref, dv_ref))):
        for z in range(Z):
            for g in range(local):
                start = (flat.index(g) * 3 + index) * 64
                value = all_ref[z, :, start : start + 64].astype(f32)
                place = (z * local + g) * 64
                out[:, place : place + 64] = value
        dot = dot + jnp.sum(out[...] * weight[...].astype(f32), 1, keepdims=True)
    for z in range(Z):
        for g in range(local):
            n = local * 192 + g
            rate = jnp.where(lanes == z * local + g, all_ref[z, :, n : n + 1].astype(f32), rate)
    dr_ref[...] = rate
    dot = dot + jnp.sum(rate * r_ref[...].astype(f32), 1, keepdims=True) + gate_ref[...]
    dot_ref[...] = dot / pre_ref[...].astype(f32)


def finish_call(gathered, q_w, k_w, v_w, r_w, gate_dot, pre, layout):
    own, width = q_w.shape
    Z = gathered.shape[0]
    shapes = [(own, width)] * 3 + [(own, Z * layout["local"]), (own, 1)]
    return pl.pallas_call(
        functools.partial(finish_kernel, layout),
        out_shape=[jax.ShapeDtypeStruct(s, f32) for s in shapes],
        compiler_params=pltpu.CompilerParams(vmem_limit_bytes=VMEM_BYTES),
        name="weight_gradients",
        cost_estimate=pl.CostEstimate(flops=10_000_000, bytes_accessed=2_000_000, transcendentals=0),
    )(gathered, q_w, k_w, v_w, r_w, gate_dot, pre)


def rear_kernel(layout, got_ref, act_ref, slope_ref, tok_ref, w_hbm, post_ref, gh_ref, go_ref,
                send_ref, lhs_ref, rhs_ref, hid_ref, gm_ref, mid_ref, w_all, sems):
    groups, slots, local, micro = layout["groups"], layout["slots"], layout["local"], layout["micro"]
    Z, rows = got_ref.shape[1], got_ref.shape[2]
    total, width = act_ref.shape
    ff = hid_ref.shape[1]
    w_ref = w_all
    part = 512
    regions = [(0, width)]
    for c in range(ff // part):
        regions += [(2 * width + c * part, part), (2 * width + ff + c * part, part)]
    copies = [
        pltpu.make_async_copy(w_hbm.at[:, pl.ds(first, size)], w_all.at[:, pl.ds(first, size)], sems.at[n])
        for n, (first, size) in enumerate(regions)
    ]
    for copy in copies:
        copy.start()
    blocks = []
    for m in range(micro):
        pieces = []
        for z in range(Z):
            for g in range(local):
                h, j = g % groups, g // groups
                pieces.append(got_ref[h * micro + m, z, :, 64 * j : 64 * j + 64])
        blocks.append(jnp.concatenate(pieces, 1))
    mixed = cat(*blocks).astype(f32)
    copies[0].wait()
    gated = (act_ref[...] * mixed).astype(bf16)
    lhs_ref[0] = gated.T
    middle = tok_ref[...].astype(f32) + nn(gated, w_ref[:, :width])
    mid_ref[...] = middle
    scale = lax.rsqrt(jnp.mean(middle * middle, -1, keepdims=True) + EPS)
    post = post_ref[...]
    low = (middle * scale * post).astype(bf16)
    lhs_ref[1] = low.T
    gm_ref[...] = jnp.zeros((total, width), f32)
    step = 256

    def chunk(c):
        here = pl.ds(pl.multiple_of(c * step, step), step)
        gate_at = pl.ds(pl.multiple_of(2 * width + c * step, step), step)
        up_at = pl.ds(pl.multiple_of(2 * width + ff + c * step, step), step)
        gate_w, up_w = w_ref[:, gate_at], w_ref[:, up_at]
        gate_pre, up_pre = nn(low, gate_w), nn(low, up_w)
        sig = 0.5 + 0.5 * jnp.tanh(0.5 * gate_pre)
        silu = gate_pre * sig
        hid_ref[:, here] = (silu * up_pre).astype(bf16)
        grad = gh_ref[:, here]
        g_gate = (grad * up_pre * sig * (1.0 + gate_pre * (1.0 - sig))).astype(bf16)
        g_up = (grad * silu).astype(bf16)
        rhs_ref[:, gate_at] = g_gate
        rhs_ref[:, up_at] = g_up
        gm_ref[...] += nt(g_gate, gate_w) + nt(g_up, up_w)

    for n in range(ff // part):
        copies[1 + 2 * n].wait()
        copies[2 + 2 * n].wait()
        pl.loop(n * (part // step), (n + 1) * (part // step))(chunk)

    middle = mid_ref[...]
    grad_middle = go_ref[...].astype(f32) + rms_back(gm_ref[...] * post, middle, scale)
    gm_ref[...] = grad_middle
    branch = grad_middle.astype(bf16)
    rhs_ref[:, :width] = branch
    grad_gated = nt(branch, w_ref[:, :width])
    grad_mixed = (grad_gated * act_ref[...]).astype(bf16)
    rhs_ref[:, width : 2 * width] = (grad_gated * mixed * slope_ref[...]).astype(bf16)
    for m in range(micro):
        for z in range(Z):
            for h in range(groups):
                for j in range(slots):
                    g = h + j * groups
                    if g < local:
                        lane = (z * local + g) * 64
                        value = grad_mixed[m * rows : m * rows + rows, lane : lane + 64]
                    else:
                        value = jnp.zeros((rows, 64), bf16)
                    send_ref[h * micro + m, z, :, 64 * j : 64 * j + 64] = value


def rear_call(layout, got, act, slope, tok, weights, post, grad_hidden, grad_low):
    total, width = act.shape
    ff = grad_hidden.shape[1]
    S_ = jax.ShapeDtypeStruct
    specs = [pl.BlockSpec(memory_space=pltpu.VMEM)] * 8
    specs[4] = pl.BlockSpec(memory_space=pl.ANY)
    return pl.pallas_call(
        functools.partial(rear_kernel, layout),
        in_specs=specs,
        scratch_shapes=[pltpu.VMEM(weights.shape, bf16), pltpu.SemaphoreType.DMA((1 + 2 * (ff // 512),))],
        out_shape=[
            S_(got.shape, bf16), S_((2, width, total), bf16), S_((total, weights.shape[1]), bf16),
            S_((total, ff), bf16), S_((total, width), f32), S_((total, width), f32),
        ],
        compiler_params=pltpu.CompilerParams(vmem_limit_bytes=VMEM_BYTES),
        name="rear",
        cost_estimate=pl.CostEstimate(flops=5_000_000_000, bytes_accessed=16_000_000, transcendentals=0),
    )(got, act, slope, tok, weights, post, grad_hidden, grad_low)


def rear_grad_kernel(starts, per_step, lhs_ref, normed_ref, low_ref, rhs_ref, hid_ref, out_ref):
    S = out_ref.shape[0]
    own = out_ref.shape[1] // per_step
    gate_at, ffn_at, down_at = starts

    def block(n, top):
        here = pl.ds(top * own, own)

        def write(left):
            right = rhs_ref[:, pl.ds(pl.multiple_of(n * 256, 256), 256)]
            out_ref[:, here] = nn(left, right).astype(bf16).reshape(S, own, 256)

        @pl.when(n < gate_at)
        def _():
            write(lhs_ref[0])

        @pl.when((n >= gate_at) & (n < ffn_at))
        def _():
            write(normed_ref[...])

        @pl.when((n >= ffn_at) & (n < down_at))
        def _():
            write(lhs_ref[1])

        @pl.when(n >= down_at)
        def _():
            i = n - down_at
            part = hid_ref.shape[1] // S
            k = 256 // part
            gap = low_ref.shape[0] // k
            left = [low_ref[pl.ds(pl.multiple_of(c * gap + i * own, 8), own)] for c in range(k)]
            product = nn(cat(*left), hid_ref[...]).astype(bf16)
            for d in range(S):
                parts = [product[c * own : c * own + own, part * d : part * d + part] for c in range(k)]
                out_ref[d, here] = parts[0] if k == 1 else jnp.concatenate(parts, 1)

    for u in range(per_step):
        block(pl.program_id(0) * per_step + u, u)


def rear_grad_call(lhs, normed_t, low_t, rhs, hidden, S):
    _, width, total = lhs.shape
    own = width // S
    starts = (width // 256, 2 * width // 256, rhs.shape[1] // 256)
    blocks = starts[2] + width * hidden.shape[1] // S // 256 // own
    per_step = 2 - blocks % 2
    full = lambda a: pl.BlockSpec(a.shape, lambda n: (0,) * a.ndim, pipeline_mode=pl.Buffered(1))
    return pl.pallas_call(
        functools.partial(rear_grad_kernel, starts, per_step),
        grid=(blocks // per_step,),
        in_specs=[full(a) for a in (lhs, normed_t, low_t, rhs, hidden)],
        out_specs=pl.BlockSpec((S, per_step * own, 256), lambda n: (0, n, 0)),
        out_shape=jax.ShapeDtypeStruct((S, blocks * own, 256), bf16),
        compiler_params=pltpu.CompilerParams(dimension_semantics=("arbitrary",), vmem_limit_bytes=VMEM_BYTES),
        name="rear_gradients",
        cost_estimate=pl.CostEstimate(flops=4_000_000_000, bytes_accessed=16_000_000, transcendentals=0),
    )(lhs, normed_t, low_t, rhs, hidden)


def unpack_kernel(down_at, part, sum_ref, gate_w, fgate_w, fup_w, post_ref,
                  out_ref, gate_ref, fgate_ref, fup_ref, down_ref, dot_ref, post_grad_ref):
    own = out_ref.shape[0]
    n = 0
    for ref in (out_ref, gate_ref, fgate_ref, fup_ref):
        for c in range(ref.shape[1] // 256):
            ref[:, c * 256 : c * 256 + 256] = sum_ref[n * own : n * own + own].astype(f32)
            n += 1
    gap = down_ref.shape[1] * part // 256
    for c in range(256 // part):
        block = sum_ref[down_at * own : down_at * own + gap, c * part : c * part + part].astype(f32)
        down_ref[:, c * gap : c * gap + gap] = block.T

    def row_dot(grad, weight):
        return jnp.sum(grad[...] * weight[...].astype(f32), 1, keepdims=True)

    dot_ref[...] = row_dot(gate_ref, gate_w)
    post_grad_ref[...] = (row_dot(fgate_ref, fgate_w) + row_dot(fup_ref, fup_w)) / post_ref[...].astype(f32)


def unpack_call(packed, gate_w, fgate_w, fup_w, post, ff_own):
    own, width = gate_w.shape
    ff = fgate_w.shape[1]
    shapes = [(own, width), (own, width), (own, ff), (own, ff), (ff_own, width), (own, 1), (own, 1)]
    return pl.pallas_call(
        functools.partial(unpack_kernel, (2 * width + 2 * ff) // 256, ff_own),
        out_shape=[jax.ShapeDtypeStruct(s, f32) for s in shapes],
        compiler_params=pltpu.CompilerParams(vmem_limit_bytes=VMEM_BYTES),
        name="rear_unpack",
        cost_estimate=pl.CostEstimate(flops=1_000_000, bytes_accessed=1_000_000, transcendentals=0),
    )(packed, gate_w, fgate_w, fup_w, post)


def token_kernel(parts_ref, gate_ref, tok_ref, gain_ref, middle_ref, out_ref):
    grad = gate_ref[...]
    for z in range(parts_ref.shape[0]):
        grad = grad + parts_ref[z].astype(f32)
    tok = tok_ref[...].astype(f32)
    scale = lax.rsqrt(jnp.mean(tok * tok, -1, keepdims=True) + EPS)
    out_ref[...] = (middle_ref[...] + rms_back(grad * gain_ref[...], tok, scale)).astype(bf16)


def token_call(parts, gate, tok, gain, middle):
    return pl.pallas_call(
        token_kernel,
        out_shape=jax.ShapeDtypeStruct(tok.shape, bf16),
        compiler_params=pltpu.CompilerParams(vmem_limit_bytes=VMEM_BYTES),
        name="token_gradients",
        cost_estimate=pl.CostEstimate(flops=10_000_000, bytes_accessed=4_000_000, transcendentals=0),
    )(parts, gate, tok, gain, middle)


def front_kernel(layout, piece, tiles, tok_ref, w_ref, normed_ref, slope_ref, send_ref, gains_ref):
    local, order = layout["local"], layout["order"]
    width, packed = w_ref.shape
    extra = local * 192
    eye = lax.broadcasted_iota(jnp.int32, (128, 128), 0) == lax.broadcasted_iota(jnp.int32, (128, 128), 1)

    def to_row(column):
        return jnp.sum(jnp.where(eye, column, 0.0), 0, keepdims=True)

    @pl.when(pl.program_id(0) == 0)
    def _():
        for n in range(2):
            lane = extra + local + n
            for c in range(width // 128):
                column = w_ref[c * 128 : c * 128 + 128, lane : lane + 1].astype(f32)
                gains_ref[n : n + 1, c * 128 : c * 128 + 128] = to_row(column)

    tok = tok_ref[:, 0].reshape(piece, width).astype(f32)
    scale = lax.rsqrt(jnp.mean(tok * tok, -1, keepdims=True) + EPS)
    normed = (tok * scale * gains_ref[0:1]).astype(bf16)
    normed_ref[:, 0] = normed.reshape(normed_ref.shape[0], -1, width)
    projected = nn(normed, w_ref[...])
    sig = 0.5 + 0.5 * jnp.tanh(0.5 * projected[:, extra : extra + local])
    slope = jnp.concatenate([RATE * sig * (1.0 - sig), jnp.zeros((piece, 128 - local), f32)], 1)
    slope_ref[:, 0] = slope.reshape(slope_ref.shape[0], -1, 128)
    rates = (RATE * sig).astype(bf16).astype(f32)
    low = projected.astype(bf16)
    start = 0
    for h, part in enumerate(order):
        for t in range(tiles):
            first, stop = start + t * 128, min(start + t * 128 + 128, packed)
            if first >= packed:
                value = jnp.zeros((piece, 128), bf16)
            else:
                value = low[:, first:stop]
                if stop - first < 128:
                    value = jnp.concatenate([value, jnp.zeros((piece, 128 - stop + first), bf16)], 1)
            send_ref[h, 0, t * piece : t * piece + piece] = value
        start += len(part) * 192
        rows = []
        for j in range(layout["slots"]):
            for i in range(piece // 128):
                if j < len(part):
                    g = part[j]
                    rows.append(to_row(rates[i * 128 : i * 128 + 128, g : g + 1]))
                else:
                    rows.append(jnp.zeros((1, 128), f32))
        rows.append(jnp.zeros((16 - len(rows), 128), f32))
        send_ref[h, 0, tiles * piece : tiles * piece + 16] = cat(*rows).astype(bf16)


def front_call(tokens, weights, layout, piece, tiles):
    Z, micro, rows, width = tokens.shape
    groups = layout["groups"]
    extent = tiles * piece + 16
    step = lambda w: pl.BlockSpec((Z, 1, rows, w), lambda m: (0, m, 0, 0))
    full = lambda s: pl.BlockSpec(s, lambda m: (0,) * len(s), pipeline_mode=pl.Buffered(1))
    S_ = jax.ShapeDtypeStruct
    return pl.pallas_call(
        functools.partial(front_kernel, layout, piece, tiles),
        grid=(micro,),
        in_specs=[step(width), full(weights.shape)],
        out_specs=[step(width), step(128), pl.BlockSpec((groups, 1, extent, 128), lambda m: (0, m, 0, 0)), full((2, width))],
        out_shape=[
            S_((Z, micro, rows, width), bf16), S_((Z, micro, rows, 128), f32),
            S_((groups, micro, extent, 128), bf16), S_((2, width), f32),
        ],
        compiler_params=pltpu.CompilerParams(dimension_semantics=("arbitrary",), vmem_limit_bytes=VMEM_BYTES),
        name="front",
        cost_estimate=pl.CostEstimate(flops=1_000_000_000, bytes_accessed=7_000_000, transcendentals=0),
    )(tokens, weights)


def shards(
    tokens,
    lengths,
    cotangent,
    pre_gain,
    query_weight,
    key_weight,
    value_weight,
    gate_weight,
    rate_weight,
    out_weight,
    post_gain,
    ffn_gate,
    ffn_up,
    ffn_down,
    inner_first,
    inner_first_bias,
    inner_second,
    inner_second_bias,
    inner_gain,
    inner_shift,
):
    micro, _, rows, width = tokens.shape
    local, head, inner = inner_first.shape
    ff = ffn_gate.shape[1]
    Z = lax.axis_size("sp")
    S = lax.axis_size("fsdp")
    z = lax.axis_index("sp")
    d = lax.axis_index("fsdp")
    groups = S // micro
    slots = -(-local // groups)
    order = [[g for g in range(h, local, groups)] for h in range(groups)]
    flat = [g for part in order for g in part]
    span = 3 * head
    tiles = -(-slots * span // 128)
    piece = Z * rows
    length = S * piece
    total = micro * rows
    own = query_weight.shape[0]
    extra = local * span
    packed_width = -(-(extra + local + 2) // 128) * 128

    def columns(weight, count):
        return lax.dynamic_slice_in_dim(weight, z * count, count, 1)

    q_w, k_w, v_w = (
        columns(w, local * head).reshape(own, local, head)
        for w in (query_weight, key_weight, value_weight)
    )
    r_w = columns(rate_weight, local)
    parts = []
    for g in flat:
        parts += [q_w[:, g], k_w[:, g], v_w[:, g]]
    parts += [r_w, pre_gain[:, None], post_gain[:, None]]
    packed = pad_to(jnp.concatenate(parts, 1), packed_width, 1)
    front = gather(packed)
    all_tokens = lax.all_gather(tokens[:, 0], "sp", axis=0)
    rear_in = (jnp.concatenate([out_weight, gate_weight, ffn_gate, ffn_up], 1), ffn_down)
    rear_in, front, all_tokens = lax.optimization_barrier((rear_in, front, all_tokens))
    layout = dict(groups=groups, slots=slots, local=local, micro=micro, order=order, flat=flat)
    normed, rate_slope, send, gains = front_call(all_tokens, front, layout, piece, tiles)
    normed = normed.reshape(Z * total, width)
    pre_full, post_full = gains[:1], gains[1:]
    arrived = swap(send.reshape(S, tiles * piece + 16, 128), "fsdp")

    half = d // micro
    heads_here = [jnp.minimum(half + j * groups, local - 1) for j in range(slots)]

    def of_slots(array_in):
        return jnp.stack([lax.dynamic_index_in_dim(array_in, g, 0, keepdims=False) for g in heads_here])

    w1 = of_slots(inner_first)
    b1 = of_slots(inner_first_bias)[:, None]
    w2 = of_slots(inner_second)
    w2 = (w2 - jnp.mean(w2, -1, keepdims=True)).transpose(0, 2, 1)
    b2 = of_slots(inner_second_bias)[:, None]
    b2 = b2 - jnp.mean(b2, -1, keepdims=True)
    gain = of_slots(inner_gain)[:, None]
    shift = of_slots(inner_shift)[:, None]
    mix, *saved = fwd_call(arrived, w1, b1, w2, b2, gain, shift, piece, tiles)
    w1s, w2s, z1, h, q1, n, g_, nq = saved

    rear_own, down_in = rear_in
    rear = gather(rear_own)
    out_full = rear[:, :width]
    gate_full = rear[:, width : 2 * width]
    fgate_full = rear[:, 2 * width : 2 * width + ff]
    fup_full = rear[:, 2 * width + ff :]
    down_full = gather(down_in)

    got = swap(mix.reshape(S * Z, rows, slots * head), ("fsdp", "sp"))
    own_tokens = tokens.reshape(total, width)
    own_normed = lax.dynamic_slice_in_dim(normed, z * total, total, 0)
    gate_act, gate_slope = gelu2(nn(own_normed, gate_full))
    position = d * piece + z * rows + lax.broadcasted_iota(jnp.int32, (micro, rows), 1)
    live = (position < lengths[:, None]).astype(f32).reshape(total, 1)
    grad_low = (cotangent.reshape(total, width).astype(f32) * live).astype(bf16)
    grad_hidden = nt(grad_low, down_full)
    got, gate_act, gate_slope, grad_hidden, normed_t, low_t = lax.optimization_barrier(
        (got, gate_act, gate_slope, grad_hidden, own_normed.T, grad_low.T)
    )
    sent, lhs, rhs, hidden, grad_middle, middle = rear_call(
        layout, got.reshape(S, Z, rows, slots * head), gate_act, gate_slope, own_tokens, rear, post_full,
        grad_hidden, grad_low,
    )
    d_mix = swap(sent.reshape(S * Z, rows, slots * head), ("fsdp", "sp")).reshape(length, slots * head)
    rear_grad = rear_grad_call(lhs, normed_t, low_t, rhs, hidden, S)
    d_mix, rear_grad = lax.optimization_barrier((d_mix, rear_grad))
    packed_rows = rear_grad.shape[1]
    rear_part = lax.psum_scatter(rear_grad.reshape(S * packed_rows, 256), "fsdp", scatter_dimension=0, tiled=True)
    output = (middle + nn(hidden, down_full)).astype(bf16)
    grad_normed_gate = nt(rhs[:, width : 2 * width], gate_full)

    packed_back, dw1, db1, dw2, db2, dgn, dsh = bwd_call(
        arrived, d_mix, n, g_, nq, w1s, w2s, z1, h, q1, gain, shift, piece, tiles, unroll=4
    )
    packed_back, rear_part = lax.optimization_barrier((packed_back, rear_part))
    rear_sum = lax.psum(rear_part, "sp")
    dw2 = dw2 - jnp.mean(dw2, 1, keepdims=True)
    db2 = db2 - jnp.mean(db2, -1, keepdims=True)
    small = jnp.concatenate([db1[:, 0], db2[:, 0], dgn[:, 0], dsh[:, 0], jnp.zeros((slots, head), f32)], 1)
    inner_rows = jnp.concatenate([dw1, dw2, pad_to(small.reshape(slots, 2, inner), -(-(2 * head + 2) // S) * S - 2 * head, 1)], 1)
    share = inner_rows.shape[1] // S
    inner_send = inner_rows.astype(bf16).reshape(slots, S, share, 2, 128).transpose(1, 0, 3, 2, 4)
    inner_send = inner_send.reshape(S, slots * 2 * share, 128)

    arrived = swap(packed_back, "fsdp")
    grad_packed, normed_parts = back_call(arrived, rate_slope, front, layout, piece, tiles)
    weight_parts = tn(normed, grad_packed.reshape(Z * total, packed_width)).astype(bf16)
    weight_parts = weight_parts.reshape(S, own, packed_width)
    extent = -(-inner_send.shape[1] * 128 // packed_width)
    inner_send = pad_to(inner_send.reshape(S, -1), extent * packed_width, 1).reshape(S, extent, packed_width)
    got = swap(jnp.concatenate([weight_parts, inner_send], 1), "fsdp")
    got, normed_parts = lax.optimization_barrier((got, normed_parts))
    got_sum = jnp.sum(got[:, :own].astype(f32), 0).astype(bf16)
    weight_all = lax.all_gather(got_sum, "sp", axis=0)
    normed_parts, rear_sum, weight_all = lax.optimization_barrier((normed_parts, rear_sum, weight_all))
    normed_parts = swap(normed_parts.reshape(Z, total, width), "sp")
    out_grad, gate_grad, fgate_grad, fup_grad, down_grad, gate_dot, post_grad = unpack_call(
        rear_sum, gate_weight, ffn_gate, ffn_up, post_gain[:, None], ff // S
    )
    post_grad = post_grad[:, 0]
    inner_part = got[:, own:].reshape(S, -1)[:, : slots * 2 * share * 128].astype(f32)
    inner_part = jnp.sum(inner_part.reshape(groups, micro, slots, 2, share, 128), 1)
    inner_part = inner_part.transpose(1, 0, 3, 2, 4).reshape(slots * groups, share, 2 * 128)[:local]
    query_grad, key_grad, value_grad, rate_grad, pre_grad = finish_call(
        weight_all, query_weight, key_weight, value_weight, rate_weight, gate_dot, pre_gain[:, None], layout
    )
    pre_grad = pre_grad[:, 0]
    rear_done = (out_grad, gate_grad, fgate_grad, fup_grad, down_grad, post_grad, pre_grad)
    rear_done, inner_part = lax.optimization_barrier((rear_done, inner_part.astype(bf16)))
    out_grad, gate_grad, fgate_grad, fup_grad, down_grad, post_grad, pre_grad = rear_done
    inner_sum = lax.all_gather(inner_part, "fsdp", axis=1, tiled=True).astype(f32)
    tokens_grad = token_call(normed_parts, grad_normed_gate, own_tokens, pre_full, grad_middle)
    tail = inner_sum[:, 2 * head : 2 * head + 2].reshape(local, 2 * inner)
    return (
        output.reshape(tokens.shape),
        tokens_grad.reshape(tokens.shape),
        pre_grad,
        query_grad,
        key_grad,
        value_grad,
        gate_grad,
        rate_grad,
        out_grad,
        post_grad,
        fgate_grad,
        fup_grad,
        down_grad,
        inner_sum[:, :head],
        tail[:, :inner],
        inner_sum[:, head : 2 * head].transpose(0, 2, 1),
        tail[:, inner : inner + head],
        tail[:, inner + head : inner + 2 * head],
        tail[:, inner + 2 * head : inner + 3 * head],
    )


def solution(mesh):
    return jax.shard_map(
        shards,
        mesh=mesh,
        in_specs=(
            P(None, "fsdp", "sp", None),
            P(),
            P(None, "fsdp", "sp", None),
            P("fsdp"),
            P("fsdp", None),
            P("fsdp", None),
            P("fsdp", None),
            P("fsdp", None),
            P("fsdp", None),
            P("fsdp", None),
            P("fsdp"),
            P("fsdp", None),
            P("fsdp", None),
            P("fsdp", None),
            P("sp", None, None),
            P("sp", None),
            P("sp", None, None),
            P("sp", None),
            P("sp", None),
            P("sp", None),
        ),
        out_specs=(
            P(None, "fsdp", "sp", None),
            P(None, "fsdp", "sp", None),
            P("fsdp"),
            P("fsdp", None),
            P("fsdp", None),
            P("fsdp", None),
            P("fsdp", None),
            P("fsdp", None),
            P("fsdp", None),
            P("fsdp"),
            P("fsdp", None),
            P("fsdp", None),
            P("fsdp", None),
            P("sp", None, None),
            P("sp", None),
            P("sp", None, None),
            P("sp", None),
            P("sp", None),
            P("sp", None),
        ),
        check_vma=False,
    )
```

```python
import functools

import jax
import jax.numpy as jnp
from jax import lax
from jax.experimental import pallas as pl
from jax.experimental.pallas import tpu as pltpu
from jax.sharding import PartitionSpec as P

MINI = 16
EPS = 1e-06
RATE = 1.0 / 1024.0
GELU_C = 0.7978845608028654
GELU_K = 0.044715
VMEM_BYTES = 58 * 1024 * 1024
f32 = jnp.float32
bf16 = jnp.bfloat16

def nn(x,y): return lax.dot_general(x.astype(bf16),y.astype(bf16),(((1,),(0,)),((),())),preferred_element_type=f32)
def nt(x,y): return lax.dot_general(x.astype(bf16),y.astype(bf16),(((1,),(1,)),((),())),preferred_element_type=f32)
def tn(x,y): return lax.dot_general(x.astype(bf16),y.astype(bf16),(((0,),(0,)),((),())),preferred_element_type=f32)
def gelu1(z):
    t=jnp.tanh(GELU_C*z*(1.0+GELU_K*(z*z)))
    return 0.5*z*(1.0+t)
def gelu2(z):
    z2=z*z
    t=jnp.tanh(z*(GELU_C+(GELU_C*GELU_K)*z2))
    h=0.5+0.5*t
    return z*h, h+0.5*z*(1.0-t*t)*(GELU_C+(3.0*GELU_C*GELU_K)*z2)
def gelu3(z):
    z2=z*z
    t=jnp.tanh(z*(GELU_C+(GELU_C*GELU_K)*z2))
    h=0.5+0.5*t
    u=GELU_C+(3.0*GELU_C*GELU_K)*z2
    c=1.0-t*t
    return z*h, h+0.5*z*c*u, c*(u+z*((3.0*GELU_C*GELU_K)*z-t*u*u))

def cat(*xs): return jnp.concatenate(xs,0)
def rs(x): return jnp.sum(x,-1,keepdims=True)*(1.0/64)

def interleave(gens):
    gens=list(gens)
    while gens:
        alive=[]
        for g in gens:
            try:
                next(g); alive.append(g)
            except StopIteration: pass
        gens=alive

def masks():
    lower=lax.broadcasted_iota(jnp.int32,(MINI,MINI),0)>=lax.broadcasted_iota(jnp.int32,(MINI,MINI),1)
    return lower.astype(f32), jnp.where(lower,0.0,1.0)

def split_rows(slots,piece,tiles,x_ref,q_ref,k_ref,v_ref,e_ref):
    eye=lax.broadcasted_iota(jnp.int32,(128,128),0)==lax.broadcasted_iota(jnp.int32,(128,128),1)
    @pl.loop(0,x_ref.shape[0])
    def _(src):
        base=pl.multiple_of(src*piece,piece)
        for j in range(slots):
            for index,ref in enumerate((q_ref,k_ref,v_ref)):
                lane=(3*j+index)*64
                top=lane//128*piece
                ref[j,pl.ds(base,piece)]=x_ref[src,top:top+piece,lane%128:lane%128+64]
        rates=x_ref[src,tiles*piece:tiles*piece+16].astype(f32)
        for j in range(slots):
            for i in range(piece//128):
                n=j*(piece//128)+i
                column=jnp.sum(jnp.where(eye,rates[n:n+1],0.0),1,keepdims=True)
                e_ref[j,pl.ds(base+i*128,128)]=jnp.broadcast_to(column,(128,128))

def fwd_kernel(slots,count,unroll,piece,tiles,x_ref,w1_ref,b1_ref,w2_ref,b2_ref,gain_ref,shift_ref,
    mix_ref,w1s_ref,w2s_ref,z1_ref,h_ref,q1_ref,n_ref,g_ref,nq_ref,
    q_ref,k_ref,v_ref,e_ref,W1,B1,W2,B2,Z,ZQ,AP,EP):
    lower,upper=masks()
    steps=q_ref.shape[1]//MINI
    pid=pl.program_id(0)
    @pl.when(pid==0)
    def _():
        split_rows(slots,piece,tiles,x_ref,q_ref,k_ref,v_ref,e_ref)
        for j in range(slots):
            W1[j]=w1_ref[j]; B1[j]=b1_ref[j]; W2[j]=w2_ref[j]; B2[j]=b2_ref[j]
            Z[j]=nn(k_ref[j,:MINI],w1_ref[j])+b1_ref[j]
            ZQ[j]=jnp.zeros((MINI,256),f32); AP[j]=jnp.zeros((MINI,256),bf16); EP[j]=jnp.zeros((MINI,64),bf16)
    def chain(j,i):
        t=pid*count+i
        rows=pl.ds(pl.multiple_of(t*MINI,MINI),MINI)
        prow=pl.ds(pl.multiple_of(jnp.maximum(t-1,0)*MINI,MINI),MINI)
        nrow=pl.ds(pl.multiple_of(jnp.minimum(t+1,steps-1)*MINI,MINI),MINI)
        brow=pl.ds(pl.multiple_of(i*MINI,MINI),MINI)
        gain=gain_ref[j]; shift=shift_ref[j]; g2=gain*gain; mg=rs(g2)
        z1=Z[j]; q1=ZQ[j]; w2=W2[j]; b2=B2[j]
        w2b=w2.astype(bf16)
        Ap=AP[j]; Ep=EP[j]
        A,Ad=gelu2(z1); AQ=gelu1(q1)
        Ab=A.astype(bf16); AQb=AQ.astype(bf16)
        z1_ref[j,brow]=z1.astype(bf16)
        yield
        zz=nt(cat(Ab,AQb),w2b)
        z=zz[:MINI]+b2; qb=zz[MINI:]+b2
        yield
        P2=upper*(nt(AQb,Ap)+1.0)
        K=k_ref[j,rows]; Q=q_ref[j,rows]; Kn=k_ref[j,nrow]
        w1=W1[j]; w1b=w1.astype(bf16); b1=B1[j]
        w1s_ref[j,i]=w1b; w2s_ref[j,i]=w2b
        KQ=cat(Kn,Q)
        KK=nt(KQ,K)+1.0
        L=cat(KK[:MINI].astype(bf16),(lower*KK[MINI:]).astype(bf16),K.T)
        base=nn(KQ,w1b)+b1
        U=gain*(shift-v_ref[j,rows].astype(f32)+K.astype(f32)); mU=rs(U)
        e=e_ref[j,rows]; e64=e[:,:64]; e256=jnp.concatenate([e,e],1)
        yield
        Q2=qb+nn(P2,Ep)
        yield
        zg=z*g2
        mz=rs(z); p0=rs(z*z); p1=rs(zg); p2=rs(z*zg); p3=rs(z*U)
        s=lax.rsqrt(p0-mz*mz+EPS)
        m1=s*(p1-mz*mg)+mU
        m2=s*(s*(p2-2.0*mz*p1+mz*mz*mg)+(p3-mz*mU))
        N=s*(z-mz)
        G=s*(N*(g2-m2)+(U-m1))
        Gb=G.astype(bf16)
        yield
        H=nn(Gb,w2b)
        E2=e64*G; E2b=E2.astype(bf16)
        n_ref[j,brow]=(z-mz).astype(bf16); g_ref[j,brow]=Gb
        EP[j]=E2b; AP[j]=Ab
        yield
        W2[j]=w2-tn(E2b,Ab)
        B2[j]=b2-jnp.sum(E2,0,keepdims=True)
        yield
        E1=(e256*Ad)*H; E1b=E1.astype(bf16)
        X=nn(L,E1b)
        Z[j]=base[:MINI]-X[:MINI]
        Q1=base[MINI:]-X[MINI:2*MINI]
        ZQ[j]=Q1
        W1[j]=w1-X[2*MINI:]
        B1[j]=b1-jnp.sum(E1,0,keepdims=True)
        h_ref[j,brow]=H.astype(bf16); q1_ref[j,brow]=Q1.astype(bf16)
        yield
        mq=rs(Q2); vq=rs(Q2*Q2)
        sq=lax.rsqrt(vq-mq*mq+EPS)
        Nq=sq*(Q2-mq)
        Qp=q_ref[j,prow].astype(f32)
        mix_ref[prow,64*j:64*j+64]=(Qp+Nq*gain+shift).astype(bf16)
        nq_ref[j,prow]=(Q2-mq).astype(bf16)
    @pl.loop(0,count//unroll)
    def _(i):
        for u in range(unroll):
            interleave(chain(j,i*unroll+u) for j in range(slots))
    @pl.when(pid==pl.num_programs(0)-1)
    def _():
        for j in range(slots):
            prow=pl.ds((steps-1)*MINI,MINI)
            AQb=gelu1(ZQ[j]).astype(bf16)
            Q2=nt(AQb,W2[j])+B2[j]+nn(upper*(nt(AQb,AP[j])+1.0),EP[j])
            mq=rs(Q2); vq=rs(Q2*Q2)
            sq=lax.rsqrt(vq-mq*mq+EPS)
            Nq=sq*(Q2-mq)
            mix_ref[prow,64*j:64*j+64]=(q_ref[j,prow].astype(f32)+Nq*gain_ref[j]+shift_ref[j]).astype(bf16)
            nq_ref[j,prow]=(Q2-mq).astype(bf16)

def fwd_call(x,w1,b1,w2,b2,gain,shift,piece,tiles,block=256,unroll=2,**kw):
    slots=w1.shape[0]; length=x.shape[0]*piece
    count=block//MINI; nb=length//block; steps=length//MINI
    row=lambda w: pl.BlockSpec((slots,block,w),lambda i:(0,i,0))
    full=lambda s: pl.BlockSpec(s,lambda i:(0,)*len(s),pipeline_mode=pl.Buffered(1))
    r64=full((slots,length,64)); r1=full((slots,length,128)); rm_=full((length,64*slots))
    st=pl.BlockSpec((slots,count,64,256),lambda i:(0,i,0,0))
    S=jax.ShapeDtypeStruct
    return pl.pallas_call(functools.partial(fwd_kernel,slots,count,unroll,piece,tiles),
        grid=(nb,),
        in_specs=[full(a.shape) for a in (x,w1,b1,w2,b2,gain,shift)],
        out_specs=[rm_,st,st,row(256),row(256),row(256),row(64),row(64),r64],
        out_shape=[S((length,64*slots),bf16)]+[S((slots,steps,64,256),bf16)]*2+[S((slots,length,256),bf16)]*3+[S((slots,length,64),bf16)]*3,
        scratch_shapes=[pltpu.VMEM((slots,length,64),bf16)]*3+[pltpu.VMEM((slots,length,128),f32)]+[pltpu.VMEM((slots,64,256),f32),pltpu.VMEM((slots,1,256),f32),pltpu.VMEM((slots,64,256),f32),pltpu.VMEM((slots,1,64),f32),pltpu.VMEM((slots,MINI,256),f32),pltpu.VMEM((slots,MINI,256),f32),pltpu.VMEM((slots,MINI,256),bf16),pltpu.VMEM((slots,MINI,64),bf16)],
        compiler_params=pltpu.CompilerParams(dimension_semantics=("arbitrary",),vmem_limit_bytes=VMEM_BYTES),
        name="inner_forward",cost_estimate=pl.CostEstimate(flops=90_000_000_000,bytes_accessed=40_000_000,transcendentals=0),**kw)(x,w1,b1,w2,b2,gain,shift)


def bwd_kernel(slots,count,unroll,piece,tiles,x_ref,dx_ref,n_ref,g_ref,nq_ref,w1s_ref,w2s_ref,z1_ref,h_ref,q1_ref,gain_ref,shift_ref,
    out_ref,dw1_ref,db1_ref,dw2_ref,db2_ref,dgn_ref,dsh_ref,
    q_ref,k_ref,v_ref,e_ref,do_ref,de_ref,    DW1,DB1,G2,DB2,KD,DGN,DSH,DGQ,DSQ,
    sA,sAd,sHA,sGZ,sE1,sE2,sW1,sW2,sR1,sR2,sDA,sQ1,sQ2,sAQ,sb1,sb2):
    lower,_=masks()
    steps=q_ref.shape[1]//MINI
    pid=pl.program_id(0); nb=pl.num_programs(0)
    @pl.when(pid==0)
    def _():
        split_rows(slots,piece,tiles,x_ref,q_ref,k_ref,v_ref,e_ref)
        @pl.loop(0,out_ref.shape[0])
        def _(src):
            rows=pl.ds(pl.multiple_of(src*piece,piece),piece)
            for j in range(slots):
                do_ref[j,rows]=dx_ref[rows,64*j:64*j+64]
        for r in (DW1,DB1,G2,DB2,KD,DGN,DSH,DGQ,DSQ):
            r[...]=jnp.zeros(r.shape,r.dtype)
        for r in (sA,sAd,sHA,sGZ,sE1,sE2,sW1,sW2,sR1,sR2,sDA,sQ1,sQ2,sAQ,sb1,sb2):
            r[0]=jnp.zeros(r.shape[1:],r.dtype)
    def put(j,index,t,value):
        t=jnp.minimum(t,steps-1)
        lane=(3*j+index)*64
        top=lane//128*piece
        part=piece//MINI
        rows=pl.ds(pl.multiple_of(top+lax.rem(t,part)*MINI,MINI),MINI)
        out_ref[lax.div(t,part),rows,lane%128:lane%128+64]=value.astype(bf16)
    def crit(j,p,t):
        rows=pl.ds(pl.multiple_of(jnp.minimum(t,steps-1)*MINI,MINI),MINI)
        prow=pl.ds(pl.multiple_of(jnp.maximum(t-1,0)*MINI,MINI),MINI)
        gain=gain_ref[j]; shift=shift_ref[j]; g2=gain*gain; mg=rs(g2)
        e=e_ref[j,rows]; e64=e[:,:64]; e=jnp.concatenate([e,e],1)
        nE1=sR1[p,j]+KD[j]
        dgZ1=(-e)*nE1
        dH=dgZ1*sAd[p,j]
        dHb=dH.astype(bf16)
        w2b=sW2[p,j]
        G2f=G2[j]; G2b=G2f.astype(bf16)
        Ab=sA[p,j]; E2b=sE2[p,j]
        yield
        a1=nt(Ab,G2b)
        yP=nt(dHb,w2b)
        yield
        Zc=n_ref[j,rows].astype(f32); G=g_ref[j,rows].astype(f32)
        s=lax.rsqrt(rs(Zc*Zc)+EPS); N=s*Zc
        K=k_ref[j,rows]; Q=q_ref[j,rows]; Kp=k_ref[j,prow]
        T=shift-v_ref[j,rows].astype(f32)+K.astype(f32)
        U=gain*T
        gN=N*g2
        c1=rs(gN); c2=rs(gN*N); mU=rs(U); UN=rs(U*N)
        a=gN+U; ma=c1+mU; m2=c2+UN
        a2=nn(E2b,G2b)
        E1b=sE1[p,j]; dQ1b=sQ1[p,j]
        DW=DW1[j]; DWb=DW.astype(bf16)
        KDb=nn(Kp,DWb)+DB1[j]
        yield
        a3=nt(E1b,DWb)
        X1=(lower*nt(dQ1b,E1b)).astype(bf16)
        L2=cat((nt(Kp,cat(Q,K))+1.0).astype(bf16),cat(Q,K).T)
        yield
        nE2=sR2[p,j]+a1+DB2[j]
        y=yP-e64*nE2
        yg=y*g2; yn=y*N
        ym=rs(y); yN=rs(yn); yG=rs(y*G); ygm=rs(yg); ygN=rs(yg*N)
        mdy=s*ym; mdyN=s*yN
        da=s*y-mdy-N*mdyN
        sN=s*ygN-mdy*c1-mdyN*c2-2.0*m2*mdyN
        mN=s*ygm-mdy*mg-mdyN*c1-ma*mdyN-m2*mdy
        kap=yG+sN
        dN=da*g2-a*mdyN-(s*m2)*y
        dZc=s*(dN-mN-N*kap)
        dZb=dZc.astype(bf16)
        dT=da*gain
        yield
        dA=nn(dZb,w2b)+sDA[p,j]-a2
        yield
        G2[j]=G2f+tn(cat(sQ2[p,j],g_ref[j,rows],dZb),cat(sAQ[p,j],dHb,Ab))
        DB2[j]=DB2[j]+sb2[p,j]+jnp.sum(dZc,0,keepdims=True)
        dQs=nn(X1,K); dKs=tn(X1,Q)
        put(j,2,t,-dT)
        dO=do_ref[j,rows].astype(f32)
        DGN[j]=DGN[j]+da*(2.0*gain*N+T)
        DSH[j]=DSH[j]+dT
        de_ref[j,rows]=-(jnp.sum(nE1*sGZ[p,j],-1,keepdims=True)+jnp.sum(nE2*G,-1,keepdims=True))
        yield
        dZ1=dA*sAd[p,j]+dgZ1*sHA[p,j]
        dZ1b=dZ1.astype(bf16)
        dd=cat(dQ1b,dZ1b)
        X=nn(L2,dd)
        KD[j]=KDb+X[:MINI]
        DW1[j]=DW+X[MINI:]
        DB1[j]=DB1[j]+sb1[p,j]+jnp.sum(dZ1,0,keepdims=True)
        yield
        qk=nt(dd,sW1[p,j])
        put(j,0,t,dO+qk[:MINI]-dQs)
        put(j,1,t,qk[MINI:]-dKs-a3+dT)
    def qside(j,p,t,i):
        rows=pl.ds(pl.multiple_of(t*MINI,MINI),MINI)
        brow=pl.ds(pl.multiple_of(i*MINI,MINI),MINI)
        gain=gain_ref[j]
        dO=do_ref[j,rows].astype(f32); Qc=nq_ref[j,rows].astype(f32)
        sq=lax.rsqrt(rs(Qc*Qc)+EPS); Nq=sq*Qc
        dNq=dO*gain
        dQ2=sq*(dNq-rs(dNq)-Nq*rs(dNq*Nq))
        dQ2b=dQ2.astype(bf16)
        A,Ad,Add=gelu3(z1_ref[j,brow].astype(f32))
        AQ,AQd=gelu2(q1_ref[j,brow].astype(f32))
        H=h_ref[j,brow].astype(f32); e=e_ref[j,rows]; e64=e[:,:64]; e=jnp.concatenate([e,e],1)
        Ab=A.astype(bf16); AQb=AQ.astype(bf16)
        gZ1=H*Ad
        E1b=(e*gZ1).astype(bf16); E2b=(e64*g_ref[j,rows].astype(f32)).astype(bf16)
        w1b=w1s_ref[j,i]; w2b=w2s_ref[j,i]
        yield
        sA[p,j]=Ab; sAd[p,j]=Ad; sHA[p,j]=H*Add; sGZ[p,j]=gZ1; sE1[p,j]=E1b; sE2[p,j]=E2b; sW1[p,j]=w1b; sW2[p,j]=w2b; sAQ[p,j]=AQb
        sQ2[p,j]=dQ2b; sb2[p,j]=jnp.sum(dQ2,0,keepdims=True)
        DGQ[j]=DGQ[j]+dO*Nq; DSQ[j]=DSQ[j]+dO
        Q=q_ref[j,rows]; K=k_ref[j,rows]
        P1=(lower*(nt(Q,K)+1.0)).astype(bf16)
        P2=(lower*(nt(AQb,Ab)+1.0)).astype(bf16)
        yield
        X2=(lower*nt(dQ2b,E2b)).astype(bf16)
        yield
        b1=nn(dQ2b,w2b)
        yield
        sR2[p,j]=tn(P2,dQ2b)
        yield
        dAQ=b1-nn(X2,Ab)
        sDA[p,j]=-tn(X2,AQb)
        yield
        yield
        dQ1=dAQ*AQd
        dQ1b=dQ1.astype(bf16)
        sQ1[p,j]=dQ1b; sb1[p,j]=jnp.sum(dQ1,0,keepdims=True)
        sR1[p,j]=tn(P1,dQ1b)
    @pl.loop(0,count//unroll)
    def _(i):
        for u in range(unroll):
            ii=count-1-(i*unroll+u)
            t=(nb-1-pid)*count+ii
            interleave([crit(j,u%2,t+1) for j in range(slots)]+[qside(j,(u+1)%2,t,ii) for j in range(slots)])
    @pl.when(pid==nb-1)
    def _():
        interleave([crit(j,0,jnp.int32(0)) for j in range(slots)])
        eye=lax.broadcasted_iota(jnp.int32,(128,128),0)==lax.broadcasted_iota(jnp.int32,(128,128),1)
        @pl.loop(0,out_ref.shape[0])
        def _(dst):
            base=pl.multiple_of(dst*piece,piece)
            rows=[jnp.sum(jnp.where(eye,de_ref[j,pl.ds(base+i*128,128)],0.0),0,keepdims=True) for j in range(slots) for i in range(piece//128)]
            rows.append(jnp.zeros((16-len(rows),128),f32))
            out_ref[dst,tiles*piece:tiles*piece+16]=cat(*rows).astype(bf16)
            if tiles*128>slots*192:
                out_ref[dst,(tiles-1)*piece:tiles*piece,(slots*192)%128:]=jnp.zeros((piece,128-(slots*192)%128),bf16)
        for j in range(slots):
            dw1_ref[j]=DW1[j]; db1_ref[j]=DB1[j]; dw2_ref[j]=G2[j]; db2_ref[j]=DB2[j]
            dgn_ref[j]=jnp.sum(DGN[j]+DGQ[j],0,keepdims=True); dsh_ref[j]=jnp.sum(DSH[j]+DSQ[j],0,keepdims=True)

def bwd_call(x,dO,n,g,nq,w1s,w2s,z1,h,q1,gain,shift,piece,tiles,block=256,unroll=2,**kw):
    slots,length,_=n.shape
    count=block//MINI; nb=length//block; steps=length//MINI
    row=lambda w: pl.BlockSpec((slots,block,w),lambda i:(0,nb-1-i,0))
    full=lambda s: pl.BlockSpec(s,lambda i:(0,)*len(s),pipeline_mode=pl.Buffered(1))
    r64=full((slots,length,64)); r1=full((slots,length,128))
    st=pl.BlockSpec((slots,count,64,256),lambda i:(0,nb-1-i,0,0))
    S=jax.ShapeDtypeStruct
    outs=[((length//piece,tiles*piece+16,128),bf16),((slots,64,256),f32),((slots,1,256),f32),((slots,64,256),f32),((slots,1,64),f32),((slots,1,64),f32),((slots,1,64),f32)]
    V=lambda *s,d=f32: pltpu.VMEM(s,d)
    return pl.pallas_call(functools.partial(bwd_kernel,slots,count,unroll,piece,tiles),
        grid=(nb,),
        in_specs=[full(x.shape),full(dO.shape)]+[r64]*3+[st,st]+[row(256)]*3+[full(gain.shape)]*2,
        out_specs=[full(o[0]) for o in outs],
        out_shape=[S(*o) for o in outs],
        scratch_shapes=[V(slots,length,64,d=bf16)]*3+[V(slots,length,128)]+[V(slots,length,64,d=bf16),V(slots,length,1),V(slots,64,256),V(slots,1,256),V(slots,64,256),V(slots,1,64),V(slots,MINI,256),V(slots,MINI,64),V(slots,MINI,64),V(slots,MINI,64),V(slots,MINI,64),
          V(2,slots,MINI,256,d=bf16),V(2,slots,MINI,256),V(2,slots,MINI,256),V(2,slots,MINI,256),V(2,slots,MINI,256,d=bf16),V(2,slots,MINI,64,d=bf16),
          V(2,slots,64,256,d=bf16),V(2,slots,64,256,d=bf16),V(2,slots,MINI,256),V(2,slots,MINI,64),V(2,slots,MINI,256),V(2,slots,MINI,256,d=bf16),V(2,slots,MINI,64,d=bf16),V(2,slots,MINI,256,d=bf16),V(2,slots,1,256),V(2,slots,1,64)],
        compiler_params=pltpu.CompilerParams(dimension_semantics=("arbitrary",),vmem_limit_bytes=VMEM_BYTES),
        name="inner_backward",cost_estimate=pl.CostEstimate(flops=110_000_000_000,bytes_accessed=40_000_000,transcendentals=0),**kw)(x,dO,n,g,nq,w1s,w2s,z1,h,q1,gain,shift)


def rms_back(grad_scaled, inputs, scale):
    return scale * (
        grad_scaled - inputs * scale * scale * jnp.mean(grad_scaled * inputs, -1, keepdims=True)
    )


def gather(block):
    return lax.all_gather(block, "fsdp", axis=0, tiled=True)


def swap(block, axes):
    return lax.all_to_all(block, axes, split_axis=0, concat_axis=0, tiled=True)


def pad_to(array_in, size, dim):
    widths = [(0, 0)] * array_in.ndim
    widths[dim] = (0, size - array_in.shape[dim])
    return jnp.pad(array_in, widths)


def back_kernel(layout, piece, tiles, a_ref, slope_ref, front_ref, grad_ref, parts_ref):
    micro_step = pl.program_id(0)
    groups, slots, local, micro = layout["groups"], layout["slots"], layout["local"], layout["micro"]
    eye = lax.broadcasted_iota(jnp.int32, (128, 128), 0) == lax.broadcasted_iota(jnp.int32, (128, 128), 1)
    lanes = lax.broadcasted_iota(jnp.int32, (piece, 64), 1)
    rates = jnp.zeros((piece, 64), f32)
    for h, part in enumerate(layout["order"]):
        block = a_ref[h * micro + micro_step, tiles * piece : tiles * piece + 16].astype(f32)
        for j, g in enumerate(part):
            column = []
            for i in range(piece // 128):
                n = j * (piece // 128) + i
                column.append(jnp.sum(jnp.where(eye, block[n : n + 1], 0.0), 1, keepdims=True))
            rates = jnp.where(lanes == g, cat(*column), rates)
    slope = slope_ref[:, 0].reshape(piece, slope_ref.shape[-1])
    rates = rates * slope[:, :64]
    halves = []
    for h, part in enumerate(layout["order"]):
        for lane in range(0, len(part) * 192, 64):
            halves.append((h, lane))
    halves.append(None)
    chunks = []
    for n in range(0, len(halves), 2):
        pair = halves[n : n + 2]
        if pair[0] is not None and len(pair) == 2 and pair[1] is not None:
            (h, lane), (h2, lane2) = pair
            if h == h2 and lane % 128 == 0:
                top = lane // 128 * piece
                chunks.append(a_ref[h * micro + micro_step, top : top + piece])
                continue
        values = []
        for half in pair:
            if half is None:
                values.append(rates.astype(bf16))
            else:
                h, lane = half
                top = lane // 128 * piece
                values.append(a_ref[h * micro + micro_step, top : top + piece, lane % 128 : lane % 128 + 64])
        if len(values) == 1:
            values.append(jnp.zeros((piece, 64), bf16))
        chunks.append(jnp.concatenate(values, 1))
    grad = jnp.concatenate(chunks, 1)
    product = nt(grad, front_ref[...]).astype(bf16)
    rows = piece // grad_ref.shape[0]
    grad_ref[:, 0] = grad.reshape(grad_ref.shape[0], rows, grad.shape[1])
    parts_ref[:, 0] = product.reshape(parts_ref.shape[0], rows, product.shape[1])


def back_call(arrived, slope, front, layout, piece, tiles):
    Z, micro, rows, _ = slope.shape
    width = front.shape[0]
    packed = front.shape[1]
    full = lambda s: pl.BlockSpec(s, lambda i: (0,) * len(s), pipeline_mode=pl.Buffered(1))
    step = lambda w: pl.BlockSpec((Z, 1, rows, w), lambda i: (0, i, 0, 0))
    return pl.pallas_call(
        functools.partial(back_kernel, layout, piece, tiles),
        grid=(micro,),
        in_specs=[full(arrived.shape), step(slope.shape[-1]), full(front.shape)],
        out_specs=[step(packed), step(width)],
        out_shape=[
            jax.ShapeDtypeStruct((Z, micro, rows, packed), bf16),
            jax.ShapeDtypeStruct((Z, micro, rows, width), bf16),
        ],
        compiler_params=pltpu.CompilerParams(dimension_semantics=("arbitrary",), vmem_limit_bytes=VMEM_BYTES),
        name="projection_gradients",
        cost_estimate=pl.CostEstimate(flops=1_000_000_000, bytes_accessed=8_000_000, transcendentals=0),
    )(arrived, slope, front)


def finish_kernel(layout, all_ref, q_ref, k_ref, v_ref, r_ref, gate_ref, pre_ref, dq_ref, dk_ref, dv_ref, dr_ref, dot_ref):
    local = layout["local"]
    flat = layout["flat"]
    Z = all_ref.shape[0]
    own = dq_ref.shape[0]
    dot = jnp.zeros((own, 1), f32)
    rate = jnp.zeros((own, dr_ref.shape[1]), f32)
    lanes = lax.broadcasted_iota(jnp.int32, rate.shape, 1)
    for index, (weight, out) in enumerate(((q_ref, dq_ref), (k_ref, dk_ref), (v_ref, dv_ref))):
        for z in range(Z):
            for g in range(local):
                start = (flat.index(g) * 3 + index) * 64
                value = all_ref[z, :, start : start + 64].astype(f32)
                place = (z * local + g) * 64
                out[:, place : place + 64] = value
        dot = dot + jnp.sum(out[...] * weight[...].astype(f32), 1, keepdims=True)
    for z in range(Z):
        for g in range(local):
            n = local * 192 + g
            rate = jnp.where(lanes == z * local + g, all_ref[z, :, n : n + 1].astype(f32), rate)
    dr_ref[...] = rate
    dot = dot + jnp.sum(rate * r_ref[...].astype(f32), 1, keepdims=True) + gate_ref[...]
    dot_ref[...] = dot / pre_ref[...].astype(f32)


def finish_call(gathered, q_w, k_w, v_w, r_w, gate_dot, pre, layout):
    own, width = q_w.shape
    Z = gathered.shape[0]
    shapes = [(own, width)] * 3 + [(own, Z * layout["local"]), (own, 1)]
    return pl.pallas_call(
        functools.partial(finish_kernel, layout),
        out_shape=[jax.ShapeDtypeStruct(s, f32) for s in shapes],
        compiler_params=pltpu.CompilerParams(vmem_limit_bytes=VMEM_BYTES),
        name="weight_gradients",
        cost_estimate=pl.CostEstimate(flops=10_000_000, bytes_accessed=2_000_000, transcendentals=0),
    )(gathered, q_w, k_w, v_w, r_w, gate_dot, pre)


def rear_kernel(layout, got_ref, act_ref, slope_ref, tok_ref, w_hbm, post_ref, gh_ref, go_ref,
                send_ref, lhs_ref, rhs_ref, hid_ref, gm_ref, mid_ref, w_all, sems):
    groups, slots, local, micro = layout["groups"], layout["slots"], layout["local"], layout["micro"]
    Z, rows = got_ref.shape[1], got_ref.shape[2]
    total, width = act_ref.shape
    ff = hid_ref.shape[1]
    w_ref = w_all
    part = 512
    regions = [(0, width)]
    for c in range(ff // part):
        regions += [(2 * width + c * part, part), (2 * width + ff + c * part, part)]
    copies = [
        pltpu.make_async_copy(w_hbm.at[:, pl.ds(first, size)], w_all.at[:, pl.ds(first, size)], sems.at[n])
        for n, (first, size) in enumerate(regions)
    ]
    for copy in copies:
        copy.start()
    blocks = []
    for m in range(micro):
        pieces = []
        for z in range(Z):
            for g in range(local):
                h, j = g % groups, g // groups
                pieces.append(got_ref[h * micro + m, z, :, 64 * j : 64 * j + 64])
        blocks.append(jnp.concatenate(pieces, 1))
    mixed = cat(*blocks).astype(f32)
    copies[0].wait()
    gated = (act_ref[...] * mixed).astype(bf16)
    lhs_ref[0] = gated.T
    middle = tok_ref[...].astype(f32) + nn(gated, w_ref[:, :width])
    mid_ref[...] = middle
    scale = lax.rsqrt(jnp.mean(middle * middle, -1, keepdims=True) + EPS)
    post = post_ref[...]
    low = (middle * scale * post).astype(bf16)
    lhs_ref[1] = low.T
    gm_ref[...] = jnp.zeros((total, width), f32)
    step = 256

    def chunk(c):
        here = pl.ds(pl.multiple_of(c * step, step), step)
        gate_at = pl.ds(pl.multiple_of(2 * width + c * step, step), step)
        up_at = pl.ds(pl.multiple_of(2 * width + ff + c * step, step), step)
        gate_w, up_w = w_ref[:, gate_at], w_ref[:, up_at]
        gate_pre, up_pre = nn(low, gate_w), nn(low, up_w)
        sig = 0.5 + 0.5 * jnp.tanh(0.5 * gate_pre)
        silu = gate_pre * sig
        hid_ref[:, here] = (silu * up_pre).astype(bf16)
        grad = gh_ref[:, here]
        g_gate = (grad * up_pre * sig * (1.0 + gate_pre * (1.0 - sig))).astype(bf16)
        g_up = (grad * silu).astype(bf16)
        rhs_ref[:, gate_at] = g_gate
        rhs_ref[:, up_at] = g_up
        gm_ref[...] += nt(g_gate, gate_w) + nt(g_up, up_w)

    for n in range(ff // part):
        copies[1 + 2 * n].wait()
        copies[2 + 2 * n].wait()
        pl.loop(n * (part // step), (n + 1) * (part // step))(chunk)

    middle = mid_ref[...]
    grad_middle = go_ref[...].astype(f32) + rms_back(gm_ref[...] * post, middle, scale)
    gm_ref[...] = grad_middle
    branch = grad_middle.astype(bf16)
    rhs_ref[:, :width] = branch
    grad_gated = nt(branch, w_ref[:, :width])
    grad_mixed = (grad_gated * act_ref[...]).astype(bf16)
    rhs_ref[:, width : 2 * width] = (grad_gated * mixed * slope_ref[...]).astype(bf16)
    for m in range(micro):
        for z in range(Z):
            for h in range(groups):
                for j in range(slots):
                    g = h + j * groups
                    if g < local:
                        lane = (z * local + g) * 64
                        value = grad_mixed[m * rows : m * rows + rows, lane : lane + 64]
                    else:
                        value = jnp.zeros((rows, 64), bf16)
                    send_ref[h * micro + m, z, :, 64 * j : 64 * j + 64] = value


def rear_call(layout, got, act, slope, tok, weights, post, grad_hidden, grad_low):
    total, width = act.shape
    ff = grad_hidden.shape[1]
    S_ = jax.ShapeDtypeStruct
    specs = [pl.BlockSpec(memory_space=pltpu.VMEM)] * 8
    specs[4] = pl.BlockSpec(memory_space=pl.ANY)
    return pl.pallas_call(
        functools.partial(rear_kernel, layout),
        in_specs=specs,
        scratch_shapes=[pltpu.VMEM(weights.shape, bf16), pltpu.SemaphoreType.DMA((1 + 2 * (ff // 512),))],
        out_shape=[
            S_(got.shape, bf16), S_((2, width, total), bf16), S_((total, weights.shape[1]), bf16),
            S_((total, ff), bf16), S_((total, width), f32), S_((total, width), f32),
        ],
        compiler_params=pltpu.CompilerParams(vmem_limit_bytes=VMEM_BYTES),
        name="rear",
        cost_estimate=pl.CostEstimate(flops=5_000_000_000, bytes_accessed=16_000_000, transcendentals=0),
    )(got, act, slope, tok, weights, post, grad_hidden, grad_low)


def rear_grad_kernel(starts, per_step, lhs_ref, normed_ref, low_ref, rhs_ref, hid_ref, out_ref):
    S = out_ref.shape[0]
    own = out_ref.shape[1] // per_step
    gate_at, ffn_at, down_at = starts

    def block(n, top):
        here = pl.ds(top * own, own)

        def write(left):
            right = rhs_ref[:, pl.ds(pl.multiple_of(n * 256, 256), 256)]
            out_ref[:, here] = nn(left, right).astype(bf16).reshape(S, own, 256)

        @pl.when(n < gate_at)
        def _():
            write(lhs_ref[0])

        @pl.when((n >= gate_at) & (n < ffn_at))
        def _():
            write(normed_ref[...])

        @pl.when((n >= ffn_at) & (n < down_at))
        def _():
            write(lhs_ref[1])

        @pl.when(n >= down_at)
        def _():
            i = n - down_at
            part = hid_ref.shape[1] // S
            k = 256 // part
            gap = low_ref.shape[0] // k
            left = [low_ref[pl.ds(pl.multiple_of(c * gap + i * own, 8), own)] for c in range(k)]
            product = nn(cat(*left), hid_ref[...]).astype(bf16)
            for d in range(S):
                parts = [product[c * own : c * own + own, part * d : part * d + part] for c in range(k)]
                out_ref[d, here] = parts[0] if k == 1 else jnp.concatenate(parts, 1)

    for u in range(per_step):
        block(pl.program_id(0) * per_step + u, u)


def rear_grad_call(lhs, normed_t, low_t, rhs, hidden, S):
    _, width, total = lhs.shape
    own = width // S
    starts = (width // 256, 2 * width // 256, rhs.shape[1] // 256)
    blocks = starts[2] + width * hidden.shape[1] // S // 256 // own
    per_step = next(n for n in (5, 3, 2, 1) if blocks % n == 0)
    full = lambda a: pl.BlockSpec(a.shape, lambda n: (0,) * a.ndim, pipeline_mode=pl.Buffered(1))
    return pl.pallas_call(
        functools.partial(rear_grad_kernel, starts, per_step),
        grid=(blocks // per_step,),
        in_specs=[full(a) for a in (lhs, normed_t, low_t, rhs, hidden)],
        out_specs=pl.BlockSpec((S, per_step * own, 256), lambda n: (0, n, 0)),
        out_shape=jax.ShapeDtypeStruct((S, blocks * own, 256), bf16),
        compiler_params=pltpu.CompilerParams(dimension_semantics=("arbitrary",), vmem_limit_bytes=VMEM_BYTES),
        name="rear_gradients",
        cost_estimate=pl.CostEstimate(flops=4_000_000_000, bytes_accessed=16_000_000, transcendentals=0),
    )(lhs, normed_t, low_t, rhs, hidden)


def unpack_kernel(down_at, part, sum_ref, gate_w, fgate_w, fup_w, post_ref,
                  out_ref, gate_ref, fgate_ref, fup_ref, down_ref, dot_ref, post_grad_ref):
    own = out_ref.shape[0]
    n = 0
    for ref in (out_ref, gate_ref, fgate_ref, fup_ref):
        for c in range(ref.shape[1] // 256):
            ref[:, c * 256 : c * 256 + 256] = sum_ref[n * own : n * own + own].astype(f32)
            n += 1
    gap = down_ref.shape[1] * part // 256
    for c in range(256 // part):
        block = sum_ref[down_at * own : down_at * own + gap, c * part : c * part + part].astype(f32)
        down_ref[:, c * gap : c * gap + gap] = block.T

    def row_dot(grad, weight):
        return jnp.sum(grad[...] * weight[...].astype(f32), 1, keepdims=True)

    dot_ref[...] = row_dot(gate_ref, gate_w)
    post_grad_ref[...] = (row_dot(fgate_ref, fgate_w) + row_dot(fup_ref, fup_w)) / post_ref[...].astype(f32)


def unpack_call(packed, gate_w, fgate_w, fup_w, post, ff_own):
    own, width = gate_w.shape
    ff = fgate_w.shape[1]
    shapes = [(own, width), (own, width), (own, ff), (own, ff), (ff_own, width), (own, 1), (own, 1)]
    return pl.pallas_call(
        functools.partial(unpack_kernel, (2 * width + 2 * ff) // 256, ff_own),
        out_shape=[jax.ShapeDtypeStruct(s, f32) for s in shapes],
        compiler_params=pltpu.CompilerParams(vmem_limit_bytes=VMEM_BYTES),
        name="rear_unpack",
        cost_estimate=pl.CostEstimate(flops=1_000_000, bytes_accessed=1_000_000, transcendentals=0),
    )(packed, gate_w, fgate_w, fup_w, post)


def token_kernel(parts_ref, gate_ref, tok_ref, gain_ref, middle_ref, out_ref):
    grad = gate_ref[...]
    for z in range(parts_ref.shape[0]):
        grad = grad + parts_ref[z].astype(f32)
    tok = tok_ref[...].astype(f32)
    scale = lax.rsqrt(jnp.mean(tok * tok, -1, keepdims=True) + EPS)
    out_ref[...] = (middle_ref[...] + rms_back(grad * gain_ref[...], tok, scale)).astype(bf16)


def token_call(parts, gate, tok, gain, middle):
    return pl.pallas_call(
        token_kernel,
        out_shape=jax.ShapeDtypeStruct(tok.shape, bf16),
        compiler_params=pltpu.CompilerParams(vmem_limit_bytes=VMEM_BYTES),
        name="token_gradients",
        cost_estimate=pl.CostEstimate(flops=10_000_000, bytes_accessed=4_000_000, transcendentals=0),
    )(parts, gate, tok, gain, middle)


def front_kernel(layout, piece, tiles, tok_ref, w_ref, normed_ref, slope_ref, send_ref, gains_ref):
    local, order = layout["local"], layout["order"]
    width, packed = w_ref.shape
    extra = local * 192
    eye = lax.broadcasted_iota(jnp.int32, (128, 128), 0) == lax.broadcasted_iota(jnp.int32, (128, 128), 1)

    def to_row(column):
        return jnp.sum(jnp.where(eye, column, 0.0), 0, keepdims=True)

    @pl.when(pl.program_id(0) == 0)
    def _():
        for n in range(2):
            lane = extra + local + n
            for c in range(width // 128):
                column = w_ref[c * 128 : c * 128 + 128, lane : lane + 1].astype(f32)
                gains_ref[n : n + 1, c * 128 : c * 128 + 128] = to_row(column)

    tok = tok_ref[:, 0].reshape(piece, width).astype(f32)
    scale = lax.rsqrt(jnp.mean(tok * tok, -1, keepdims=True) + EPS)
    normed = (tok * scale * gains_ref[0:1]).astype(bf16)
    normed_ref[:, 0] = normed.reshape(normed_ref.shape[0], -1, width)
    projected = nn(normed, w_ref[...])
    sig = 0.5 + 0.5 * jnp.tanh(0.5 * projected[:, extra : extra + local])
    slope = jnp.concatenate([RATE * sig * (1.0 - sig), jnp.zeros((piece, 128 - local), f32)], 1)
    slope_ref[:, 0] = slope.reshape(slope_ref.shape[0], -1, 128)
    rates = (RATE * sig).astype(bf16).astype(f32)
    low = projected.astype(bf16)
    start = 0
    for h, part in enumerate(order):
        for t in range(tiles):
            first, stop = start + t * 128, min(start + t * 128 + 128, packed)
            if first >= packed:
                value = jnp.zeros((piece, 128), bf16)
            else:
                value = low[:, first:stop]
                if stop - first < 128:
                    value = jnp.concatenate([value, jnp.zeros((piece, 128 - stop + first), bf16)], 1)
            send_ref[h, 0, t * piece : t * piece + piece] = value
        start += len(part) * 192
        rows = []
        for j in range(layout["slots"]):
            for i in range(piece // 128):
                if j < len(part):
                    g = part[j]
                    rows.append(to_row(rates[i * 128 : i * 128 + 128, g : g + 1]))
                else:
                    rows.append(jnp.zeros((1, 128), f32))
        rows.append(jnp.zeros((16 - len(rows), 128), f32))
        send_ref[h, 0, tiles * piece : tiles * piece + 16] = cat(*rows).astype(bf16)


def front_call(tokens, weights, layout, piece, tiles):
    Z, micro, rows, width = tokens.shape
    groups = layout["groups"]
    extent = tiles * piece + 16
    step = lambda w: pl.BlockSpec((Z, 1, rows, w), lambda m: (0, m, 0, 0))
    full = lambda s: pl.BlockSpec(s, lambda m: (0,) * len(s), pipeline_mode=pl.Buffered(1))
    S_ = jax.ShapeDtypeStruct
    return pl.pallas_call(
        functools.partial(front_kernel, layout, piece, tiles),
        grid=(micro,),
        in_specs=[step(width), full(weights.shape)],
        out_specs=[step(width), step(128), pl.BlockSpec((groups, 1, extent, 128), lambda m: (0, m, 0, 0)), full((2, width))],
        out_shape=[
            S_((Z, micro, rows, width), bf16), S_((Z, micro, rows, 128), f32),
            S_((groups, micro, extent, 128), bf16), S_((2, width), f32),
        ],
        compiler_params=pltpu.CompilerParams(dimension_semantics=("arbitrary",), vmem_limit_bytes=VMEM_BYTES),
        name="front",
        cost_estimate=pl.CostEstimate(flops=1_000_000_000, bytes_accessed=7_000_000, transcendentals=0),
    )(tokens, weights)


def shards(
    tokens,
    lengths,
    cotangent,
    pre_gain,
    query_weight,
    key_weight,
    value_weight,
    gate_weight,
    rate_weight,
    out_weight,
    post_gain,
    ffn_gate,
    ffn_up,
    ffn_down,
    inner_first,
    inner_first_bias,
    inner_second,
    inner_second_bias,
    inner_gain,
    inner_shift,
):
    micro, _, rows, width = tokens.shape
    local, head, inner = inner_first.shape
    ff = ffn_gate.shape[1]
    Z = lax.axis_size("sp")
    S = lax.axis_size("fsdp")
    z = lax.axis_index("sp")
    d = lax.axis_index("fsdp")
    groups = S // micro
    slots = -(-local // groups)
    order = [[g for g in range(h, local, groups)] for h in range(groups)]
    flat = [g for part in order for g in part]
    span = 3 * head
    tiles = -(-slots * span // 128)
    piece = Z * rows
    length = S * piece
    total = micro * rows
    own = query_weight.shape[0]
    extra = local * span
    packed_width = -(-(extra + local + 2) // 128) * 128

    def columns(weight, count):
        return lax.dynamic_slice_in_dim(weight, z * count, count, 1)

    q_w, k_w, v_w = (
        columns(w, local * head).reshape(own, local, head)
        for w in (query_weight, key_weight, value_weight)
    )
    r_w = columns(rate_weight, local)
    parts = []
    for g in flat:
        parts += [q_w[:, g], k_w[:, g], v_w[:, g]]
    parts += [r_w, pre_gain[:, None], post_gain[:, None]]
    packed = pad_to(jnp.concatenate(parts, 1), packed_width, 1)
    front = gather(packed)
    all_tokens = lax.all_gather(tokens[:, 0], "sp", axis=0)
    rear_in = (jnp.concatenate([out_weight, gate_weight, ffn_gate, ffn_up], 1), ffn_down)
    rear_in, front, all_tokens = lax.optimization_barrier((rear_in, front, all_tokens))
    layout = dict(groups=groups, slots=slots, local=local, micro=micro, order=order, flat=flat)
    normed, rate_slope, send, gains = front_call(all_tokens, front, layout, piece, tiles)
    normed = normed.reshape(Z * total, width)
    pre_full, post_full = gains[:1], gains[1:]
    arrived = swap(send.reshape(S, tiles * piece + 16, 128), "fsdp")

    half = d // micro
    heads_here = [jnp.minimum(half + j * groups, local - 1) for j in range(slots)]

    def of_slots(array_in):
        return jnp.stack([lax.dynamic_index_in_dim(array_in, g, 0, keepdims=False) for g in heads_here])

    w1 = of_slots(inner_first)
    b1 = of_slots(inner_first_bias)[:, None]
    w2 = of_slots(inner_second)
    w2 = (w2 - jnp.mean(w2, -1, keepdims=True)).transpose(0, 2, 1)
    b2 = of_slots(inner_second_bias)[:, None]
    b2 = b2 - jnp.mean(b2, -1, keepdims=True)
    gain = of_slots(inner_gain)[:, None]
    shift = of_slots(inner_shift)[:, None]
    mix, *saved = fwd_call(arrived, w1, b1, w2, b2, gain, shift, piece, tiles)
    w1s, w2s, z1, h, q1, n, g_, nq = saved

    rear_own, down_in = rear_in
    rear = gather(rear_own)
    out_full = rear[:, :width]
    gate_full = rear[:, width : 2 * width]
    fgate_full = rear[:, 2 * width : 2 * width + ff]
    fup_full = rear[:, 2 * width + ff :]
    down_full = gather(down_in)

    got = swap(mix.reshape(S * Z, rows, slots * head), ("fsdp", "sp"))
    own_tokens = tokens.reshape(total, width)
    own_normed = lax.dynamic_slice_in_dim(normed, z * total, total, 0)
    gate_act, gate_slope = gelu2(nn(own_normed, gate_full))
    position = d * piece + z * rows + lax.broadcasted_iota(jnp.int32, (micro, rows), 1)
    live = (position < lengths[:, None]).astype(f32).reshape(total, 1)
    grad_low = (cotangent.reshape(total, width).astype(f32) * live).astype(bf16)
    grad_hidden = nt(grad_low, down_full)
    got, gate_act, gate_slope, grad_hidden, normed_t, low_t = lax.optimization_barrier(
        (got, gate_act, gate_slope, grad_hidden, own_normed.T, grad_low.T)
    )
    sent, lhs, rhs, hidden, grad_middle, middle = rear_call(
        layout, got.reshape(S, Z, rows, slots * head), gate_act, gate_slope, own_tokens, rear, post_full,
        grad_hidden, grad_low,
    )
    d_mix = swap(sent.reshape(S * Z, rows, slots * head), ("fsdp", "sp")).reshape(length, slots * head)
    rear_grad = rear_grad_call(lhs, normed_t, low_t, rhs, hidden, S)
    d_mix, rear_grad = lax.optimization_barrier((d_mix, rear_grad))
    packed_rows = rear_grad.shape[1]
    rear_part = lax.psum_scatter(rear_grad.reshape(S * packed_rows, 256), "fsdp", scatter_dimension=0, tiled=True)
    output = (middle + nn(hidden, down_full)).astype(bf16)
    grad_normed_gate = nt(rhs[:, width : 2 * width], gate_full)

    packed_back, dw1, db1, dw2, db2, dgn, dsh = bwd_call(
        arrived, d_mix, n, g_, nq, w1s, w2s, z1, h, q1, gain, shift, piece, tiles, unroll=4
    )
    packed_back, rear_part = lax.optimization_barrier((packed_back, rear_part))
    rear_sum = lax.psum(rear_part, "sp")
    dw2 = dw2 - jnp.mean(dw2, 1, keepdims=True)
    db2 = db2 - jnp.mean(db2, -1, keepdims=True)
    small = jnp.concatenate([db1[:, 0], db2[:, 0], dgn[:, 0], dsh[:, 0], jnp.zeros((slots, head), f32)], 1)
    inner_rows = jnp.concatenate([dw1, dw2, pad_to(small.reshape(slots, 2, inner), -(-(2 * head + 2) // S) * S - 2 * head, 1)], 1)
    share = inner_rows.shape[1] // S
    inner_send = inner_rows.astype(bf16).reshape(slots, S, share, 2, 128).transpose(1, 0, 3, 2, 4)
    inner_send = inner_send.reshape(S, slots * 2 * share, 128)

    arrived = swap(packed_back, "fsdp")
    grad_packed, normed_parts = back_call(arrived, rate_slope, front, layout, piece, tiles)
    weight_parts = tn(normed, grad_packed.reshape(Z * total, packed_width)).astype(bf16)
    weight_parts = weight_parts.reshape(S, own, packed_width)
    extent = -(-inner_send.shape[1] * 128 // packed_width)
    inner_send = pad_to(inner_send.reshape(S, -1), extent * packed_width, 1).reshape(S, extent, packed_width)
    got = swap(jnp.concatenate([weight_parts, inner_send], 1), "fsdp")
    got, normed_parts = lax.optimization_barrier((got, normed_parts))
    got_sum = jnp.sum(got[:, :own].astype(f32), 0).astype(bf16)
    weight_all = lax.all_gather(got_sum, "sp", axis=0)
    normed_parts, rear_sum, weight_all = lax.optimization_barrier((normed_parts, rear_sum, weight_all))
    normed_parts = swap(normed_parts.reshape(Z, total, width), "sp")
    out_grad, gate_grad, fgate_grad, fup_grad, down_grad, gate_dot, post_grad = unpack_call(
        rear_sum, gate_weight, ffn_gate, ffn_up, post_gain[:, None], ff // S
    )
    post_grad = post_grad[:, 0]
    inner_part = got[:, own:].reshape(S, -1)[:, : slots * 2 * share * 128].astype(f32)
    inner_part = jnp.sum(inner_part.reshape(groups, micro, slots, 2, share, 128), 1)
    inner_part = inner_part.transpose(1, 0, 3, 2, 4).reshape(slots * groups, share, 2 * 128)[:local]
    query_grad, key_grad, value_grad, rate_grad, pre_grad = finish_call(
        weight_all, query_weight, key_weight, value_weight, rate_weight, gate_dot, pre_gain[:, None], layout
    )
    pre_grad = pre_grad[:, 0]
    rear_done = (out_grad, gate_grad, fgate_grad, fup_grad, down_grad, post_grad, pre_grad)
    rear_done, inner_part = lax.optimization_barrier((rear_done, inner_part.astype(bf16)))
    out_grad, gate_grad, fgate_grad, fup_grad, down_grad, post_grad, pre_grad = rear_done
    inner_sum = lax.all_gather(inner_part, "fsdp", axis=1, tiled=True).astype(f32)
    tokens_grad = token_call(normed_parts, grad_normed_gate, own_tokens, pre_full, grad_middle)
    tail = inner_sum[:, 2 * head : 2 * head + 2].reshape(local, 2 * inner)
    return (
        output.reshape(tokens.shape),
        tokens_grad.reshape(tokens.shape),
        pre_grad,
        query_grad,
        key_grad,
        value_grad,
        gate_grad,
        rate_grad,
        out_grad,
        post_grad,
        fgate_grad,
        fup_grad,
        down_grad,
        inner_sum[:, :head],
        tail[:, :inner],
        inner_sum[:, head : 2 * head].transpose(0, 2, 1),
        tail[:, inner : inner + head],
        tail[:, inner + head : inner + 2 * head],
        tail[:, inner + 2 * head : inner + 3 * head],
    )


def solution(mesh):
    return jax.shard_map(
        shards,
        mesh=mesh,
        in_specs=(
            P(None, "fsdp", "sp", None),
            P(),
            P(None, "fsdp", "sp", None),
            P("fsdp"),
            P("fsdp", None),
            P("fsdp", None),
            P("fsdp", None),
            P("fsdp", None),
            P("fsdp", None),
            P("fsdp", None),
            P("fsdp"),
            P("fsdp", None),
            P("fsdp", None),
            P("fsdp", None),
            P("sp", None, None),
            P("sp", None),
            P("sp", None, None),
            P("sp", None),
            P("sp", None),
            P("sp", None),
        ),
        out_specs=(
            P(None, "fsdp", "sp", None),
            P(None, "fsdp", "sp", None),
            P("fsdp"),
            P("fsdp", None),
            P("fsdp", None),
            P("fsdp", None),
            P("fsdp", None),
            P("fsdp", None),
            P("fsdp", None),
            P("fsdp"),
            P("fsdp", None),
            P("fsdp", None),
            P("fsdp", None),
            P("sp", None, None),
            P("sp", None),
            P("sp", None, None),
            P("sp", None),
            P("sp", None),
            P("sp", None),
        ),
        check_vma=False,
    )
```
